32 devices in a mesh: streams: 2 (over y), span: 4 (over z), head: 2 (over x), seq: 2 (over core).
Axes of the slice: x: 2, y: 2, z: 4, core: 2. Of those that a mesh axis runs over, the one named last changes fastest.
Arguments:
- query_rows: bfloat16 [4096, 1280], P(('streams', 'span', 'seq'), 'head'), parts along dimension 0, may hold values from -100 to 100
- key_rows: bfloat16 [4096, 1280], P(('streams', 'span', 'seq'), 'head'), parts along dimension 0, may hold values from -5 to 5
- value_rows: bfloat16 [4096, 1280], P(('streams', 'span', 'seq'), 'head'), parts along dimension 0, may hold values from -6 to 6
- out_weight: bfloat16 [1280, 5120], P('head', 'seq'), may hold values from -0.59765625 to 0.59765625
- gate_table: float32 [4, 5120], P(None, 'head'), may hold values from 0.5 to 2
- step_index: int32 [8], P('streams'), parts along dimension 0, may hold values from 0 to 3
- block_mask: int32 [8, 4], P('streams'), parts along dimension 0, may hold values from 0 to 1, as said below
Outputs:
- gated_update: bfloat16 [4096, 5120], P(('streams', 'span', 'seq'), 'head'), parts along dimension 0
The draws below stay inside these ranges and needn't reach their ends.
There are 2 independent parts, one for each index of `streams`. The reference program is written for one: setup_inputs(seed, part) draws one part's arguments, and reference() takes and returns one part's arrays. A program takes and returns all parts, laid end to end along the dimension named above; an argument that names none is the same for every part. Nothing has to cross between parts.
Inputs may be any that keep to these rules, and one draw needn't show every extreme that they name: block_mask[c, c] = 1 and block_mask[c, e] = 0 for e > c; entries below the diagonal are 0 or 1.
All inputs are finite; a program needn't handle non-finite values.
Results may differ from the reference program's by a relative error of at most 0.017.
Values may be sent and summed in bfloat16 or wider, within the bound.
A program may use at most 192 MiB of HBM per device.

```python
import math
import jax
import jax.numpy as jnp
from jax import lax

D = 5120
HD = 128
TOK_DEV = 256
STEPS = 4
HEADS = 10
SPANS = 4
TOKENS = 2048
N_SPAN = 4
N_SEQ = 2


def paired_draw(key):
    base = jax.random.fold_in(key, 7701)
    key_vals = jax.random.normal(jax.random.fold_in(base, 1), (TOKENS, HEADS * HD), jnp.float32)
    key_vals = jnp.clip(key_vals, -5.0, 5.0)
    query_vals = 1.5 * jax.random.normal(jax.random.fold_in(base, 2), (TOKENS, HEADS * HD), jnp.float32)
    query_vals = jnp.clip(query_vals, -8.0, 8.0)
    return (query_vals, key_vals)


def draw_query_rows(key, part):
    return paired_draw(key)[0].astype(jnp.bfloat16)


def draw_key_rows(key, part):
    return paired_draw(key)[1].astype(jnp.bfloat16)


def draw_block_mask(key, part):
    bits = jax.random.randint(jax.random.fold_in(key, 4411), (SPANS, SPANS), 0, 4)
    rows = jnp.arange(SPANS, dtype=jnp.int32)[:, None]
    cols = jnp.arange(SPANS, dtype=jnp.int32)[None, :]
    lower = jnp.where(rows > cols, jnp.where(bits > 0, 1, 0), 0)
    return (lower + jnp.where(rows == cols, 1, 0)).astype(jnp.int32)


def set_ends(drawn, key, smallest, largest):
    longest = drawn.shape.index(max(drawn.shape))
    spots = []
    for shift in (0, 1):
        where = [jax.random.randint(jax.random.fold_in(key, axis), (), 0, length) for axis, length in enumerate(drawn.shape)]
        where[longest] = (where[longest] + shift) % drawn.shape[longest]
        spots.append(tuple(where))
    return drawn.at[spots[0]].set(smallest).at[spots[1]].set(largest)


def shard_levels(own_key, shape, split, low, high):
    gain, own = 1.0, jax.random.fold_in(own_key, 6)
    for axis_at, parts in split:
        steps = jnp.exp(jax.random.uniform(jax.random.fold_in(own, axis_at), (parts,), jnp.float32, low / len(split), high / len(split)))
        gain = gain * jnp.repeat(steps, shape[axis_at] // parts).reshape([-1 if axis == axis_at else 1 for axis in range(len(shape))])
    return gain


def noise(own_key, dims, deviation, reach, cuts=(), kind=jnp.bfloat16):
    level = shard_levels(own_key, dims, cuts, -0.22, 0.18) if cuts else 1.0
    values = jax.random.normal(own_key, dims, jnp.float32) * deviation * level
    return jnp.minimum(jnp.maximum(values, -reach), reach).astype(kind)


def setup_inputs(seed: int = 0, part: int = 0) -> dict:
    keys = jax.random.split(jax.random.key(seed), 8)
    own_keys = jax.random.split(jax.random.fold_in(keys[7], part), 8)
    query_rows = draw_query_rows(jax.random.fold_in(jax.random.fold_in(keys[7], part), 71), part)
    key_rows = draw_key_rows(jax.random.fold_in(jax.random.fold_in(keys[7], part), 71), part)
    value_rows = noise(own_keys[2], (TOKENS, HEADS * HD), 1.0, 6.0, ((0, 8), (1, 2)))
    out_weight = noise(keys[3], (HEADS * HD, D), 0.1, 0.59765625, ((0, 2), (1, 2)))
    gate_table = jnp.clip(0.5 + 1.5 * jax.random.uniform(keys[4], (STEPS, D), jnp.float32) ** shard_levels(keys[4], (STEPS, D), ((1, 2),), -0.2, 0.2), 0.5, 2.0)
    step_index = set_ends(jax.random.randint(own_keys[5], (SPANS,), 0, STEPS), jax.random.fold_in(own_keys[5], 1), 0, STEPS - 1).astype(jnp.int32)
    block_mask = draw_block_mask(jax.random.fold_in(jax.random.fold_in(keys[7], part), 71), part)
    return dict(query_rows=query_rows, key_rows=key_rows, value_rows=value_rows, out_weight=out_weight, gate_table=gate_table, step_index=step_index, block_mask=block_mask)


def reference(query_rows, key_rows, value_rows, out_weight, gate_table, step_index, block_mask):
    span_tok = TOK_DEV * N_SEQ
    span_count = N_SPAN
    head_count = query_rows.shape[1] // HD
    query_blocks = query_rows.reshape(span_count, span_tok, head_count, HD)
    key_all = key_rows.reshape(-1, head_count, HD).astype(jnp.float32)
    value_all = value_rows.reshape(-1, head_count, HD).astype(jnp.float32)
    key_group = (jnp.arange(key_all.shape[0], dtype=jnp.int32) // span_tok).astype(jnp.int32)

    def one_span(packed):
        query_block, group = packed
        visible = block_mask[group][key_group] == 1
        scores = jnp.einsum('thd,khd->htk', query_block.astype(jnp.float32), key_all) / math.sqrt(HD)
        scores = jnp.where(visible[None, None, :], scores, -jnp.inf)
        top_score = lax.optimization_barrier(jnp.max(scores, axis=2, keepdims=True))
        probs = jnp.where(visible[None, None, :], jnp.exp(scores - top_score), 0.0)
        denom = lax.optimization_barrier(jnp.sum(probs, axis=2))
        probs_low = probs.astype(jnp.bfloat16).astype(jnp.float32)
        summed = jnp.einsum('htk,khd->htd', probs_low, value_all) / denom[:, :, None]
        attended = jnp.transpose(summed, (1, 0, 2)).reshape(span_tok, head_count * HD).astype(jnp.bfloat16)
        projected = jnp.dot(attended, out_weight, preferred_element_type=jnp.float32)
        gate_row = gate_table[step_index[group]]
        return (gate_row[None, :] * projected).astype(jnp.bfloat16)
    outputs = lax.map(one_span, (query_blocks, jnp.arange(span_count, dtype=jnp.int32)))
    return outputs.reshape(span_count * span_tok, -1)
```

```python
import functools
import math

import jax
import jax.numpy as jnp
from jax import lax
from jax.experimental import pallas as pl
from jax.experimental.pallas import tpu as pltpu
from jax.sharding import PartitionSpec as P

HD = 128
NEG_FLOOR = -1e30
MESH = pl.DeviceIdType.MESH
SCORE_SCALE = math.log2(math.e) / math.sqrt(HD)


def kernel(
    sizes,
    step_ref,
    mask_ref,
    q_ref,
    k_ref,
    v_ref,
    w_ref,
    gate_ref,
    out_ref,
    q_all,
    k_own,
    v_own,
    k_zero,
    v_zero,
    part_acc,
    part_stat,
    acc_out,
    stat_out,
    acc_in,
    stat_in,
    att,
    w_full,
    load_sem,
    sib_send,
    sib_recv,
    zero_send,
    zero_recv,
    fwd_send,
    fwd_recv,
    q_send,
    q_recv,
    acc_send,
    acc_recv,
    stat_send,
    stat_recv,
    x_send,
    x_recv,
    y_send,
    y_recv,
    d_send,
    d_recv,
    own_load,
    own_send,
    own_recv,
    att_send,
    att_recv,
):
    n_str, n_span, n_head, n_seq = sizes
    y = lax.axis_index("streams")
    z = lax.axis_index("span")
    x = lax.axis_index("head")
    s = lax.axis_index("seq")
    sib = 1 - s
    tok = q_ref.shape[0]
    heads = q_ref.shape[1] // HD
    w_rows = w_ref.shape[0]
    cols = out_ref.shape[1]
    y_rows = w_rows // n_str
    sub_rows = y_rows // n_seq
    piece = sub_rows // heads
    own_piece = w_rows // heads

    def remote(src, dst, ss, rs, **where):
        return pltpu.make_async_remote_copy(
            src_ref=src, dst_ref=dst, send_sem=ss, recv_sem=rs, device_id=where, device_id_type=MESH
        )

    def head_cols(h):
        return pl.ds(pl.multiple_of(h * HD, HD), HD)

    def each_head(body):
        lax.fori_loop(0, heads, lambda h, c: (body(h), c)[1], 0)

    def down(body, low):
        lax.fori_loop(0, n_span - low, lambda i, c: (body(n_span - 1 - i), c)[1], 0)

    tok_half = pl.ds(pl.multiple_of(s * tok, tok), tok)
    sib_half = pl.ds(pl.multiple_of(sib * tok, tok), tok)

    def load_q(h):
        return pltpu.make_async_copy(q_ref.at[:, head_cols(h)], q_all.at[z, h], load_sem.at[0, h])

    def load_k(h):
        return pltpu.make_async_copy(
            k_ref.at[:, head_cols(h)], k_own.at[h, tok_half], load_sem.at[1, h]
        )

    def load_v(h):
        return pltpu.make_async_copy(
            v_ref.at[:, head_cols(h)], v_own.at[h, tok_half], load_sem.at[2, h]
        )

    def sib_k(h, half):
        return remote(
            k_ref.at[:, head_cols(h)], k_own.at[h, half], sib_send.at[0, h], sib_recv.at[0, h], seq=sib
        )

    def sib_v(h, half):
        return remote(
            v_ref.at[:, head_cols(h)], v_own.at[h, half], sib_send.at[1, h], sib_recv.at[1, h], seq=sib
        )

    def zero_k(h):
        return remote(
            k_ref.at[:, head_cols(h)], k_zero.at[h, tok_half], zero_send.at[0, h], zero_recv.at[0, h],
            span=1,
        )

    def zero_v(h):
        return remote(
            v_ref.at[:, head_cols(h)], v_zero.at[h, tok_half], zero_send.at[1, h], zero_recv.at[1, h],
            span=1,
        )

    def fwd_k(h, half):
        return remote(
            k_zero.at[h, half], k_zero.at[h, half], fwd_send.at[0, h], fwd_recv.at[0, h], seq=sib
        )

    def fwd_v(h, half):
        return remote(
            v_zero.at[h, half], v_zero.at[h, half], fwd_send.at[1, h], fwd_recv.at[1, h], seq=sib
        )

    def own_q(h):
        return remote(
            q_ref.at[:, head_cols(h)], q_all.at[z, h], q_send.at[z, h], q_recv.at[z, h], span=z - 1
        )

    def pass_q(c, h):
        return remote(q_all.at[c, h], q_all.at[c, h], q_send.at[c, h], q_recv.at[c, h], span=z - 1)

    def pass_acc(c, h):
        return remote(
            acc_out.at[c, h], acc_in.at[c, h], acc_send.at[c, h], acc_recv.at[c, h], span=z + 1
        )

    def pass_stat(c, h):
        return remote(
            stat_out.at[c, h], stat_in.at[c, h], stat_send.at[c, h], stat_recv.at[c, h], span=z + 1
        )

    def w_at(src_x, part, sub, i):
        first = src_x * w_rows + part * y_rows + sub * sub_rows + i * piece
        return w_full.at[pl.ds(pl.multiple_of(first, piece), piece)]

    def block_core(dst_x):
        return (dst_x * n_seq) // n_head

    def block_cols(dst_x):
        first = lax.rem(dst_x, n_head // n_seq) * cols
        return pl.ds(pl.multiple_of(first, HD), cols)

    def x_piece(dst_x, sub, i):
        first = y * y_rows + sub * sub_rows + i * piece
        return remote(
            w_ref.at[pl.ds(pl.multiple_of(first, piece), piece), block_cols(dst_x)],
            w_at(x, y, sub, i),
            x_send.at[dst_x, sub, i],
            x_recv.at[x, i],
            head=dst_x,
            seq=sub,
        )

    def x_wait(src_x, i):
        ref = w_at(src_x, y, s, i)
        remote(ref, ref, x_send.at[src_x, 0, i], x_recv.at[src_x, i], head=src_x).wait_recv()

    def y_piece(src_x, dy, i):
        ref = w_at(src_x, y, s, i)
        return remote(
            ref, ref, y_send.at[src_x, dy, i], y_recv.at[src_x, dy, i], streams=lax.rem(y + dy, n_str)
        )

    def y_wait(src_x, dy, i):
        from_y = lax.rem(y - dy + n_str, n_str)
        ref = w_at(src_x, from_y, s, i)
        remote(
            ref, ref, y_send.at[src_x, dy, i], y_recv.at[src_x, dy, i], streams=from_y
        ).wait_recv()

    def d_piece(src_x, dy, i, sub):
        ref = w_at(src_x, lax.rem(y - dy + n_str, n_str), sub, i)
        return remote(ref, ref, d_send.at[src_x, dy, i], d_recv.at[src_x, dy, i], seq=sib)

    def own_rows(i):
        return pl.ds(pl.multiple_of(i * own_piece, own_piece), own_piece)

    def own_at(i):
        first = x * w_rows + i * own_piece
        return w_full.at[pl.ds(pl.multiple_of(first, own_piece), own_piece)]

    def own_copy(i):
        return pltpu.make_async_copy(w_ref.at[own_rows(i), block_cols(x)], own_at(i), own_load.at[i])

    def own_share(i):
        return remote(
            w_ref.at[own_rows(i), block_cols(x)], own_at(i), own_send.at[i], own_recv.at[i], seq=sib
        )

    def att_piece(dst_x, h):
        ref = att.at[x * heads + h]
        return remote(ref, ref, att_send.at[dst_x, h], att_recv.at[x, h], head=dst_x)

    def att_wait(src_x, h):
        ref = att.at[src_x * heads + h]
        remote(ref, ref, att_send.at[src_x, h], att_recv.at[src_x, h], head=src_x).wait_recv()

    others = [lax.rem(x + dx, n_head) for dx in range(1, n_head)]

    barrier = pltpu.get_barrier_semaphore()

    def greet(**where):
        pl.semaphore_signal(barrier, inc=1, device_id=where, device_id_type=MESH)

    greet(seq=sib)
    for other in others:
        for core in range(n_seq):
            greet(head=other, seq=core)
    for dy in range(1, n_str):
        greet(streams=lax.rem(y + dy, n_str))

    @pl.when(z > 0)
    def _():
        greet(span=z - 1)

    @pl.when(z < n_span - 1)
    def _():
        greet(span=z + 1)

    each_head(lambda h: (load_q(h).start(), load_k(h).start(), load_v(h).start()))
    beside = jnp.where(z > 0, 1, 0) + jnp.where(z < n_span - 1, 1, 0)
    pl.semaphore_wait(barrier, 1 + n_seq * (n_head - 1) + (n_str - 1) + beside)

    @pl.when(z >= 2)
    def _():
        own_q(0).start()

    @pl.when(z == 0)
    def _():
        each_head(lambda h: (zero_k(h).start(), zero_v(h).start()))

    each_head(lambda h: (sib_k(h, tok_half).start(), sib_v(h, tok_half).start()))
    for other in others:

        @pl.when(block_core(other) == s)
        def _(other=other):
            each_head(lambda i: [x_piece(other, sub, i).start() for sub in range(n_seq)])

    def block(q, k, v_t, flag):
        scores = (
            lax.dot_general(k, q, (((1,), (1,)), ((), ())), preferred_element_type=jnp.float32)
            * SCORE_SCALE
        )
        top = jnp.max(scores, axis=0, keepdims=True)
        probs = jnp.exp2(scores - top)
        total = jnp.sum(probs, axis=0, keepdims=True)
        acc = jnp.dot(v_t, probs.astype(jnp.bfloat16), preferred_element_type=jnp.float32)
        return jnp.where(flag == 1, top, NEG_FLOOR), total, acc

    def merge(a, b):
        top = jnp.maximum(a[0], b[0])
        wa, wb = jnp.exp2(a[0] - top), jnp.exp2(b[0] - top)
        return top, wa * a[1] + wb * b[1], wa * a[2] + wb * b[2]

    def get_part(c, h):
        return part_stat[c, h, 0:1], part_stat[c, h, 1:2], part_acc[c, h]

    def put_part(c, h, part):
        part_stat[c, h, 0:1] = part[0]
        part_stat[c, h, 1:2] = part[1]
        part_acc[c, h] = part[2]

    def emit(c, h, part):
        @pl.when(c > z)
        def _():
            stat_out[c, h, 0:1] = part[0]
            stat_out[c, h, 1:2] = part[1]
            acc_out[c, h] = part[2].astype(jnp.bfloat16)
            pass_acc(c, h).start()
            pass_stat(c, h).start()

        @pl.when(c == z)
        def _():
            att[x * heads + h] = (part[2] / part[1]).T.astype(jnp.bfloat16)
            for other in others:
                att_piece(other, h).start()

    def pass_on(h):
        def one(c):
            pass_q(c, h).wait_recv()

            @pl.when(z >= 2)
            def _():
                pass_q(c, h).start()

        down(one, z + 1)

        @pl.when((z >= 2) & (h + 1 < heads))
        def _():
            own_q(h + 1).start()

    @pl.when(z >= 2)
    def _():
        pass_on(0)

    def head_step(h):
        @pl.when((z >= 2) & (h + 1 < heads))
        def _():
            pass_on(h + 1)

        @pl.when(z == 1)
        def _():
            zero_k(h).wait_recv()
            fwd_k(h, tok_half).start()
            zero_v(h).wait_recv()
            fwd_v(h, tok_half).start()
            pass_on(h)

        @pl.when(block_core(x) == s)
        def _():
            own_copy(h).start()
            own_share(h).start()

        load_q(h).wait()
        load_k(h).wait()
        load_v(h).wait()
        sib_k(h, sib_half).wait_recv()
        sib_v(h, sib_half).wait_recv()

        k_here = k_own[h]
        v_here = v_own[h].T

        def own_block(c):
            put_part(c, h, block(q_all[c, h], k_here, v_here, mask_ref[c, z]))

        down(own_block, z)

        @pl.when(z == 1)
        def _():
            fwd_k(h, sib_half).wait_recv()
            fwd_v(h, sib_half).wait_recv()
            k_first = k_zero[h]
            v_first = v_zero[h].T

            def first_block(c):
                first = block(q_all[c, h], k_first, v_first, mask_ref[c, 0])
                emit(c, h, merge(get_part(c, h), first))

            down(first_block, z)

        @pl.when(z == 0)
        def _():
            emit(z, h, get_part(z, h))

        for other in others:
            x_wait(other, h)
            for dy in range(1, n_str):
                y_piece(other, dy, h).start()
            d_piece(other, 0, h, s).start()

            @pl.when(h > 0)
            def _(other=other):
                for dy in range(1, n_str):
                    y_wait(other, dy, h - 1)
                    d_piece(other, dy, h - 1, s).start()

    each_head(head_step)

    @pl.when(z >= 2)
    def _():
        def merge_step(h):
            def one(c):
                pass_acc(c, h).wait_recv()
                pass_stat(c, h).wait_recv()
                before = (
                    stat_in[c, h, 0:1],
                    stat_in[c, h, 1:2],
                    acc_in[c, h].astype(jnp.float32),
                )
                emit(c, h, merge(get_part(c, h), before))

            down(one, z)

        each_head(merge_step)

    for other in others:
        for dy in range(1, n_str):
            y_wait(other, dy, heads - 1)
            d_piece(other, dy, heads - 1, s).start()

    @pl.when(block_core(x) == s)
    def _():
        each_head(lambda i: own_copy(i).wait())

    @pl.when(block_core(x) != s)
    def _():
        each_head(lambda i: own_share(i).wait_recv())

    for other in others:

        def last_waits(i, other=other):
            for dy in range(n_str):
                d_piece(other, dy, i, sib).wait_recv()
            att_wait(other, i)

        each_head(last_waits)

    step = step_ref[z]
    tile = 256
    attended = jnp.concatenate([att[i] for i in range(n_head * heads)], axis=1)

    def project(t, carry):
        at = pl.ds(pl.multiple_of(t * tile, tile), tile)
        projected = jnp.dot(attended, w_full[:, at], preferred_element_type=jnp.float32)
        gate_row = jnp.zeros((1, tile), jnp.float32)
        for i in range(gate_ref.shape[0]):
            gate_row = jnp.where(step == i, gate_ref[i : i + 1, at], gate_row)
        out_ref[:, at] = (gate_row * projected).astype(jnp.bfloat16)
        return carry

    lax.fori_loop(0, cols // tile, project, 0)

    def sent(h):
        sib_k(h, tok_half).wait_send()
        sib_v(h, tok_half).wait_send()
        for other in others:
            att_piece(other, h).wait_send()
            for dy in range(1, n_str):
                y_piece(other, dy, h).wait_send()
            for dy in range(n_str):
                d_piece(other, dy, h, s).wait_send()

            @pl.when(block_core(other) == s)
            def _(other=other):
                for sub in range(n_seq):
                    x_piece(other, sub, h).wait_send()

        @pl.when(block_core(x) == s)
        def _():
            own_share(h).wait_send()

        @pl.when(z == 0)
        def _():
            zero_k(h).wait_send()
            zero_v(h).wait_send()

        @pl.when(z == 1)
        def _():
            fwd_k(h, tok_half).wait_send()
            fwd_v(h, tok_half).wait_send()

        @pl.when(z >= 2)
        def _():
            own_q(h).wait_send()
            down(lambda c: pass_q(c, h).wait_send(), z + 1)

        @pl.when(z >= 1)
        def _():
            down(lambda c: (pass_acc(c, h).wait_send(), pass_stat(c, h).wait_send()), z + 1)

    each_head(sent)


def solution(mesh):
    n_str, n_span = mesh.shape["streams"], mesh.shape["span"]
    n_head, n_seq = mesh.shape["head"], mesh.shape["seq"]
    sizes = (n_str, n_span, n_head, n_seq)

    def on_device(query_rows, key_rows, value_rows, out_weight, gate_table, step_index, block_mask):
        tok = query_rows.shape[0]
        heads = query_rows.shape[1] // HD
        cols = gate_table.shape[1]
        vmem, any_space = pltpu.VMEM, pl.ANY
        dma = pltpu.SemaphoreType.DMA
        low, wide = jnp.bfloat16, jnp.float32
        flops = 4 * heads * tok * tok * n_seq * n_span * HD + 2 * tok * n_head * heads * HD * cols
        return pl.pallas_call(
            functools.partial(kernel, sizes),
            out_shape=jax.ShapeDtypeStruct((tok, cols), low),
            in_specs=[
                pl.BlockSpec(memory_space=pltpu.SMEM),
                pl.BlockSpec(memory_space=pltpu.SMEM),
                pl.BlockSpec(memory_space=any_space),
                pl.BlockSpec(memory_space=any_space),
                pl.BlockSpec(memory_space=any_space),
                pl.BlockSpec(memory_space=any_space),
                pl.BlockSpec(memory_space=vmem),
            ],
            out_specs=pl.BlockSpec(memory_space=vmem),
            scratch_shapes=[
                vmem((n_span, heads, tok, HD), low),
                vmem((heads, n_seq * tok, HD), low),
                vmem((heads, n_seq * tok, HD), low),
                vmem((heads, n_seq * tok, HD), low),
                vmem((heads, n_seq * tok, HD), low),
                vmem((n_span, heads, HD, tok), wide),
                vmem((n_span, heads, 8, tok), wide),
                vmem((n_span, heads, HD, tok), low),
                vmem((n_span, heads, 8, tok), wide),
                vmem((n_span, heads, HD, tok), low),
                vmem((n_span, heads, 8, tok), wide),
                vmem((n_head * heads, tok, HD), low),
                vmem((n_head * heads * HD, cols), low),
                dma((3, heads)),
                dma((2, heads)),
                dma((2, heads)),
                dma((2, heads)),
                dma((2, heads)),
                dma((2, heads)),
                dma((2, heads)),
                dma((n_span, heads)),
                dma((n_span, heads)),
                dma((n_span, heads)),
                dma((n_span, heads)),
                dma((n_span, heads)),
                dma((n_span, heads)),
                dma((n_head, n_seq, heads)),
                dma((n_head, heads)),
                dma((n_head, n_str, heads)),
                dma((n_head, n_str, heads)),
                dma((n_head, n_str, heads)),
                dma((n_head, n_str, heads)),
                dma((heads,)),
                dma((heads,)),
                dma((heads,)),
                dma((n_head, heads)),
                dma((n_head, heads)),
            ],
            compiler_params=pltpu.CompilerParams(
                collective_id=0, has_side_effects=True, vmem_limit_bytes=56 * 1024 * 1024
            ),
            cost_estimate=pl.CostEstimate(
                flops=flops, bytes_accessed=6 * out_weight.size, transcendentals=0
            ),
        )(step_index, block_mask, query_rows, key_rows, value_rows, out_weight, gate_table)

    in_specs = (
        P(("streams", "span", "seq"), "head"),
        P(("streams", "span", "seq"), "head"),
        P(("streams", "span", "seq"), "head"),
        P("head", "seq"),
        P(None, "head"),
        P("streams"),
        P("streams", None),
    )
    out_specs = P(("streams", "span", "seq"), "head")
    return jax.shard_map(
        on_device, mesh=mesh, in_specs=in_specs, out_specs=out_specs, check_vma=False
    )
```

```python
import functools
import math

import jax
import jax.numpy as jnp
from jax import lax
from jax.experimental import pallas as pl
from jax.experimental.pallas import tpu as pltpu
from jax.sharding import PartitionSpec as P

HD = 128
NEG_FLOOR = -1e30
MESH = pl.DeviceIdType.MESH
SCORE_SCALE = math.log2(math.e) / math.sqrt(HD)


def kernel(
    sizes,
    step_ref,
    mask_ref,
    q_ref,
    k_ref,
    v_ref,
    w_ref,
    gate_ref,
    out_ref,
    q_all,
    k_own,
    v_own,
    k_zero,
    v_zero,
    part_acc,
    part_stat,
    acc_out,
    stat_out,
    acc_in,
    stat_in,
    att,
    w_full,
    out_half,
    load_sem,
    sib_send,
    sib_recv,
    zero_send,
    zero_recv,
    fwd_send,
    fwd_recv,
    q_send,
    q_recv,
    acc_send,
    acc_recv,
    stat_send,
    stat_recv,
    x_send,
    x_recv,
    y_send,
    y_recv,
    own_load,
    own_send,
    own_recv,
    att_send,
    att_recv,
    pair_send,
    pair_recv,
    out_send,
    out_recv,
):
    n_str, n_span, n_head, n_seq = sizes
    y = lax.axis_index("streams")
    z = lax.axis_index("span")
    x = lax.axis_index("head")
    s = lax.axis_index("seq")
    sib = 1 - s
    tok = q_ref.shape[0]
    heads = q_ref.shape[1] // HD
    w_rows = w_ref.shape[0]
    cols = out_ref.shape[1]
    half = cols // n_seq
    tile = 256 if half % 256 == 0 else 128
    tiles = half // tile
    y_rows = w_rows // n_str
    piece = y_rows // heads
    own_piece = w_rows // heads

    def remote(src, dst, ss, rs, **where):
        return pltpu.make_async_remote_copy(
            src_ref=src, dst_ref=dst, send_sem=ss, recv_sem=rs, device_id=where, device_id_type=MESH
        )

    def head_cols(h):
        return pl.ds(pl.multiple_of(h * HD, HD), HD)

    def each_head(body):
        lax.fori_loop(0, heads, lambda h, c: (body(h), c)[1], 0)

    def down(body, low):
        lax.fori_loop(0, n_span - low, lambda i, c: (body(n_span - 1 - i), c)[1], 0)

    tok_half = pl.ds(pl.multiple_of(s * tok, tok), tok)
    sib_half = pl.ds(pl.multiple_of(sib * tok, tok), tok)

    def load_q(h):
        return pltpu.make_async_copy(q_ref.at[:, head_cols(h)], q_all.at[z, h], load_sem.at[0, h])

    def load_k(h):
        return pltpu.make_async_copy(
            k_ref.at[:, head_cols(h)], k_own.at[h, tok_half], load_sem.at[1, h]
        )

    def load_v(h):
        return pltpu.make_async_copy(
            v_ref.at[:, head_cols(h)], v_own.at[h, tok_half], load_sem.at[2, h]
        )

    def sib_k(h, half):
        return remote(
            k_ref.at[:, head_cols(h)], k_own.at[h, half], sib_send.at[0, h], sib_recv.at[0, h], seq=sib
        )

    def sib_v(h, half):
        return remote(
            v_ref.at[:, head_cols(h)], v_own.at[h, half], sib_send.at[1, h], sib_recv.at[1, h], seq=sib
        )

    def zero_k(h):
        return remote(
            k_ref.at[:, head_cols(h)], k_zero.at[h, tok_half], zero_send.at[0, h], zero_recv.at[0, h],
            span=1,
        )

    def zero_v(h):
        return remote(
            v_ref.at[:, head_cols(h)], v_zero.at[h, tok_half], zero_send.at[1, h], zero_recv.at[1, h],
            span=1,
        )

    def fwd_k(h, half):
        return remote(
            k_zero.at[h, half], k_zero.at[h, half], fwd_send.at[0, h], fwd_recv.at[0, h], seq=sib
        )

    def fwd_v(h, half):
        return remote(
            v_zero.at[h, half], v_zero.at[h, half], fwd_send.at[1, h], fwd_recv.at[1, h], seq=sib
        )

    def own_q(h):
        return remote(
            q_ref.at[:, head_cols(h)], q_all.at[z, h], q_send.at[z, h], q_recv.at[z, h], span=z - 1
        )

    def pass_q(c, h):
        return remote(q_all.at[c, h], q_all.at[c, h], q_send.at[c, h], q_recv.at[c, h], span=z - 1)

    def pass_acc(c, h):
        return remote(
            acc_out.at[c, h], acc_in.at[c, h], acc_send.at[c, h], acc_recv.at[c, h], span=z + 1
        )

    def pass_stat(c, h):
        return remote(
            stat_out.at[c, h], stat_in.at[c, h], stat_send.at[c, h], stat_recv.at[c, h], span=z + 1
        )

    def w_at(src_x, part, i):
        first = src_x * w_rows + part * y_rows + i * piece
        return w_full.at[pl.ds(pl.multiple_of(first, piece), piece)]

    def block_core(dst_x):
        return (dst_x * n_seq) // n_head

    def block_cols(dst_x, core):
        first = lax.rem(dst_x, n_head // n_seq) * cols + core * half
        return pl.ds(pl.multiple_of(first, HD), half)

    def x_piece(dst_x, core, i):
        first = y * y_rows + i * piece
        return remote(
            w_ref.at[pl.ds(pl.multiple_of(first, piece), piece), block_cols(dst_x, core)],
            w_at(x, y, i),
            x_send.at[dst_x, core, i],
            x_recv.at[x, i],
            head=dst_x,
            seq=core,
        )

    def x_wait(src_x, i):
        ref = w_at(src_x, y, i)
        remote(ref, ref, x_send.at[src_x, 0, i], x_recv.at[src_x, i], head=src_x).wait_recv()

    def y_piece(src_x, dy, i):
        ref = w_at(src_x, y, i)
        return remote(
            ref, ref, y_send.at[src_x, dy, i], y_recv.at[src_x, dy, i], streams=lax.rem(y + dy, n_str)
        )

    def y_wait(src_x, dy, i):
        from_y = lax.rem(y - dy + n_str, n_str)
        ref = w_at(src_x, from_y, i)
        remote(
            ref, ref, y_send.at[src_x, dy, i], y_recv.at[src_x, dy, i], streams=from_y
        ).wait_recv()

    def own_rows(i):
        return pl.ds(pl.multiple_of(i * own_piece, own_piece), own_piece)

    def own_at(i):
        first = x * w_rows + i * own_piece
        return w_full.at[pl.ds(pl.multiple_of(first, own_piece), own_piece)]

    def own_copy(i):
        return pltpu.make_async_copy(
            w_ref.at[own_rows(i), block_cols(x, s)], own_at(i), own_load.at[i]
        )

    def own_share(i):
        return remote(
            w_ref.at[own_rows(i), block_cols(x, sib)], own_at(i), own_send.at[i], own_recv.at[i], seq=sib
        )

    def att_piece(dst_x, h):
        ref = att.at[x * heads + h, tok_half]
        return remote(ref, ref, att_send.at[dst_x, h], att_recv.at[x, h], head=dst_x)

    def att_wait(src_x, h):
        ref = att.at[src_x * heads + h, tok_half]
        remote(ref, ref, att_send.at[src_x, h], att_recv.at[src_x, h], head=src_x).wait_recv()

    def att_pair(src_x, h, rows):
        ref = att.at[src_x * heads + h, rows]
        return remote(ref, ref, pair_send.at[src_x, h], pair_recv.at[src_x, h], seq=sib)

    def out_cols(core, t):
        return pl.ds(pl.multiple_of(core * half + t * tile, tile), tile)

    def out_piece(core, t):
        return remote(
            out_half.at[t], out_ref.at[:, out_cols(core, t)], out_send.at[t], out_recv.at[t], seq=sib
        )

    others = [lax.rem(x + dx, n_head) for dx in range(1, n_head)]

    barrier = pltpu.get_barrier_semaphore()

    def greet(**where):
        pl.semaphore_signal(barrier, inc=1, device_id=where, device_id_type=MESH)

    greet(seq=sib)
    for other in others:
        for core in range(n_seq):
            greet(head=other, seq=core)
    for dy in range(1, n_str):
        greet(streams=lax.rem(y + dy, n_str))

    @pl.when(z > 0)
    def _():
        greet(span=z - 1)

    @pl.when(z < n_span - 1)
    def _():
        greet(span=z + 1)

    each_head(lambda h: (load_q(h).start(), load_k(h).start(), load_v(h).start()))
    beside = jnp.where(z > 0, 1, 0) + jnp.where(z < n_span - 1, 1, 0)
    pl.semaphore_wait(barrier, 1 + n_seq * (n_head - 1) + (n_str - 1) + beside)

    @pl.when(z >= 2)
    def _():
        own_q(0).start()

    @pl.when(z == 0)
    def _():
        each_head(lambda h: (zero_k(h).start(), zero_v(h).start()))

    each_head(lambda h: (sib_k(h, tok_half).start(), sib_v(h, tok_half).start()))
    for other in others:

        @pl.when(block_core(other) == s)
        def _(other=other):
            each_head(lambda i: [x_piece(other, sub, i).start() for sub in range(n_seq)])

    def block(q, k, v_t, flag):
        scores = (
            lax.dot_general(k, q, (((1,), (1,)), ((), ())), preferred_element_type=jnp.float32)
            * SCORE_SCALE
        )
        top = jnp.max(scores, axis=0, keepdims=True)
        probs = jnp.exp2(scores - top)
        total = jnp.sum(probs, axis=0, keepdims=True)
        acc = jnp.dot(v_t, probs.astype(jnp.bfloat16), preferred_element_type=jnp.float32)
        return jnp.where(flag == 1, top, NEG_FLOOR), total, acc

    def merge(a, b):
        top = jnp.maximum(a[0], b[0])
        wa, wb = jnp.exp2(a[0] - top), jnp.exp2(b[0] - top)
        return top, wa * a[1] + wb * b[1], wa * a[2] + wb * b[2]

    def get_part(c, h):
        return part_stat[c, h, 0:1], part_stat[c, h, 1:2], part_acc[c, h]

    def put_part(c, h, part):
        part_stat[c, h, 0:1] = part[0]
        part_stat[c, h, 1:2] = part[1]
        part_acc[c, h] = part[2]

    def emit(c, h, part):
        @pl.when(c > z)
        def _():
            stat_out[c, h, 0:1] = part[0]
            stat_out[c, h, 1:2] = part[1]
            acc_out[c, h] = part[2].astype(jnp.bfloat16)
            pass_acc(c, h).start()
            pass_stat(c, h).start()

        @pl.when(c == z)
        def _():
            att[x * heads + h, tok_half] = (part[2] / part[1]).T.astype(jnp.bfloat16)
            for other in others:
                att_piece(other, h).start()
            att_pair(x, h, tok_half).start()

    def pass_on(h):
        def one(c):
            pass_q(c, h).wait_recv()

            @pl.when(z >= 2)
            def _():
                pass_q(c, h).start()

        down(one, z + 1)

        @pl.when((z >= 2) & (h + 1 < heads))
        def _():
            own_q(h + 1).start()

    @pl.when(z >= 2)
    def _():
        pass_on(0)

    def pass_w(i):
        for other in others:
            x_wait(other, i)
            for dy in range(1, n_str):
                y_piece(other, dy, i).start()

    def head_step(h):
        @pl.when((z >= 2) & (h + 1 < heads))
        def _():
            pass_on(h + 1)

        @pl.when(z == 1)
        def _():
            zero_k(h).wait_recv()
            fwd_k(h, tok_half).start()
            zero_v(h).wait_recv()
            fwd_v(h, tok_half).start()
            pass_on(h)

        @pl.when(block_core(x) == s)
        def _():
            own_copy(h).start()
            own_share(h).start()

        load_q(h).wait()
        load_k(h).wait()
        load_v(h).wait()
        sib_k(h, sib_half).wait_recv()
        sib_v(h, sib_half).wait_recv()

        k_here = k_own[h]
        v_here = v_own[h].T

        def own_block(c):
            put_part(c, h, block(q_all[c, h], k_here, v_here, mask_ref[c, z]))

        down(own_block, z)

        @pl.when(z == 1)
        def _():
            fwd_k(h, sib_half).wait_recv()
            fwd_v(h, sib_half).wait_recv()
            k_first = k_zero[h]
            v_first = v_zero[h].T

            def first_block(c):
                first = block(q_all[c, h], k_first, v_first, mask_ref[c, 0])
                emit(c, h, merge(get_part(c, h), first))

            down(first_block, z)

        @pl.when(z == 0)
        def _():
            emit(z, h, get_part(z, h))

        @pl.when(z == 0)
        def _():
            pass_w(h)

        @pl.when((z == 1) & (h > 0))
        def _():
            pass_w(h - 1)

        @pl.when((z >= 2) & ((h == 2) | (h == 4)))
        def _():
            pass_w(h // 2 - 1)

    each_head(head_step)

    @pl.when(z == 1)
    def _():
        pass_w(heads - 1)

    @pl.when(z >= 2)
    def _():
        def merge_step(h):
            def one(c):
                pass_acc(c, h).wait_recv()
                pass_stat(c, h).wait_recv()
                before = (
                    stat_in[c, h, 0:1],
                    stat_in[c, h, 1:2],
                    acc_in[c, h].astype(jnp.float32),
                )
                emit(c, h, merge(get_part(c, h), before))

            down(one, z)

            @pl.when(h + 2 < heads)
            def _():
                pass_w(h + 2)

        each_head(merge_step)

    for other in others:

        def pass_att(h, other=other):
            att_wait(other, h)
            att_pair(other, h, tok_half).start()

        each_head(pass_att)

    @pl.when(block_core(x) == s)
    def _():
        each_head(lambda i: own_copy(i).wait())

    @pl.when(block_core(x) != s)
    def _():
        each_head(lambda i: own_share(i).wait_recv())

    def last_waits(h):
        for other in others:
            for dy in range(1, n_str):
                y_wait(other, dy, h)
            att_pair(other, h, sib_half).wait_recv()
        att_pair(x, h, sib_half).wait_recv()

    each_head(last_waits)

    step = step_ref[z]

    def gathered(rows):
        return jnp.concatenate([att[i, rows] for i in range(n_head * heads)], axis=1)

    attended = jnp.concatenate([gathered(sib_half), gathered(tok_half)], axis=0)

    def project(t, carry):
        at = pl.ds(pl.multiple_of(t * tile, tile), tile)
        projected = jnp.dot(attended, w_full[:, at], preferred_element_type=jnp.float32)
        here = out_cols(s, t)
        gate_row = jnp.zeros((1, tile), jnp.float32)
        for i in range(gate_ref.shape[0]):
            gate_row = jnp.where(step == i, gate_ref[i : i + 1, here], gate_row)
        gated = (gate_row * projected).astype(jnp.bfloat16)
        out_half[t] = gated[:tok]
        out_piece(s, t).start()
        out_ref[:, here] = gated[tok:]
        return carry

    lax.fori_loop(0, tiles, project, 0)

    def out_wait(t, carry):
        out_piece(sib, t).wait_recv()
        out_piece(s, t).wait_send()
        return carry

    lax.fori_loop(0, tiles, out_wait, 0)

    def sent(h):
        sib_k(h, tok_half).wait_send()
        sib_v(h, tok_half).wait_send()
        att_pair(x, h, tok_half).wait_send()
        for other in others:
            att_piece(other, h).wait_send()
            for dy in range(1, n_str):
                y_piece(other, dy, h).wait_send()
            att_pair(other, h, tok_half).wait_send()

            @pl.when(block_core(other) == s)
            def _(other=other):
                for sub in range(n_seq):
                    x_piece(other, sub, h).wait_send()

        @pl.when(block_core(x) == s)
        def _():
            own_share(h).wait_send()

        @pl.when(z == 0)
        def _():
            zero_k(h).wait_send()
            zero_v(h).wait_send()

        @pl.when(z == 1)
        def _():
            fwd_k(h, tok_half).wait_send()
            fwd_v(h, tok_half).wait_send()

        @pl.when(z >= 2)
        def _():
            own_q(h).wait_send()
            down(lambda c: pass_q(c, h).wait_send(), z + 1)

        @pl.when(z >= 1)
        def _():
            down(lambda c: (pass_acc(c, h).wait_send(), pass_stat(c, h).wait_send()), z + 1)

    each_head(sent)


def solution(mesh):
    n_str, n_span = mesh.shape["streams"], mesh.shape["span"]
    n_head, n_seq = mesh.shape["head"], mesh.shape["seq"]
    sizes = (n_str, n_span, n_head, n_seq)

    def on_device(query_rows, key_rows, value_rows, out_weight, gate_table, step_index, block_mask):
        tok = query_rows.shape[0]
        heads = query_rows.shape[1] // HD
        cols = gate_table.shape[1]
        half = cols // n_seq
        tile = 256 if half % 256 == 0 else 128
        tiles = half // tile
        vmem, any_space = pltpu.VMEM, pl.ANY
        dma = pltpu.SemaphoreType.DMA
        low, wide = jnp.bfloat16, jnp.float32
        flops = 4 * heads * tok * tok * n_seq * n_span * HD + 2 * tok * n_head * heads * HD * cols
        return pl.pallas_call(
            functools.partial(kernel, sizes),
            out_shape=jax.ShapeDtypeStruct((tok, cols), low),
            in_specs=[
                pl.BlockSpec(memory_space=pltpu.SMEM),
                pl.BlockSpec(memory_space=pltpu.SMEM),
                pl.BlockSpec(memory_space=any_space),
                pl.BlockSpec(memory_space=any_space),
                pl.BlockSpec(memory_space=any_space),
                pl.BlockSpec(memory_space=any_space),
                pl.BlockSpec(memory_space=vmem),
            ],
            out_specs=pl.BlockSpec(memory_space=vmem),
            scratch_shapes=[
                vmem((n_span, heads, tok, HD), low),
                vmem((heads, n_seq * tok, HD), low),
                vmem((heads, n_seq * tok, HD), low),
                vmem((heads, n_seq * tok, HD), low),
                vmem((heads, n_seq * tok, HD), low),
                vmem((n_span, heads, HD, tok), wide),
                vmem((n_span, heads, 8, tok), wide),
                vmem((n_span, heads, HD, tok), low),
                vmem((n_span, heads, 8, tok), wide),
                vmem((n_span, heads, HD, tok), low),
                vmem((n_span, heads, 8, tok), wide),
                vmem((n_head * heads, n_seq * tok, HD), low),
                vmem((n_head * heads * HD, half), low),
                vmem((tiles, tok, tile), low),
                dma((3, heads)),
                dma((2, heads)),
                dma((2, heads)),
                dma((2, heads)),
                dma((2, heads)),
                dma((2, heads)),
                dma((2, heads)),
                dma((n_span, heads)),
                dma((n_span, heads)),
                dma((n_span, heads)),
                dma((n_span, heads)),
                dma((n_span, heads)),
                dma((n_span, heads)),
                dma((n_head, n_seq, heads)),
                dma((n_head, heads)),
                dma((n_head, n_str, heads)),
                dma((n_head, n_str, heads)),
                dma((heads,)),
                dma((heads,)),
                dma((heads,)),
                dma((n_head, heads)),
                dma((n_head, heads)),
                dma((n_head, heads)),
                dma((n_head, heads)),
                dma((tiles,)),
                dma((tiles,)),
            ],
            compiler_params=pltpu.CompilerParams(
                collective_id=0, has_side_effects=True, vmem_limit_bytes=56 * 1024 * 1024
            ),
            cost_estimate=pl.CostEstimate(
                flops=flops, bytes_accessed=6 * out_weight.size, transcendentals=0
            ),
        )(step_index, block_mask, query_rows, key_rows, value_rows, out_weight, gate_table)

    in_specs = (
        P(("streams", "span", "seq"), "head"),
        P(("streams", "span", "seq"), "head"),
        P(("streams", "span", "seq"), "head"),
        P("head", "seq"),
        P(None, "head"),
        P("streams"),
        P("streams", None),
    )
    out_specs = P(("streams", "span", "seq"), "head")
    return jax.shard_map(
        on_device, mesh=mesh, in_specs=in_specs, out_specs=out_specs, check_vma=False
    )
```

```python
import functools
import math

import jax
import jax.numpy as jnp
from jax import lax
from jax.experimental import pallas as pl
from jax.experimental.pallas import tpu as pltpu
from jax.sharding import PartitionSpec as P

HD = 128
NEG_FLOOR = -1e30
MESH = pl.DeviceIdType.MESH
SCORE_SCALE = math.log2(math.e) / math.sqrt(HD)


def kernel(
    sizes,
    step_ref,
    mask_ref,
    q_ref,
    k_ref,
    v_ref,
    w_ref,
    gate_ref,
    out_ref,
    q_all,
    k_own,
    v_own,
    k_zero,
    v_zero,
    part_acc,
    part_stat,
    acc_out,
    stat_out,
    acc_in,
    stat_in,
    att,
    w_full,
    out_half,
    load_sem,
    sib_send,
    sib_recv,
    zero_send,
    zero_recv,
    fwd_send,
    fwd_recv,
    q_send,
    q_recv,
    acc_send,
    acc_recv,
    stat_send,
    stat_recv,
    x_send,
    x_recv,
    y_send,
    y_recv,
    own_load,
    own_send,
    own_recv,
    att_send,
    att_recv,
    pair_send,
    pair_recv,
    out_send,
    out_recv,
):
    n_str, n_span, n_head, n_seq = sizes
    y = lax.axis_index("streams")
    z = lax.axis_index("span")
    x = lax.axis_index("head")
    s = lax.axis_index("seq")
    sib = 1 - s
    tok = q_ref.shape[0]
    heads = q_ref.shape[1] // HD
    w_rows = w_ref.shape[0]
    cols = out_ref.shape[1]
    half = cols // n_seq
    tile = 256 if half % 256 == 0 else 128
    tiles = half // tile
    y_rows = w_rows // n_str
    piece = y_rows // heads
    own_piece = w_rows // heads

    def remote(src, dst, ss, rs, **where):
        return pltpu.make_async_remote_copy(
            src_ref=src, dst_ref=dst, send_sem=ss, recv_sem=rs, device_id=where, device_id_type=MESH
        )

    def head_cols(h):
        return pl.ds(pl.multiple_of(h * HD, HD), HD)

    def each_head(body):
        lax.fori_loop(0, heads, lambda h, c: (body(h), c)[1], 0)

    def down(body, low):
        lax.fori_loop(0, n_span - low, lambda i, c: (body(n_span - 1 - i), c)[1], 0)

    tok_half = pl.ds(pl.multiple_of(s * tok, tok), tok)
    sib_half = pl.ds(pl.multiple_of(sib * tok, tok), tok)

    def load_q(h):
        return pltpu.make_async_copy(q_ref.at[:, head_cols(h)], q_all.at[z, h], load_sem.at[0, h])

    def load_k(h):
        return pltpu.make_async_copy(
            k_ref.at[:, head_cols(h)], k_own.at[h, tok_half], load_sem.at[1, h]
        )

    def load_v(h):
        return pltpu.make_async_copy(
            v_ref.at[:, head_cols(h)], v_own.at[h, tok_half], load_sem.at[2, h]
        )

    def sib_k(h, half):
        return remote(
            k_ref.at[:, head_cols(h)], k_own.at[h, half], sib_send.at[0, h], sib_recv.at[0, h], seq=sib
        )

    def sib_v(h, half):
        return remote(
            v_ref.at[:, head_cols(h)], v_own.at[h, half], sib_send.at[1, h], sib_recv.at[1, h], seq=sib
        )

    def zero_k(h):
        return remote(
            k_ref.at[:, head_cols(h)], k_zero.at[h, tok_half], zero_send.at[0, h], zero_recv.at[0, h],
            span=1,
        )

    def zero_v(h):
        return remote(
            v_ref.at[:, head_cols(h)], v_zero.at[h, tok_half], zero_send.at[1, h], zero_recv.at[1, h],
            span=1,
        )

    def fwd_k(h, half):
        return remote(
            k_zero.at[h, half], k_zero.at[h, half], fwd_send.at[0, h], fwd_recv.at[0, h], seq=sib
        )

    def fwd_v(h, half):
        return remote(
            v_zero.at[h, half], v_zero.at[h, half], fwd_send.at[1, h], fwd_recv.at[1, h], seq=sib
        )

    def own_q(h):
        return remote(
            q_ref.at[:, head_cols(h)], q_all.at[z, h], q_send.at[z, h], q_recv.at[z, h], span=z - 1
        )

    def pass_q(c, h):
        return remote(q_all.at[c, h], q_all.at[c, h], q_send.at[c, h], q_recv.at[c, h], span=z - 1)

    def pass_acc(c, h):
        return remote(
            acc_out.at[c, h], acc_in.at[c, h], acc_send.at[c, h], acc_recv.at[c, h], span=z + 1
        )

    def pass_stat(c, h):
        return remote(
            stat_out.at[c, h], stat_in.at[c, h], stat_send.at[c, h], stat_recv.at[c, h], span=z + 1
        )

    def w_at(src_x, part, i):
        first = src_x * w_rows + part * y_rows + i * piece
        return w_full.at[pl.ds(pl.multiple_of(first, piece), piece)]

    def block_core(dst_x):
        return (dst_x * n_seq) // n_head

    def block_cols(dst_x, core):
        first = lax.rem(dst_x, n_head // n_seq) * cols + core * half
        return pl.ds(pl.multiple_of(first, HD), half)

    def x_piece(dst_x, core, i):
        first = y * y_rows + i * piece
        return remote(
            w_ref.at[pl.ds(pl.multiple_of(first, piece), piece), block_cols(dst_x, core)],
            w_at(x, y, i),
            x_send.at[dst_x, core, i],
            x_recv.at[x, i],
            head=dst_x,
            seq=core,
        )

    def x_wait(src_x, i):
        ref = w_at(src_x, y, i)
        remote(ref, ref, x_send.at[src_x, 0, i], x_recv.at[src_x, i], head=src_x).wait_recv()

    def y_piece(src_x, dy, i):
        ref = w_at(src_x, y, i)
        return remote(
            ref, ref, y_send.at[src_x, dy, i], y_recv.at[src_x, dy, i], streams=lax.rem(y + dy, n_str)
        )

    def y_wait(src_x, dy, i):
        from_y = lax.rem(y - dy + n_str, n_str)
        ref = w_at(src_x, from_y, i)
        remote(
            ref, ref, y_send.at[src_x, dy, i], y_recv.at[src_x, dy, i], streams=from_y
        ).wait_recv()

    def own_rows(i):
        return pl.ds(pl.multiple_of(i * own_piece, own_piece), own_piece)

    def own_at(i):
        first = x * w_rows + i * own_piece
        return w_full.at[pl.ds(pl.multiple_of(first, own_piece), own_piece)]

    def own_copy(i):
        return pltpu.make_async_copy(
            w_ref.at[own_rows(i), block_cols(x, s)], own_at(i), own_load.at[i]
        )

    def own_share(i):
        return remote(
            w_ref.at[own_rows(i), block_cols(x, sib)], own_at(i), own_send.at[i], own_recv.at[i], seq=sib
        )

    def att_piece(dst_x, h):
        ref = att.at[x * heads + h, tok_half]
        return remote(ref, ref, att_send.at[dst_x, h], att_recv.at[x, h], head=dst_x)

    def att_wait(src_x, h):
        ref = att.at[src_x * heads + h, tok_half]
        remote(ref, ref, att_send.at[src_x, h], att_recv.at[src_x, h], head=src_x).wait_recv()

    def att_pair(src_x, h, rows):
        ref = att.at[src_x * heads + h, rows]
        return remote(ref, ref, pair_send.at[src_x, h], pair_recv.at[src_x, h], seq=sib)

    def out_cols(core, t):
        return pl.ds(pl.multiple_of(core * half + t * tile, tile), tile)

    def out_piece(core, t):
        return remote(
            out_half.at[t], out_ref.at[:, out_cols(core, t)], out_send.at[t], out_recv.at[t], seq=sib
        )

    others = [lax.rem(x + dx, n_head) for dx in range(1, n_head)]

    barrier = pltpu.get_barrier_semaphore()

    def greet(**where):
        pl.semaphore_signal(barrier, inc=1, device_id=where, device_id_type=MESH)

    greet(seq=sib)
    for other in others:
        for core in range(n_seq):
            greet(head=other, seq=core)
    for dy in range(1, n_str):
        greet(streams=lax.rem(y + dy, n_str))

    @pl.when(z > 0)
    def _():
        greet(span=z - 1)

    @pl.when(z < n_span - 1)
    def _():
        greet(span=z + 1)

    each_head(lambda h: (load_q(h).start(), load_k(h).start(), load_v(h).start()))
    beside = jnp.where(z > 0, 1, 0) + jnp.where(z < n_span - 1, 1, 0)
    pl.semaphore_wait(barrier, 1 + n_seq * (n_head - 1) + (n_str - 1) + beside)

    @pl.when(z >= 2)
    def _():
        own_q(0).start()

    @pl.when(z == 0)
    def _():
        each_head(lambda h: (zero_k(h).start(), zero_v(h).start()))

    each_head(lambda h: (sib_k(h, tok_half).start(), sib_v(h, tok_half).start()))
    for other in others:

        @pl.when(block_core(other) == s)
        def _(other=other):
            each_head(lambda i: [x_piece(other, sub, i).start() for sub in range(n_seq)])

    def block(q, keys, v_t, flags):
        scores = [
            lax.dot_general(k, q, (((1,), (1,)), ((), ())), preferred_element_type=jnp.float32)
            * SCORE_SCALE
            for k in keys
        ]
        tops = [
            jnp.where(flag == 1, jnp.max(each, axis=0, keepdims=True), NEG_FLOOR)
            for each, flag in zip(scores, flags)
        ]
        top = functools.reduce(jnp.maximum, tops)
        probs = [
            jnp.exp2(each - jnp.where(flag == 1, top, -NEG_FLOOR))
            for each, flag in zip(scores, flags)
        ]
        total = sum(jnp.sum(each, axis=0, keepdims=True) for each in probs)
        low = jnp.concatenate([each.astype(jnp.bfloat16) for each in probs], axis=0)
        return top, total, jnp.dot(v_t, low, preferred_element_type=jnp.float32)

    def merge(a, b):
        top = jnp.maximum(a[0], b[0])
        wa, wb = jnp.exp2(a[0] - top), jnp.exp2(b[0] - top)
        return top, wa * a[1] + wb * b[1], wa * a[2] + wb * b[2]

    def get_part(c, h):
        return part_stat[c, h, 0:1], part_stat[c, h, 1:2], part_acc[c, h]

    def put_part(c, h, part):
        part_stat[c, h, 0:1] = part[0]
        part_stat[c, h, 1:2] = part[1]
        part_acc[c, h] = part[2]

    def emit(c, h, part):
        @pl.when(c > z)
        def _():
            stat_out[c, h, 0:1] = part[0]
            stat_out[c, h, 1:2] = part[1]
            acc_out[c, h] = part[2].astype(jnp.bfloat16)
            pass_acc(c, h).start()
            pass_stat(c, h).start()

        @pl.when(c == z)
        def _():
            att[x * heads + h, tok_half] = (part[2] / part[1]).T.astype(jnp.bfloat16)
            for other in others:
                att_piece(other, h).start()
            att_pair(x, h, tok_half).start()

    def pass_on(h):
        def one(c):
            pass_q(c, h).wait_recv()

            @pl.when(z >= 2)
            def _():
                pass_q(c, h).start()

        down(one, z + 1)

        @pl.when((z >= 2) & (h + 1 < heads))
        def _():
            own_q(h + 1).start()

    @pl.when(z >= 2)
    def _():
        pass_on(0)

    def pass_w(i):
        for other in others:
            x_wait(other, i)
            for dy in range(1, n_str):
                y_piece(other, dy, i).start()

    def head_step(h):
        @pl.when((z >= 2) & (h + 1 < heads))
        def _():
            pass_on(h + 1)

        @pl.when(z == 1)
        def _():
            zero_k(h).wait_recv()
            fwd_k(h, tok_half).start()
            zero_v(h).wait_recv()
            fwd_v(h, tok_half).start()
            pass_on(h)

        @pl.when(block_core(x) == s)
        def _():
            own_copy(h).start()
            own_share(h).start()

        load_q(h).wait()
        load_k(h).wait()
        load_v(h).wait()
        sib_k(h, sib_half).wait_recv()
        sib_v(h, sib_half).wait_recv()

        k_here = k_own[h]
        v_here = v_own[h].T

        @pl.when(z != 1)
        def _():
            def own_block(c):
                put_part(c, h, block(q_all[c, h], [k_here], v_here, [mask_ref[c, z]]))

            down(own_block, z)

        @pl.when(z == 1)
        def _():
            fwd_k(h, sib_half).wait_recv()
            fwd_v(h, sib_half).wait_recv()
            keys = [k_here, k_zero[h]]
            both = jnp.concatenate([v_here, v_zero[h].T], axis=1)
            group = 3 if (n_span - 1) % 3 == 0 else 1

            def first_blocks(i, carry):
                spans = [n_span - 1 - i * group - j for j in range(group)]
                parts = [
                    block(q_all[c, h], keys, both, [mask_ref[c, 1], mask_ref[c, 0]]) for c in spans
                ]
                for c, part in zip(spans, parts):
                    put_part(c, h, part)
                return carry

            lax.fori_loop(0, (n_span - 1) // group, first_blocks, 0)
            down(lambda c: emit(c, h, get_part(c, h)), 1)

        @pl.when(z == 0)
        def _():
            emit(z, h, get_part(z, h))

        @pl.when(z == 0)
        def _():
            pass_w(h)

        @pl.when((z == 1) & (h > 1))
        def _():
            pass_w(h - 2)

        @pl.when((z >= 2) & ((h == 2) | (h == 4)))
        def _():
            pass_w(h // 2 - 1)

    each_head(head_step)

    @pl.when(z == 1)
    def _():
        pass_w(heads - 2)
        pass_w(heads - 1)

    @pl.when(z >= 2)
    def _():
        def merge_step(h):
            def one(c):
                pass_acc(c, h).wait_recv()
                pass_stat(c, h).wait_recv()
                before = (
                    stat_in[c, h, 0:1],
                    stat_in[c, h, 1:2],
                    acc_in[c, h].astype(jnp.float32),
                )
                emit(c, h, merge(get_part(c, h), before))

            down(one, z)

            @pl.when(h + 2 < heads)
            def _():
                pass_w(h + 2)

        each_head(merge_step)

    for other in others:

        def pass_att(h, other=other):
            att_wait(other, h)
            att_pair(other, h, tok_half).start()

        each_head(pass_att)

    @pl.when(block_core(x) == s)
    def _():
        each_head(lambda i: own_copy(i).wait())

    @pl.when(block_core(x) != s)
    def _():
        each_head(lambda i: own_share(i).wait_recv())

    def last_waits(h):
        for other in others:
            for dy in range(1, n_str):
                y_wait(other, dy, h)
            att_pair(other, h, sib_half).wait_recv()
        att_pair(x, h, sib_half).wait_recv()

    each_head(last_waits)

    step = step_ref[z]

    def gathered(rows):
        return jnp.concatenate([att[i, rows] for i in range(n_head * heads)], axis=1)

    attended = jnp.concatenate([gathered(sib_half), gathered(tok_half)], axis=0)

    def project(t, carry):
        at = pl.ds(pl.multiple_of(t * tile, tile), tile)
        projected = jnp.dot(attended, w_full[:, at], preferred_element_type=jnp.float32)
        here = out_cols(s, t)
        gate_row = jnp.zeros((1, tile), jnp.float32)
        for i in range(gate_ref.shape[0]):
            gate_row = jnp.where(step == i, gate_ref[i : i + 1, here], gate_row)
        gated = (gate_row * projected).astype(jnp.bfloat16)
        out_half[t] = gated[:tok]
        out_piece(s, t).start()
        out_ref[:, here] = gated[tok:]
        return carry

    lax.fori_loop(0, tiles, project, 0)

    def out_wait(t, carry):
        out_piece(sib, t).wait_recv()
        out_piece(s, t).wait_send()
        return carry

    lax.fori_loop(0, tiles, out_wait, 0)

    def sent(h):
        sib_k(h, tok_half).wait_send()
        sib_v(h, tok_half).wait_send()
        att_pair(x, h, tok_half).wait_send()
        for other in others:
            att_piece(other, h).wait_send()
            for dy in range(1, n_str):
                y_piece(other, dy, h).wait_send()
            att_pair(other, h, tok_half).wait_send()

            @pl.when(block_core(other) == s)
            def _(other=other):
                for sub in range(n_seq):
                    x_piece(other, sub, h).wait_send()

        @pl.when(block_core(x) == s)
        def _():
            own_share(h).wait_send()

        @pl.when(z == 0)
        def _():
            zero_k(h).wait_send()
            zero_v(h).wait_send()

        @pl.when(z == 1)
        def _():
            fwd_k(h, tok_half).wait_send()
            fwd_v(h, tok_half).wait_send()

        @pl.when(z >= 2)
        def _():
            own_q(h).wait_send()
            down(lambda c: pass_q(c, h).wait_send(), z + 1)

        @pl.when(z >= 1)
        def _():
            down(lambda c: (pass_acc(c, h).wait_send(), pass_stat(c, h).wait_send()), z + 1)

    each_head(sent)


def solution(mesh):
    n_str, n_span = mesh.shape["streams"], mesh.shape["span"]
    n_head, n_seq = mesh.shape["head"], mesh.shape["seq"]
    sizes = (n_str, n_span, n_head, n_seq)

    def on_device(query_rows, key_rows, value_rows, out_weight, gate_table, step_index, block_mask):
        tok = query_rows.shape[0]
        heads = query_rows.shape[1] // HD
        cols = gate_table.shape[1]
        half = cols // n_seq
        tile = 256 if half % 256 == 0 else 128
        tiles = half // tile
        vmem, any_space = pltpu.VMEM, pl.ANY
        dma = pltpu.SemaphoreType.DMA
        low, wide = jnp.bfloat16, jnp.float32
        flops = 4 * heads * tok * tok * n_seq * n_span * HD + 2 * tok * n_head * heads * HD * cols
        return pl.pallas_call(
            functools.partial(kernel, sizes),
            out_shape=jax.ShapeDtypeStruct((tok, cols), low),
            in_specs=[
                pl.BlockSpec(memory_space=pltpu.SMEM),
                pl.BlockSpec(memory_space=pltpu.SMEM),
                pl.BlockSpec(memory_space=any_space),
                pl.BlockSpec(memory_space=any_space),
                pl.BlockSpec(memory_space=any_space),
                pl.BlockSpec(memory_space=any_space),
                pl.BlockSpec(memory_space=vmem),
            ],
            out_specs=pl.BlockSpec(memory_space=vmem),
            scratch_shapes=[
                vmem((n_span, heads, tok, HD), low),
                vmem((heads, n_seq * tok, HD), low),
                vmem((heads, n_seq * tok, HD), low),
                vmem((heads, n_seq * tok, HD), low),
                vmem((heads, n_seq * tok, HD), low),
                vmem((n_span, heads, HD, tok), wide),
                vmem((n_span, heads, 8, tok), wide),
                vmem((n_span, heads, HD, tok), low),
                vmem((n_span, heads, 8, tok), wide),
                vmem((n_span, heads, HD, tok), low),
                vmem((n_span, heads, 8, tok), wide),
                vmem((n_head * heads, n_seq * tok, HD), low),
                vmem((n_head * heads * HD, half), low),
                vmem((tiles, tok, tile), low),
                dma((3, heads)),
                dma((2, heads)),
                dma((2, heads)),
                dma((2, heads)),
                dma((2, heads)),
                dma((2, heads)),
                dma((2, heads)),
                dma((n_span, heads)),
                dma((n_span, heads)),
                dma((n_span, heads)),
                dma((n_span, heads)),
                dma((n_span, heads)),
                dma((n_span, heads)),
                dma((n_head, n_seq, heads)),
                dma((n_head, heads)),
                dma((n_head, n_str, heads)),
                dma((n_head, n_str, heads)),
                dma((heads,)),
                dma((heads,)),
                dma((heads,)),
                dma((n_head, heads)),
                dma((n_head, heads)),
                dma((n_head, heads)),
                dma((n_head, heads)),
                dma((tiles,)),
                dma((tiles,)),
            ],
            compiler_params=pltpu.CompilerParams(
                collective_id=0, has_side_effects=True, vmem_limit_bytes=56 * 1024 * 1024
            ),
            cost_estimate=pl.CostEstimate(
                flops=flops, bytes_accessed=6 * out_weight.size, transcendentals=0
            ),
        )(step_index, block_mask, query_rows, key_rows, value_rows, out_weight, gate_table)

    in_specs = (
        P(("streams", "span", "seq"), "head"),
        P(("streams", "span", "seq"), "head"),
        P(("streams", "span", "seq"), "head"),
        P("head", "seq"),
        P(None, "head"),
        P("streams"),
        P("streams", None),
    )
    out_specs = P(("streams", "span", "seq"), "head")
    return jax.shard_map(
        on_device, mesh=mesh, in_specs=in_specs, out_specs=out_specs, check_vma=False
    )
```

```python
import functools
import math

import jax
import jax.numpy as jnp
from jax import lax
from jax.experimental import pallas as pl
from jax.experimental.pallas import tpu as pltpu
from jax.sharding import PartitionSpec as P

HD = 128
NEG_FLOOR = -1e30
MESH = pl.DeviceIdType.MESH
SCORE_SCALE = math.log2(math.e) / math.sqrt(HD)


def kernel(
    sizes,
    step_ref,
    mask_ref,
    q_ref,
    k_ref,
    v_ref,
    w_ref,
    gate_ref,
    out_ref,
    q_all,
    k_own,
    v_own,
    k_zero,
    v_zero,
    part_acc,
    part_stat,
    acc_out,
    stat_out,
    acc_in,
    stat_in,
    att,
    w_full,
    out_half,
    w_relay,
    relay_send,
    relay_recv,
    load_sem,
    sib_send,
    sib_recv,
    zero_send,
    zero_recv,
    fwd_send,
    fwd_recv,
    q_send,
    q_recv,
    acc_send,
    acc_recv,
    stat_send,
    stat_recv,
    x_send,
    x_recv,
    y_send,
    y_recv,
    own_load,
    own_send,
    own_recv,
    att_send,
    att_recv,
    pair_send,
    pair_recv,
    out_send,
    out_recv,
):
    n_str, n_span, n_head, n_seq = sizes
    y = lax.axis_index("streams")
    z = lax.axis_index("span")
    x = lax.axis_index("head")
    s = lax.axis_index("seq")
    sib = 1 - s
    tok = q_ref.shape[0]
    heads = q_ref.shape[1] // HD
    w_rows = w_ref.shape[0]
    cols = out_ref.shape[1]
    half = cols // n_seq
    tile = 256 if half % 256 == 0 else 128
    tiles = half // tile
    y_rows = w_rows // n_str
    piece = y_rows // heads
    own_piece = w_rows // heads

    def remote(src, dst, ss, rs, **where):
        return pltpu.make_async_remote_copy(
            src_ref=src, dst_ref=dst, send_sem=ss, recv_sem=rs, device_id=where, device_id_type=MESH
        )

    def head_cols(h):
        return pl.ds(pl.multiple_of(h * HD, HD), HD)

    def each_head(body):
        lax.fori_loop(0, heads, lambda h, c: (body(h), c)[1], 0)

    def down(body, low):
        lax.fori_loop(0, n_span - low, lambda i, c: (body(n_span - 1 - i), c)[1], 0)

    tok_half = pl.ds(pl.multiple_of(s * tok, tok), tok)
    sib_half = pl.ds(pl.multiple_of(sib * tok, tok), tok)

    def load_q(h):
        return pltpu.make_async_copy(q_ref.at[:, head_cols(h)], q_all.at[z, h], load_sem.at[0, h])

    def load_k(h):
        return pltpu.make_async_copy(
            k_ref.at[:, head_cols(h)], k_own.at[h, tok_half], load_sem.at[1, h]
        )

    def load_v(h):
        return pltpu.make_async_copy(
            v_ref.at[:, head_cols(h)], v_own.at[h, tok_half], load_sem.at[2, h]
        )

    def sib_k(h, half):
        return remote(
            k_own.at[h, half], k_own.at[h, half], sib_send.at[0, h], sib_recv.at[0, h], seq=sib
        )

    def sib_v(h, half):
        return remote(
            v_own.at[h, half], v_own.at[h, half], sib_send.at[1, h], sib_recv.at[1, h], seq=sib
        )

    def zero_k(h):
        return remote(
            k_own.at[h, tok_half], k_zero.at[h, tok_half], zero_send.at[0, h], zero_recv.at[0, h], span=1
        )

    def zero_v(h):
        return remote(
            v_own.at[h, tok_half], v_zero.at[h, tok_half], zero_send.at[1, h], zero_recv.at[1, h], span=1
        )

    def fwd_k(h, half):
        return remote(
            k_zero.at[h, half], k_zero.at[h, half], fwd_send.at[0, h], fwd_recv.at[0, h], seq=sib
        )

    def fwd_v(h, half):
        return remote(
            v_zero.at[h, half], v_zero.at[h, half], fwd_send.at[1, h], fwd_recv.at[1, h], seq=sib
        )

    def pass_q(c, h):
        return remote(q_all.at[c, h], q_all.at[c, h], q_send.at[c, h], q_recv.at[c, h], span=z - 1)

    def pass_acc(c, h):
        return remote(
            acc_out.at[c, h], acc_in.at[c, h], acc_send.at[c, h], acc_recv.at[c, h], span=z + 1
        )

    def pass_stat(c, h):
        return remote(
            stat_out.at[c, h], stat_in.at[c, h], stat_send.at[c, h], stat_recv.at[c, h], span=z + 1
        )

    def w_at(src_x, part, i):
        first = src_x * w_rows + part * y_rows + i * piece
        return w_full.at[pl.ds(pl.multiple_of(first, piece), piece)]

    def block_core(dst_x):
        return (dst_x * n_seq) // n_head

    def block_cols(dst_x, core):
        first = lax.rem(dst_x, n_head // n_seq) * cols + core * half
        return pl.ds(pl.multiple_of(first, HD), half)

    def x_piece(dst_x, i):
        first = y * y_rows + i * piece
        return remote(
            w_ref.at[pl.ds(pl.multiple_of(first, piece), piece), block_cols(dst_x, s)],
            w_at(x, y, i),
            x_send.at[dst_x, i],
            x_recv.at[x, i],
            head=dst_x,
        )

    def relay(dst_x, i):
        first = y * y_rows + i * piece
        return remote(
            w_ref.at[pl.ds(pl.multiple_of(first, piece), piece), block_cols(dst_x, sib)],
            w_relay.at[dst_x, i],
            relay_send.at[dst_x, i],
            relay_recv.at[dst_x, i],
            seq=sib,
        )

    def x_relayed(dst_x, i):
        return remote(
            w_relay.at[dst_x, i],
            w_at(x, y, i),
            x_send.at[dst_x, i],
            x_recv.at[x, i],
            head=dst_x,
        )

    def x_wait(src_x, i):
        ref = w_at(src_x, y, i)
        remote(ref, ref, x_send.at[src_x, i], x_recv.at[src_x, i], head=src_x).wait_recv()

    def y_piece(src_x, dy, i):
        ref = w_at(src_x, y, i)
        return remote(
            ref, ref, y_send.at[src_x, dy, i], y_recv.at[src_x, dy, i], streams=lax.rem(y + dy, n_str)
        )

    def y_wait(src_x, dy, i):
        from_y = lax.rem(y - dy + n_str, n_str)
        ref = w_at(src_x, from_y, i)
        remote(
            ref, ref, y_send.at[src_x, dy, i], y_recv.at[src_x, dy, i], streams=from_y
        ).wait_recv()

    def own_rows(i):
        return pl.ds(pl.multiple_of(i * own_piece, own_piece), own_piece)

    def own_at(i):
        first = x * w_rows + i * own_piece
        return w_full.at[pl.ds(pl.multiple_of(first, own_piece), own_piece)]

    def own_copy(i):
        return pltpu.make_async_copy(
            w_ref.at[own_rows(i), block_cols(x, s)], own_at(i), own_load.at[i]
        )

    def own_share(i):
        return remote(
            w_ref.at[own_rows(i), block_cols(x, sib)], own_at(i), own_send.at[i], own_recv.at[i], seq=sib
        )

    def att_piece(dst_x, h):
        ref = att.at[x * heads + h, tok_half]
        return remote(ref, ref, att_send.at[dst_x, h], att_recv.at[x, h], head=dst_x)

    def att_wait(src_x, h):
        ref = att.at[src_x * heads + h, tok_half]
        remote(ref, ref, att_send.at[src_x, h], att_recv.at[src_x, h], head=src_x).wait_recv()

    def att_pair(src_x, h, rows):
        ref = att.at[src_x * heads + h, rows]
        return remote(ref, ref, pair_send.at[src_x, h], pair_recv.at[src_x, h], seq=sib)

    def out_cols(core, t):
        return pl.ds(pl.multiple_of(core * half + t * tile, tile), tile)

    def out_piece(core, t):
        return remote(
            out_half.at[t], out_ref.at[:, out_cols(core, t)], out_send.at[t], out_recv.at[t], seq=sib
        )

    others = [lax.rem(x + dx, n_head) for dx in range(1, n_head)]

    barrier = pltpu.get_barrier_semaphore()

    def greet(**where):
        pl.semaphore_signal(barrier, inc=1, device_id=where, device_id_type=MESH)

    greet(seq=sib)
    for other in others:
        for core in range(n_seq):
            greet(head=other, seq=core)
    for dy in range(1, n_str):
        greet(streams=lax.rem(y + dy, n_str))

    @pl.when(z > 0)
    def _():
        greet(span=z - 1)

    @pl.when(z < n_span - 1)
    def _():
        greet(span=z + 1)

    each_head(lambda h: (load_q(h).start(), load_k(h).start(), load_v(h).start()))
    beside = jnp.where(z > 0, 1, 0) + jnp.where(z < n_span - 1, 1, 0)
    pl.semaphore_wait(barrier, 1 + n_seq * (n_head - 1) + (n_str - 1) + beside)

    each_head(lambda h: (load_q(h).wait(), load_k(h).wait(), load_v(h).wait()))

    @pl.when(z >= 2)
    def _():
        pass_q(z, 0).start()

    @pl.when(z == 0)
    def _():
        each_head(lambda h: (zero_k(h).start(), zero_v(h).start()))

    each_head(lambda h: (sib_k(h, tok_half).start(), sib_v(h, tok_half).start()))
    for other in others:

        @pl.when(block_core(other) == s)
        def _(other=other):
            each_head(lambda i: (relay(other, i).start(), x_piece(other, i).start()))

    def block(q, keys, v_t, flags):
        scores = [
            lax.dot_general(k, q, (((1,), (1,)), ((), ())), preferred_element_type=jnp.float32)
            * SCORE_SCALE
            for k in keys
        ]
        tops = [
            jnp.where(flag == 1, jnp.max(each, axis=0, keepdims=True), NEG_FLOOR)
            for each, flag in zip(scores, flags)
        ]
        top = functools.reduce(jnp.maximum, tops)
        probs = [
            jnp.exp2(each - jnp.where(flag == 1, top, -NEG_FLOOR))
            for each, flag in zip(scores, flags)
        ]
        total = sum(jnp.sum(each, axis=0, keepdims=True) for each in probs)
        low = jnp.concatenate([each.astype(jnp.bfloat16) for each in probs], axis=0)
        return top, total, jnp.dot(v_t, low, preferred_element_type=jnp.float32)

    def merge(a, b):
        top = jnp.maximum(a[0], b[0])
        wa, wb = jnp.exp2(a[0] - top), jnp.exp2(b[0] - top)
        return top, wa * a[1] + wb * b[1], wa * a[2] + wb * b[2]

    def get_part(c, h):
        return part_stat[c, h, 0:1], part_stat[c, h, 1:2], part_acc[c, h]

    def put_part(c, h, part):
        part_stat[c, h, 0:1] = part[0]
        part_stat[c, h, 1:2] = part[1]
        part_acc[c, h] = part[2]

    def emit(c, h, part):
        @pl.when(c > z)
        def _():
            stat_out[c, h, 0:1] = part[0]
            stat_out[c, h, 1:2] = part[1]
            acc_out[c, h] = part[2].astype(jnp.bfloat16)
            pass_acc(c, h).start()
            pass_stat(c, h).start()

        @pl.when(c == z)
        def _():
            att[x * heads + h, tok_half] = (part[2] / part[1]).T.astype(jnp.bfloat16)
            for other in others:
                att_piece(other, h).start()
            att_pair(x, h, tok_half).start()

    def pass_on(h):
        def one(c):
            pass_q(c, h).wait_recv()

            @pl.when(z >= 2)
            def _():
                pass_q(c, h).start()

        down(one, z + 1)

        @pl.when((z >= 2) & (h + 1 < heads))
        def _():
            pass_q(z, h + 1).start()

    @pl.when(z >= 2)
    def _():
        pass_on(0)

    def pass_w(i):
        for other in others:
            x_wait(other, i)
            for dy in range(1, n_str):
                y_piece(other, dy, i).start()

    for other in others:

        @pl.when(block_core(other) != s)
        def _(other=other):
            each_head(lambda i: (relay(other, i).wait_recv(), x_relayed(other, i).start()))

    def head_step(h):
        @pl.when((z >= 2) & (h + 1 < heads))
        def _():
            pass_on(h + 1)

        @pl.when(z == 1)
        def _():
            zero_k(h).wait_recv()
            fwd_k(h, tok_half).start()
            zero_v(h).wait_recv()
            fwd_v(h, tok_half).start()
            pass_on(h)

        @pl.when(block_core(x) == s)
        def _():
            own_copy(h).start()
            own_share(h).start()

        sib_k(h, sib_half).wait_recv()
        sib_v(h, sib_half).wait_recv()

        k_here = k_own[h]
        v_here = v_own[h].T

        @pl.when(z != 1)
        def _():
            def own_block(c):
                put_part(c, h, block(q_all[c, h], [k_here], v_here, [mask_ref[c, z]]))

            down(own_block, z)

        @pl.when(z == 1)
        def _():
            fwd_k(h, sib_half).wait_recv()
            fwd_v(h, sib_half).wait_recv()
            keys = [k_here, k_zero[h]]
            both = jnp.concatenate([v_here, v_zero[h].T], axis=1)
            group = 3 if (n_span - 1) % 3 == 0 else 1

            def first_blocks(i, carry):
                spans = [n_span - 1 - i * group - j for j in range(group)]
                parts = [
                    block(q_all[c, h], keys, both, [mask_ref[c, 1], mask_ref[c, 0]]) for c in spans
                ]
                for c, part in zip(spans, parts):
                    put_part(c, h, part)
                return carry

            lax.fori_loop(0, (n_span - 1) // group, first_blocks, 0)
            down(lambda c: emit(c, h, get_part(c, h)), 1)

        @pl.when(z == 0)
        def _():
            emit(z, h, get_part(z, h))

        @pl.when(z == 0)
        def _():
            pass_w(h)

        @pl.when((z == 1) & (h > 0))
        def _():
            pass_w(h - 1)

        @pl.when((z >= 2) & ((h == 2) | (h == 4)))
        def _():
            pass_w(h // 2 - 1)

    each_head(head_step)

    @pl.when(z == 1)
    def _():
        pass_w(heads - 1)

    @pl.when(z >= 2)
    def _():
        def merge_step(h):
            def one(c):
                pass_acc(c, h).wait_recv()
                pass_stat(c, h).wait_recv()
                before = (
                    stat_in[c, h, 0:1],
                    stat_in[c, h, 1:2],
                    acc_in[c, h].astype(jnp.float32),
                )
                emit(c, h, merge(get_part(c, h), before))

            down(one, z)

            @pl.when(h + 2 < heads)
            def _():
                pass_w(h + 2)

        each_head(merge_step)

    for other in others:

        def pass_att(h, other=other):
            att_wait(other, h)
            att_pair(other, h, tok_half).start()

        each_head(pass_att)

    @pl.when(block_core(x) == s)
    def _():
        each_head(lambda i: own_copy(i).wait())

    @pl.when(block_core(x) != s)
    def _():
        each_head(lambda i: own_share(i).wait_recv())

    def last_waits(h):
        for other in others:
            for dy in range(1, n_str):
                y_wait(other, dy, h)
            att_pair(other, h, sib_half).wait_recv()
        att_pair(x, h, sib_half).wait_recv()

    each_head(last_waits)

    step = step_ref[z]

    def gathered(rows):
        return jnp.concatenate([att[i, rows] for i in range(n_head * heads)], axis=1)

    attended = jnp.concatenate([gathered(sib_half), gathered(tok_half)], axis=0)

    def project(t, carry):
        at = pl.ds(pl.multiple_of(t * tile, tile), tile)
        projected = jnp.dot(attended, w_full[:, at], preferred_element_type=jnp.float32)
        here = out_cols(s, t)
        gate_row = jnp.zeros((1, tile), jnp.float32)
        for i in range(gate_ref.shape[0]):
            gate_row = jnp.where(step == i, gate_ref[i : i + 1, here], gate_row)
        gated = (gate_row * projected).astype(jnp.bfloat16)
        out_half[t] = gated[:tok]
        out_piece(s, t).start()
        out_ref[:, here] = gated[tok:]
        return carry

    lax.fori_loop(0, tiles, project, 0)

    def out_wait(t, carry):
        out_piece(sib, t).wait_recv()
        out_piece(s, t).wait_send()
        return carry

    lax.fori_loop(0, tiles, out_wait, 0)

    def sent(h):
        sib_k(h, tok_half).wait_send()
        sib_v(h, tok_half).wait_send()
        att_pair(x, h, tok_half).wait_send()
        for other in others:
            att_piece(other, h).wait_send()
            for dy in range(1, n_str):
                y_piece(other, dy, h).wait_send()
            att_pair(other, h, tok_half).wait_send()

            x_piece(other, h).wait_send()

            @pl.when(block_core(other) == s)
            def _(other=other):
                relay(other, h).wait_send()

        @pl.when(block_core(x) == s)
        def _():
            own_share(h).wait_send()

        @pl.when(z == 0)
        def _():
            zero_k(h).wait_send()
            zero_v(h).wait_send()

        @pl.when(z == 1)
        def _():
            fwd_k(h, tok_half).wait_send()
            fwd_v(h, tok_half).wait_send()

        @pl.when(z >= 2)
        def _():
            down(lambda c: pass_q(c, h).wait_send(), z)

        @pl.when(z >= 1)
        def _():
            down(lambda c: (pass_acc(c, h).wait_send(), pass_stat(c, h).wait_send()), z + 1)

    each_head(sent)


def solution(mesh):
    n_str, n_span = mesh.shape["streams"], mesh.shape["span"]
    n_head, n_seq = mesh.shape["head"], mesh.shape["seq"]
    sizes = (n_str, n_span, n_head, n_seq)

    def on_device(query_rows, key_rows, value_rows, out_weight, gate_table, step_index, block_mask):
        tok = query_rows.shape[0]
        heads = query_rows.shape[1] // HD
        cols = gate_table.shape[1]
        half = cols // n_seq
        tile = 256 if half % 256 == 0 else 128
        tiles = half // tile
        piece = out_weight.shape[0] // n_str // heads
        vmem, any_space = pltpu.VMEM, pl.ANY
        dma = pltpu.SemaphoreType.DMA
        low, wide = jnp.bfloat16, jnp.float32
        flops = 4 * heads * tok * tok * n_seq * n_span * HD + 2 * tok * n_head * heads * HD * cols
        return pl.pallas_call(
            functools.partial(kernel, sizes),
            out_shape=jax.ShapeDtypeStruct((tok, cols), low),
            in_specs=[
                pl.BlockSpec(memory_space=pltpu.SMEM),
                pl.BlockSpec(memory_space=pltpu.SMEM),
                pl.BlockSpec(memory_space=any_space),
                pl.BlockSpec(memory_space=any_space),
                pl.BlockSpec(memory_space=any_space),
                pl.BlockSpec(memory_space=any_space),
                pl.BlockSpec(memory_space=vmem),
            ],
            out_specs=pl.BlockSpec(memory_space=vmem),
            scratch_shapes=[
                vmem((n_span, heads, tok, HD), low),
                vmem((heads, n_seq * tok, HD), low),
                vmem((heads, n_seq * tok, HD), low),
                vmem((heads, n_seq * tok, HD), low),
                vmem((heads, n_seq * tok, HD), low),
                vmem((n_span, heads, HD, tok), wide),
                vmem((n_span, heads, 8, tok), wide),
                vmem((n_span, heads, HD, tok), low),
                vmem((n_span, heads, 8, tok), wide),
                vmem((n_span, heads, HD, tok), low),
                vmem((n_span, heads, 8, tok), wide),
                vmem((n_head * heads, n_seq * tok, HD), low),
                vmem((n_head * heads * HD, half), low),
                vmem((tiles, tok, tile), low),
                vmem((n_head, heads, piece, half), low),
                dma((n_head, heads)),
                dma((n_head, heads)),
                dma((3, heads)),
                dma((2, heads)),
                dma((2, heads)),
                dma((2, heads)),
                dma((2, heads)),
                dma((2, heads)),
                dma((2, heads)),
                dma((n_span, heads)),
                dma((n_span, heads)),
                dma((n_span, heads)),
                dma((n_span, heads)),
                dma((n_span, heads)),
                dma((n_span, heads)),
                dma((n_head, heads)),
                dma((n_head, heads)),
                dma((n_head, n_str, heads)),
                dma((n_head, n_str, heads)),
                dma((heads,)),
                dma((heads,)),
                dma((heads,)),
                dma((n_head, heads)),
                dma((n_head, heads)),
                dma((n_head, heads)),
                dma((n_head, heads)),
                dma((tiles,)),
                dma((tiles,)),
            ],
            compiler_params=pltpu.CompilerParams(
                collective_id=0, has_side_effects=True, vmem_limit_bytes=56 * 1024 * 1024
            ),
            cost_estimate=pl.CostEstimate(
                flops=flops, bytes_accessed=6 * out_weight.size, transcendentals=0
            ),
        )(step_index, block_mask, query_rows, key_rows, value_rows, out_weight, gate_table)

    in_specs = (
        P(("streams", "span", "seq"), "head"),
        P(("streams", "span", "seq"), "head"),
        P(("streams", "span", "seq"), "head"),
        P("head", "seq"),
        P(None, "head"),
        P("streams"),
        P("streams", None),
    )
    out_specs = P(("streams", "span", "seq"), "head")
    return jax.shard_map(
        on_device, mesh=mesh, in_specs=in_specs, out_specs=out_specs, check_vma=False
    )
```

```python
import functools
import math

import jax
import jax.numpy as jnp
from jax import lax
from jax.experimental import pallas as pl
from jax.experimental.pallas import tpu as pltpu
from jax.sharding import PartitionSpec as P

HD = 128
NEG_FLOOR = -1e30
MESH = pl.DeviceIdType.MESH
SCORE_SCALE = math.log2(math.e) / math.sqrt(HD)


def kernel(
    sizes,
    step_ref,
    mask_ref,
    q_ref,
    k_ref,
    v_ref,
    w_ref,
    gate_ref,
    out_ref,
    q_all,
    k_own,
    v_own,
    k_zero,
    v_zero,
    part_acc,
    part_stat,
    acc_out,
    stat_out,
    acc_in,
    stat_in,
    att,
    w_full,
    out_half,
    w_relay,
    v_turned,
    projected,
    relay_send,
    relay_recv,
    load_sem,
    sib_send,
    sib_recv,
    zero_send,
    zero_recv,
    fwd_send,
    fwd_recv,
    q_send,
    q_recv,
    acc_send,
    acc_recv,
    stat_send,
    stat_recv,
    x_send,
    x_recv,
    y_send,
    y_recv,
    own_load,
    own_send,
    own_recv,
    att_send,
    att_recv,
    pair_send,
    pair_recv,
    out_send,
    out_recv,
):
    n_str, n_span, n_head, n_seq = sizes
    y = lax.axis_index("streams")
    z = lax.axis_index("span")
    x = lax.axis_index("head")
    s = lax.axis_index("seq")
    sib = 1 - s
    tok = q_ref.shape[0]
    heads = q_ref.shape[1] // HD
    w_rows = w_ref.shape[0]
    cols = out_ref.shape[1]
    half = cols // n_seq
    tile = 256 if half % 256 == 0 else 128
    tiles = half // tile
    y_rows = w_rows // n_str
    piece = y_rows // heads
    own_piece = w_rows // heads

    def remote(src, dst, ss, rs, **where):
        return pltpu.make_async_remote_copy(
            src_ref=src, dst_ref=dst, send_sem=ss, recv_sem=rs, device_id=where, device_id_type=MESH
        )

    def head_cols(h):
        return pl.ds(pl.multiple_of(h * HD, HD), HD)

    def each_head(body):
        lax.fori_loop(0, heads, lambda h, c: (body(h), c)[1], 0)

    def down(body, low):
        lax.fori_loop(0, n_span - low, lambda i, c: (body(n_span - 1 - i), c)[1], 0)

    tok_half = pl.ds(pl.multiple_of(s * tok, tok), tok)
    sib_half = pl.ds(pl.multiple_of(sib * tok, tok), tok)

    def load_q(h):
        return pltpu.make_async_copy(q_ref.at[:, head_cols(h)], q_all.at[z, h], load_sem.at[0, h])

    def load_k(h):
        return pltpu.make_async_copy(
            k_ref.at[:, head_cols(h)], k_own.at[h, tok_half], load_sem.at[1, h]
        )

    def load_v(h):
        return pltpu.make_async_copy(
            v_ref.at[:, head_cols(h)], v_own.at[h, tok_half], load_sem.at[2, h]
        )

    def sib_k(h, half):
        return remote(
            k_own.at[h, half], k_own.at[h, half], sib_send.at[0, h], sib_recv.at[0, h], seq=sib
        )

    def sib_v(h, half):
        return remote(
            v_own.at[h, half], v_own.at[h, half], sib_send.at[1, h], sib_recv.at[1, h], seq=sib
        )

    def zero_k(h):
        return remote(
            k_own.at[h, tok_half], k_zero.at[h, tok_half], zero_send.at[0, h], zero_recv.at[0, h], span=1
        )

    def zero_v(h):
        return remote(
            v_own.at[h, tok_half], v_zero.at[h, tok_half], zero_send.at[1, h], zero_recv.at[1, h], span=1
        )

    def fwd_k(h, half):
        return remote(
            k_zero.at[h, half], k_zero.at[h, half], fwd_send.at[0, h], fwd_recv.at[0, h], seq=sib
        )

    def fwd_v(h, half):
        return remote(
            v_zero.at[h, half], v_zero.at[h, half], fwd_send.at[1, h], fwd_recv.at[1, h], seq=sib
        )

    def pass_q(c, h):
        return remote(q_all.at[c, h], q_all.at[c, h], q_send.at[c, h], q_recv.at[c, h], span=z - 1)

    def pass_acc(c, h):
        return remote(
            acc_out.at[c, h], acc_in.at[c, h], acc_send.at[c, h], acc_recv.at[c, h], span=z + 1
        )

    def pass_stat(c, h):
        return remote(
            stat_out.at[c, h], stat_in.at[c, h], stat_send.at[c, h], stat_recv.at[c, h], span=z + 1
        )

    def w_at(src_x, part, i):
        first = src_x * w_rows + part * y_rows + i * piece
        return w_full.at[pl.ds(pl.multiple_of(first, piece), piece)]

    def block_core(dst_x):
        return (dst_x * n_seq) // n_head

    def block_cols(dst_x, core):
        first = lax.rem(dst_x, n_head // n_seq) * cols + core * half
        return pl.ds(pl.multiple_of(first, HD), half)

    def x_piece(dst_x, i):
        first = y * y_rows + i * piece
        return remote(
            w_ref.at[pl.ds(pl.multiple_of(first, piece), piece), block_cols(dst_x, s)],
            w_at(x, y, i),
            x_send.at[dst_x, i],
            x_recv.at[x, i],
            head=dst_x,
        )

    def relay(dst_x, i):
        first = y * y_rows + i * piece
        return remote(
            w_ref.at[pl.ds(pl.multiple_of(first, piece), piece), block_cols(dst_x, sib)],
            w_relay.at[dst_x, i],
            relay_send.at[dst_x, i],
            relay_recv.at[dst_x, i],
            seq=sib,
        )

    def x_relayed(dst_x, i):
        return remote(
            w_relay.at[dst_x, i],
            w_at(x, y, i),
            x_send.at[dst_x, i],
            x_recv.at[x, i],
            head=dst_x,
        )

    def x_wait(src_x, i):
        ref = w_at(src_x, y, i)
        remote(ref, ref, x_send.at[src_x, i], x_recv.at[src_x, i], head=src_x).wait_recv()

    def y_piece(src_x, dy, i):
        ref = w_at(src_x, y, i)
        return remote(
            ref, ref, y_send.at[src_x, dy, i], y_recv.at[src_x, dy, i], streams=lax.rem(y + dy, n_str)
        )

    def y_wait(src_x, dy, i):
        from_y = lax.rem(y - dy + n_str, n_str)
        ref = w_at(src_x, from_y, i)
        remote(
            ref, ref, y_send.at[src_x, dy, i], y_recv.at[src_x, dy, i], streams=from_y
        ).wait_recv()

    def own_rows(i):
        return pl.ds(pl.multiple_of(i * own_piece, own_piece), own_piece)

    def own_at(i):
        first = x * w_rows + i * own_piece
        return w_full.at[pl.ds(pl.multiple_of(first, own_piece), own_piece)]

    def own_copy(i):
        return pltpu.make_async_copy(
            w_ref.at[own_rows(i), block_cols(x, s)], own_at(i), own_load.at[i]
        )

    def own_share(i):
        return remote(
            w_ref.at[own_rows(i), block_cols(x, sib)], own_at(i), own_send.at[i], own_recv.at[i], seq=sib
        )

    def att_piece(dst_x, h):
        ref = att.at[x * heads + h, tok_half]
        return remote(ref, ref, att_send.at[dst_x, h], att_recv.at[x, h], head=dst_x)

    def att_wait(src_x, h):
        ref = att.at[src_x * heads + h, tok_half]
        remote(ref, ref, att_send.at[src_x, h], att_recv.at[src_x, h], head=src_x).wait_recv()

    def att_pair(src_x, h, rows):
        ref = att.at[src_x * heads + h, rows]
        return remote(ref, ref, pair_send.at[src_x, h], pair_recv.at[src_x, h], seq=sib)

    def out_cols(core, t):
        return pl.ds(pl.multiple_of(core * half + t * tile, tile), tile)

    def out_piece(core, t):
        return remote(
            out_half.at[t], out_ref.at[:, out_cols(core, t)], out_send.at[t], out_recv.at[t], seq=sib
        )

    others = [lax.rem(x + dx, n_head) for dx in range(1, n_head)]

    barrier = pltpu.get_barrier_semaphore()

    def greet(**where):
        pl.semaphore_signal(barrier, inc=1, device_id=where, device_id_type=MESH)

    greet(seq=sib)
    for other in others:
        for core in range(n_seq):
            greet(head=other, seq=core)
    for dy in range(1, n_str):
        greet(streams=lax.rem(y + dy, n_str))

    @pl.when(z > 0)
    def _():
        greet(span=z - 1)

    @pl.when(z < n_span - 1)
    def _():
        greet(span=z + 1)

    each_head(lambda h: (load_q(h).start(), load_k(h).start(), load_v(h).start()))
    beside = jnp.where(z > 0, 1, 0) + jnp.where(z < n_span - 1, 1, 0)
    pl.semaphore_wait(barrier, 1 + n_seq * (n_head - 1) + (n_str - 1) + beside)

    each_head(lambda h: (load_q(h).wait(), load_k(h).wait(), load_v(h).wait()))

    @pl.when(z >= 2)
    def _():
        pass_q(z, 0).start()

    @pl.when(z == 0)
    def _():
        each_head(lambda h: (zero_k(h).start(), zero_v(h).start()))

    each_head(lambda h: (sib_k(h, tok_half).start(), sib_v(h, tok_half).start()))
    for other in others:

        @pl.when(block_core(other) == s)
        def _(other=other):
            each_head(lambda i: (relay(other, i).start(), x_piece(other, i).start()))

    def block(q, keys, v_t, flags):
        scores = [
            lax.dot_general(k, q, (((1,), (1,)), ((), ())), preferred_element_type=jnp.float32)
            * SCORE_SCALE
            for k in keys
        ]
        tops = [
            jnp.where(flag == 1, jnp.max(each, axis=0, keepdims=True), NEG_FLOOR)
            for each, flag in zip(scores, flags)
        ]
        top = functools.reduce(jnp.maximum, tops)
        probs = [
            jnp.exp2(each - jnp.where(flag == 1, top, -NEG_FLOOR))
            for each, flag in zip(scores, flags)
        ]
        total = sum(jnp.sum(each, axis=0, keepdims=True) for each in probs)
        low = jnp.concatenate([each.astype(jnp.bfloat16) for each in probs], axis=0)
        return top, total, jnp.dot(v_t, low, preferred_element_type=jnp.float32)

    def merge(a, b):
        top = jnp.maximum(a[0], b[0])
        wa, wb = jnp.exp2(a[0] - top), jnp.exp2(b[0] - top)
        return top, wa * a[1] + wb * b[1], wa * a[2] + wb * b[2]

    def get_part(c, h):
        return part_stat[c, h, 0:1], part_stat[c, h, 1:2], part_acc[c, h]

    def put_part(c, h, part):
        part_stat[c, h, 0:1] = part[0]
        part_stat[c, h, 1:2] = part[1]
        part_acc[c, h] = part[2]

    def emit(c, h, part):
        @pl.when(c > z)
        def _():
            stat_out[c, h, 0:1] = part[0]
            stat_out[c, h, 1:2] = part[1]
            acc_out[c, h] = part[2].astype(jnp.bfloat16)
            pass_acc(c, h).start()
            pass_stat(c, h).start()

        @pl.when(c == z)
        def _():
            att[x * heads + h, tok_half] = (part[2] / part[1]).T.astype(jnp.bfloat16)
            for other in others:
                att_piece(other, h).start()
            att_pair(x, h, tok_half).start()

    def pass_att(h):
        for other in others:
            att_wait(other, h)
            att_pair(other, h, tok_half).start()

    def pass_on(h):
        def one(c):
            pass_q(c, h).wait_recv()

            @pl.when(z >= 2)
            def _():
                pass_q(c, h).start()

        down(one, z + 1)

        @pl.when((z >= 2) & (h + 1 < heads))
        def _():
            pass_q(z, h + 1).start()

    @pl.when(z >= 2)
    def _():
        pass_on(0)

    def pass_w(i):
        for other in others:
            x_wait(other, i)
            for dy in range(1, n_str):
                y_piece(other, dy, i).start()

    for other in others:

        @pl.when(block_core(other) != s)
        def _(other=other):
            each_head(lambda i: (relay(other, i).wait_recv(), x_relayed(other, i).start()))

    def share_zero(h):
        zero_k(h).wait_recv()
        fwd_k(h, tok_half).start()
        zero_v(h).wait_recv()
        fwd_v(h, tok_half).start()

    @pl.when(z == 1)
    def _():
        share_zero(0)

    def zero_block(c, h, v_t):
        return block(q_all[c, h], [k_own[h], k_zero[h]], v_t, [mask_ref[c, 1], mask_ref[c, 0]])

    def head_step(h):
        @pl.when((z >= 2) & (h + 1 < heads))
        def _():
            pass_on(h + 1)

        @pl.when(z == 1)
        def _():
            pass_on(h)

        @pl.when(block_core(x) == s)
        def _():
            own_copy(h).start()
            own_share(h).start()

        sib_k(h, sib_half).wait_recv()
        sib_v(h, sib_half).wait_recv()

        k_here = k_own[h]
        v_here = v_own[h].T

        @pl.when(z != 1)
        def _():
            def own_block(c):
                put_part(c, h, block(q_all[c, h], [k_here], v_here, [mask_ref[c, z]]))

            down(own_block, z)

        @pl.when(z == 1)
        def _():
            fwd_k(h, sib_half).wait_recv()
            fwd_v(h, sib_half).wait_recv()
            both = jnp.concatenate([v_here, v_zero[h].T], axis=1)
            v_turned[h] = both

            def later(c):
                emit(c, h, zero_block(c, h, both))

                @pl.when((c == n_span - 1) & (h + 1 < heads))
                def _():
                    share_zero(h + 1)

            down(later, 2)

        @pl.when(z == 0)
        def _():
            emit(z, h, get_part(z, h))

        @pl.when(z == 0)
        def _():
            pass_w(h)

        @pl.when((z == 1) & (h > 0))
        def _():
            pass_w(h - 1)

        @pl.when((z >= 2) & ((h == 2) | (h == 4)))
        def _():
            pass_w(h // 2 - 1)

    each_head(head_step)

    @pl.when(z == 1)
    def _():
        def own_step(h):
            emit(1, h, zero_block(1, h, v_turned[h]))

            @pl.when(h == 0)
            def _():
                pass_w(heads - 1)

        each_head(own_step)

    @pl.when(z >= 2)
    def _():
        def merge_step(h):
            def one(c):
                pass_acc(c, h).wait_recv()
                pass_stat(c, h).wait_recv()
                before = (
                    stat_in[c, h, 0:1],
                    stat_in[c, h, 1:2],
                    acc_in[c, h].astype(jnp.float32),
                )
                emit(c, h, merge(get_part(c, h), before))

            down(one, z)

            @pl.when(h + 2 < heads)
            def _():
                pass_w(h + 2)

            @pl.when(h > 0)
            def _():
                pass_att(h - 1)

        each_head(merge_step)

    last = heads - 1

    @pl.when(z < 2)
    def _():
        lax.fori_loop(0, last, lambda h, c: (pass_att(h), c)[1], 0)

    @pl.when(block_core(x) == s)
    def _():
        each_head(lambda i: own_copy(i).wait())

    @pl.when(block_core(x) != s)
    def _():
        each_head(lambda i: own_share(i).wait_recv())

    def pair_wait(h):
        for other in others:
            att_pair(other, h, sib_half).wait_recv()
        att_pair(x, h, sib_half).wait_recv()

    def early_waits(h):
        for other in others:
            for dy in range(1, n_str):
                y_wait(other, dy, h)

        @pl.when(h < last)
        def _():
            pair_wait(h)

    each_head(early_waits)

    step = step_ref[z]

    def gathered(h_from, h_to):
        wanted = [src * heads + h for src in range(n_head) for h in range(h_from, h_to)]
        return jnp.concatenate(
            [
                jnp.concatenate([att[i, rows] for i in wanted], axis=1)
                for rows in (sib_half, tok_half)
            ],
            axis=0,
        )

    def weights(h_from, h_to, at):
        return jnp.concatenate(
            [w_full[(src * heads + h_from) * HD : (src * heads + h_to) * HD, at] for src in range(n_head)],
            axis=0,
        )

    def tile_at(t):
        return pl.ds(pl.multiple_of(t * tile, tile), tile)

    attended = gathered(0, last)

    def project(t, carry):
        projected[t] = jnp.dot(
            attended, weights(0, last, tile_at(t)), preferred_element_type=jnp.float32
        )
        return carry

    lax.fori_loop(0, tiles, project, 0)
    pass_att(last)
    pair_wait(last)
    attended_last = gathered(last, heads)

    def project_last(t, carry):
        whole = projected[t] + jnp.dot(
            attended_last, weights(last, heads, tile_at(t)), preferred_element_type=jnp.float32
        )
        here = out_cols(s, t)
        gate_row = jnp.zeros((1, tile), jnp.float32)
        for i in range(gate_ref.shape[0]):
            gate_row = jnp.where(step == i, gate_ref[i : i + 1, here], gate_row)
        gated = (gate_row * whole).astype(jnp.bfloat16)
        out_half[t] = gated[:tok]
        out_piece(s, t).start()
        out_ref[:, here] = gated[tok:]
        return carry

    lax.fori_loop(0, tiles, project_last, 0)

    def out_wait(t, carry):
        out_piece(sib, t).wait_recv()
        out_piece(s, t).wait_send()
        return carry

    lax.fori_loop(0, tiles, out_wait, 0)

    def sent(h):
        sib_k(h, tok_half).wait_send()
        sib_v(h, tok_half).wait_send()
        att_pair(x, h, tok_half).wait_send()
        for other in others:
            att_piece(other, h).wait_send()
            for dy in range(1, n_str):
                y_piece(other, dy, h).wait_send()
            att_pair(other, h, tok_half).wait_send()

            x_piece(other, h).wait_send()

            @pl.when(block_core(other) == s)
            def _(other=other):
                relay(other, h).wait_send()

        @pl.when(block_core(x) == s)
        def _():
            own_share(h).wait_send()

        @pl.when(z == 0)
        def _():
            zero_k(h).wait_send()
            zero_v(h).wait_send()

        @pl.when(z == 1)
        def _():
            fwd_k(h, tok_half).wait_send()
            fwd_v(h, tok_half).wait_send()

        @pl.when(z >= 2)
        def _():
            down(lambda c: pass_q(c, h).wait_send(), z)

        @pl.when(z >= 1)
        def _():
            down(lambda c: (pass_acc(c, h).wait_send(), pass_stat(c, h).wait_send()), z + 1)

    each_head(sent)


def solution(mesh):
    n_str, n_span = mesh.shape["streams"], mesh.shape["span"]
    n_head, n_seq = mesh.shape["head"], mesh.shape["seq"]
    sizes = (n_str, n_span, n_head, n_seq)

    def on_device(query_rows, key_rows, value_rows, out_weight, gate_table, step_index, block_mask):
        tok = query_rows.shape[0]
        heads = query_rows.shape[1] // HD
        cols = gate_table.shape[1]
        half = cols // n_seq
        tile = 256 if half % 256 == 0 else 128
        tiles = half // tile
        piece = out_weight.shape[0] // n_str // heads
        vmem, any_space = pltpu.VMEM, pl.ANY
        dma = pltpu.SemaphoreType.DMA
        low, wide = jnp.bfloat16, jnp.float32
        flops = 4 * heads * tok * tok * n_seq * n_span * HD + 2 * tok * n_head * heads * HD * cols
        return pl.pallas_call(
            functools.partial(kernel, sizes),
            out_shape=jax.ShapeDtypeStruct((tok, cols), low),
            in_specs=[
                pl.BlockSpec(memory_space=pltpu.SMEM),
                pl.BlockSpec(memory_space=pltpu.SMEM),
                pl.BlockSpec(memory_space=any_space),
                pl.BlockSpec(memory_space=any_space),
                pl.BlockSpec(memory_space=any_space),
                pl.BlockSpec(memory_space=any_space),
                pl.BlockSpec(memory_space=vmem),
            ],
            out_specs=pl.BlockSpec(memory_space=vmem),
            scratch_shapes=[
                vmem((n_span, heads, tok, HD), low),
                vmem((heads, n_seq * tok, HD), low),
                vmem((heads, n_seq * tok, HD), low),
                vmem((heads, n_seq * tok, HD), low),
                vmem((heads, n_seq * tok, HD), low),
                vmem((n_span, heads, HD, tok), wide),
                vmem((n_span, heads, 8, tok), wide),
                vmem((n_span, heads, HD, tok), low),
                vmem((n_span, heads, 8, tok), wide),
                vmem((n_span, heads, HD, tok), low),
                vmem((n_span, heads, 8, tok), wide),
                vmem((n_head * heads, n_seq * tok, HD), low),
                vmem((n_head * heads * HD, half), low),
                vmem((tiles, tok, tile), low),
                vmem((n_head, heads, piece, half), low),
                vmem((heads, HD, 2 * n_seq * tok), low),
                vmem((tiles, n_seq * tok, tile), wide),
                dma((n_head, heads)),
                dma((n_head, heads)),
                dma((3, heads)),
                dma((2, heads)),
                dma((2, heads)),
                dma((2, heads)),
                dma((2, heads)),
                dma((2, heads)),
                dma((2, heads)),
                dma((n_span, heads)),
                dma((n_span, heads)),
                dma((n_span, heads)),
                dma((n_span, heads)),
                dma((n_span, heads)),
                dma((n_span, heads)),
                dma((n_head, heads)),
                dma((n_head, heads)),
                dma((n_head, n_str, heads)),
                dma((n_head, n_str, heads)),
                dma((heads,)),
                dma((heads,)),
                dma((heads,)),
                dma((n_head, heads)),
                dma((n_head, heads)),
                dma((n_head, heads)),
                dma((n_head, heads)),
                dma((tiles,)),
                dma((tiles,)),
            ],
            compiler_params=pltpu.CompilerParams(
                collective_id=0, has_side_effects=True, vmem_limit_bytes=56 * 1024 * 1024
            ),
            cost_estimate=pl.CostEstimate(
                flops=flops, bytes_accessed=6 * out_weight.size, transcendentals=0
            ),
        )(step_index, block_mask, query_rows, key_rows, value_rows, out_weight, gate_table)

    in_specs = (
        P(("streams", "span", "seq"), "head"),
        P(("streams", "span", "seq"), "head"),
        P(("streams", "span", "seq"), "head"),
        P("head", "seq"),
        P(None, "head"),
        P("streams"),
        P("streams", None),
    )
    out_specs = P(("streams", "span", "seq"), "head")
    return jax.shard_map(
        on_device, mesh=mesh, in_specs=in_specs, out_specs=out_specs, check_vma=False
    )
```

```python
import functools
import math

import jax
import jax.numpy as jnp
from jax import lax
from jax.experimental import pallas as pl
from jax.experimental.pallas import tpu as pltpu
from jax.sharding import PartitionSpec as P

HD = 128
NEG_FLOOR = -1e30
COPIES = 8
MESH = pl.DeviceIdType.MESH
SCORE_SCALE = math.log2(math.e) / math.sqrt(HD)


def kernel(
    sizes,
    step_ref,
    mask_ref,
    q_ref,
    k_ref,
    v_ref,
    w_ref,
    gate_ref,
    out_ref,
    q_all,
    k_own,
    v_own,
    k_zero,
    v_zero,
    part_acc,
    part_stat,
    acc_out,
    stat_out,
    acc_in,
    stat_in,
    att,
    w_full,
    out_half,
    out_own,
    out_store,
    w_relay,
    v_turned,
    projected,
    relay_send,
    relay_recv,
    load_sem,
    sib_send,
    sib_recv,
    zero_send,
    zero_recv,
    fwd_send,
    fwd_recv,
    q_send,
    q_recv,
    acc_send,
    acc_recv,
    stat_send,
    stat_recv,
    x_send,
    x_recv,
    y_send,
    y_recv,
    own_load,
    own_send,
    own_recv,
    att_send,
    att_recv,
    pair_send,
    pair_recv,
    out_send,
    out_recv,
):
    n_str, n_span, n_head, n_seq = sizes
    y = lax.axis_index("streams")
    z = lax.axis_index("span")
    x = lax.axis_index("head")
    s = lax.axis_index("seq")
    sib = 1 - s
    tok = q_ref.shape[0]
    heads = q_ref.shape[1] // HD
    w_rows = w_ref.shape[0]
    cols = out_ref.shape[1]
    half = cols // n_seq
    tile = 256 if half % 256 == 0 else 128
    tiles = half // tile
    y_rows = w_rows // n_str
    pieces = 2 * heads
    piece = y_rows // pieces
    own_piece = w_rows // heads

    def remote(src, dst, ss, rs, **where):
        return pltpu.make_async_remote_copy(
            src_ref=src, dst_ref=dst, send_sem=ss, recv_sem=rs, device_id=where, device_id_type=MESH
        )

    def head_cols(h):
        return pl.ds(pl.multiple_of(h * HD, HD), HD)

    def each_head(body):
        lax.fori_loop(0, heads, lambda h, c: (body(h), c)[1], 0)

    def each_piece(body):
        lax.fori_loop(0, pieces, lambda i, c: (body(i), c)[1], 0)

    def down(body, low):
        lax.fori_loop(0, n_span - low, lambda i, c: (body(n_span - 1 - i), c)[1], 0)

    tok_half = pl.ds(pl.multiple_of(s * tok, tok), tok)
    sib_half = pl.ds(pl.multiple_of(sib * tok, tok), tok)

    def load_q(h):
        return pltpu.make_async_copy(q_ref.at[:, head_cols(h)], q_all.at[z, h], load_sem.at[0, h])

    def load_k(h):
        return pltpu.make_async_copy(
            k_ref.at[:, head_cols(h)], k_own.at[h, tok_half], load_sem.at[1, h]
        )

    def load_v(h):
        return pltpu.make_async_copy(
            v_ref.at[:, head_cols(h)], v_own.at[h, tok_half], load_sem.at[2, h]
        )

    def sib_k(h, half):
        return remote(
            k_own.at[h, half], k_own.at[h, half], sib_send.at[0, h], sib_recv.at[0, h], seq=sib
        )

    def sib_v(h, half):
        return remote(
            v_own.at[h, half], v_own.at[h, half], sib_send.at[1, h], sib_recv.at[1, h], seq=sib
        )

    def zero_k(h):
        return remote(
            k_own.at[h, tok_half], k_zero.at[h, tok_half], zero_send.at[0, h], zero_recv.at[0, h], span=1
        )

    def zero_v(h):
        return remote(
            v_own.at[h, tok_half], v_zero.at[h, tok_half], zero_send.at[1, h], zero_recv.at[1, h], span=1
        )

    def fwd_k(h, half):
        return remote(
            k_zero.at[h, half], k_zero.at[h, half], fwd_send.at[0, h], fwd_recv.at[0, h], seq=sib
        )

    def fwd_v(h, half):
        return remote(
            v_zero.at[h, half], v_zero.at[h, half], fwd_send.at[1, h], fwd_recv.at[1, h], seq=sib
        )

    def pass_q(c, h):
        return remote(q_all.at[c, h], q_all.at[c, h], q_send.at[c, h], q_recv.at[c, h], span=z - 1)

    def pass_acc(c, h):
        return remote(
            acc_out.at[c, h], acc_in.at[c, h], acc_send.at[c, h], acc_recv.at[c, h], span=z + 1
        )

    def pass_stat(c, h):
        return remote(
            stat_out.at[c, h], stat_in.at[c, h], stat_send.at[c, h], stat_recv.at[c, h], span=z + 1
        )

    def w_at(src_x, part, i):
        first = src_x * w_rows + part * y_rows + i * piece
        return w_full.at[pl.ds(pl.multiple_of(first, piece), piece)]

    def block_core(dst_x):
        return (dst_x * n_seq) // n_head

    def block_cols(dst_x, core):
        first = lax.rem(dst_x, n_head // n_seq) * cols + core * half
        return pl.ds(pl.multiple_of(first, HD), half)

    def x_piece(dst_x, i):
        first = y * y_rows + i * piece
        return remote(
            w_ref.at[pl.ds(pl.multiple_of(first, piece), piece), block_cols(dst_x, s)],
            w_at(x, y, i),
            x_send.at[dst_x, i],
            x_recv.at[x, i],
            head=dst_x,
        )

    def relay(dst_x, i):
        first = y * y_rows + i * piece
        return remote(
            w_ref.at[pl.ds(pl.multiple_of(first, piece), piece), block_cols(dst_x, sib)],
            w_relay.at[dst_x, i],
            relay_send.at[dst_x, i],
            relay_recv.at[dst_x, i],
            seq=sib,
        )

    def x_relayed(dst_x, i):
        return remote(
            w_relay.at[dst_x, i],
            w_at(x, y, i),
            x_send.at[dst_x, i],
            x_recv.at[x, i],
            head=dst_x,
        )

    def x_wait(src_x, i):
        ref = w_at(src_x, y, i)
        remote(ref, ref, x_send.at[src_x, i], x_recv.at[src_x, i], head=src_x).wait_recv()

    def y_piece(src_x, dy, i):
        ref = w_at(src_x, y, i)
        return remote(
            ref, ref, y_send.at[src_x, dy, i], y_recv.at[src_x, dy, i], streams=lax.rem(y + dy, n_str)
        )

    def y_wait(src_x, dy, i):
        from_y = lax.rem(y - dy + n_str, n_str)
        ref = w_at(src_x, from_y, i)
        remote(
            ref, ref, y_send.at[src_x, dy, i], y_recv.at[src_x, dy, i], streams=from_y
        ).wait_recv()

    def own_rows(i):
        return pl.ds(pl.multiple_of(i * own_piece, own_piece), own_piece)

    def own_at(i):
        first = x * w_rows + i * own_piece
        return w_full.at[pl.ds(pl.multiple_of(first, own_piece), own_piece)]

    def own_copy(i):
        return pltpu.make_async_copy(
            w_ref.at[own_rows(i), block_cols(x, s)], own_at(i), own_load.at[i]
        )

    def own_share(i):
        return remote(
            w_ref.at[own_rows(i), block_cols(x, sib)], own_at(i), own_send.at[i], own_recv.at[i], seq=sib
        )

    def att_piece(dst_x, h):
        ref = att.at[x * heads + h, tok_half]
        return remote(ref, ref, att_send.at[dst_x, h], att_recv.at[x, h], head=dst_x)

    def att_wait(src_x, h):
        ref = att.at[src_x * heads + h, tok_half]
        remote(ref, ref, att_send.at[src_x, h], att_recv.at[src_x, h], head=src_x).wait_recv()

    def att_pair(src_x, h, rows):
        ref = att.at[src_x * heads + h, rows]
        return remote(ref, ref, pair_send.at[src_x, h], pair_recv.at[src_x, h], seq=sib)

    def out_cols(core, t):
        return pl.ds(pl.multiple_of(core * half + t * tile, tile), tile)

    def out_piece(core, t):
        return remote(
            out_half.at[t], out_ref.at[:, out_cols(core, t)], out_send.at[t], out_recv.at[t], seq=sib
        )

    def out_copy(t):
        return pltpu.make_async_copy(out_own.at[t], out_ref.at[:, out_cols(s, t)], out_store.at[t])

    others = [lax.rem(x + dx, n_head) for dx in range(1, n_head)]

    barrier = pltpu.get_barrier_semaphore()

    def greet(**where):
        pl.semaphore_signal(barrier, inc=1, device_id=where, device_id_type=MESH)

    greet(seq=sib)
    for other in others:
        for core in range(n_seq):
            greet(head=other, seq=core)
    for dy in range(1, n_str):
        greet(streams=lax.rem(y + dy, n_str))

    @pl.when(z > 0)
    def _():
        greet(span=z - 1)

    @pl.when(z < n_span - 1)
    def _():
        greet(span=z + 1)

    each_head(lambda h: (load_q(h).start(), load_k(h).start(), load_v(h).start()))
    beside = jnp.where(z > 0, 1, 0) + jnp.where(z < n_span - 1, 1, 0)
    pl.semaphore_wait(barrier, 1 + n_seq * (n_head - 1) + (n_str - 1) + beside)

    each_head(lambda h: (load_q(h).wait(), load_k(h).wait(), load_v(h).wait()))

    @pl.when(z >= 2)
    def _():
        pass_q(z, 0).start()

    @pl.when(z == 0)
    def _():
        each_head(lambda h: (zero_k(h).start(), zero_v(h).start()))

    each_head(lambda h: (sib_k(h, tok_half).start(), sib_v(h, tok_half).start()))
    for other in others:

        @pl.when(block_core(other) == s)
        def _(other=other):
            each_piece(lambda i: (relay(other, i).start(), x_piece(other, i).start()))

    def block(q, keys, v_t, flags):
        scores = [
            lax.dot_general(k, q, (((1,), (1,)), ((), ())), preferred_element_type=jnp.float32)
            * SCORE_SCALE
            for k in keys
        ]
        tops = [
            jnp.where(flag == 1, jnp.max(each, axis=0, keepdims=True), NEG_FLOOR)
            for each, flag in zip(scores, flags)
        ]
        top = functools.reduce(jnp.maximum, tops)
        probs = [
            jnp.exp2(each - jnp.where(flag == 1, top, -NEG_FLOOR))
            for each, flag in zip(scores, flags)
        ]
        total = sum(jnp.sum(each, axis=0, keepdims=True) for each in probs)
        low = jnp.concatenate([each.astype(jnp.bfloat16) for each in probs], axis=0)
        return top, total, jnp.dot(v_t, low, preferred_element_type=jnp.float32)

    def merge(a, b):
        top = jnp.maximum(a[0], b[0])
        wa, wb = jnp.exp2(a[0] - top), jnp.exp2(b[0] - top)
        return top, wa * a[1] + wb * b[1], wa * a[2] + wb * b[2]

    def get_part(c, h):
        return part_stat[c, h, 0:1], part_stat[c, h, 1:2], part_acc[c, h]

    def put_part(c, h, part):
        part_stat[c, h, 0:1] = part[0]
        part_stat[c, h, 1:2] = part[1]
        part_acc[c, h] = part[2]

    def emit(c, h, part):
        @pl.when(c > z)
        def _():
            stat_out[c, h, 0:1] = part[0]
            stat_out[c, h, 1:2] = part[1]
            acc_out[c, h] = part[2].astype(jnp.bfloat16)
            pass_acc(c, h).start()
            pass_stat(c, h).start()

        @pl.when(c == z)
        def _():
            att[x * heads + h, tok_half] = (part[2] / part[1]).T.astype(jnp.bfloat16)
            for other in others:
                att_piece(other, h).start()
            att_pair(x, h, tok_half).start()

    def pass_att(h):
        for other in others:
            att_wait(other, h)
            att_pair(other, h, tok_half).start()

    def pass_on(h):
        def one(c):
            pass_q(c, h).wait_recv()

            @pl.when(z >= 2)
            def _():
                pass_q(c, h).start()

        down(one, z + 1)

        @pl.when((z >= 2) & (h + 1 < heads))
        def _():
            pass_q(z, h + 1).start()

    @pl.when(z >= 2)
    def _():
        pass_on(0)

    def pass_w(h):
        for i in (2 * h, 2 * h + 1):
            for other in others:
                x_wait(other, i)
                for dy in range(1, n_str):
                    y_piece(other, dy, i).start()

    for other in others:

        @pl.when(block_core(other) != s)
        def _(other=other):
            each_piece(lambda i: (relay(other, i).wait_recv(), x_relayed(other, i).start()))

    def share_zero(h):
        zero_k(h).wait_recv()
        fwd_k(h, tok_half).start()
        zero_v(h).wait_recv()
        fwd_v(h, tok_half).start()

    @pl.when(z == 1)
    def _():
        share_zero(0)

    def zero_block(c, h, v_t):
        return block(q_all[c, h], [k_own[h], k_zero[h]], v_t, [mask_ref[c, 1], mask_ref[c, 0]])

    def head_step(h):
        @pl.when((z >= 2) & (h + 1 < heads))
        def _():
            pass_on(h + 1)

        @pl.when(z == 1)
        def _():
            pass_on(h)

        @pl.when(block_core(x) == s)
        def _():
            own_copy(h).start()
            own_share(h).start()

        sib_k(h, sib_half).wait_recv()
        sib_v(h, sib_half).wait_recv()

        k_here = k_own[h]
        v_here = v_own[h].T

        @pl.when(z != 1)
        def _():
            def own_block(c):
                put_part(c, h, block(q_all[c, h], [k_here], v_here, [mask_ref[c, z]]))

            down(own_block, z)

        @pl.when(z == 1)
        def _():
            fwd_k(h, sib_half).wait_recv()
            fwd_v(h, sib_half).wait_recv()
            both = jnp.concatenate([v_here, v_zero[h].T], axis=1)
            v_turned[h] = both

            def later(c):
                emit(c, h, zero_block(c, h, both))

                @pl.when((c == n_span - 1) & (h + 1 < heads))
                def _():
                    share_zero(h + 1)

            down(later, 2)

        @pl.when(z == 0)
        def _():
            emit(z, h, get_part(z, h))

        @pl.when(z < 2)
        def _():
            pass_w(h)

        @pl.when((z >= 2) & ((h == 2) | (h == 4)))
        def _():
            pass_w(h // 2 - 1)

    each_head(head_step)

    @pl.when(z == 1)
    def _():
        def own_step(h):
            emit(1, h, zero_block(1, h, v_turned[h]))

        each_head(own_step)

    @pl.when(z >= 2)
    def _():
        def merge_step(h):
            def one(c):
                pass_acc(c, h).wait_recv()
                pass_stat(c, h).wait_recv()
                before = (
                    stat_in[c, h, 0:1],
                    stat_in[c, h, 1:2],
                    acc_in[c, h].astype(jnp.float32),
                )
                emit(c, h, merge(get_part(c, h), before))

            down(one, z)

            @pl.when(h + 2 < heads)
            def _():
                pass_w(h + 2)

            @pl.when(h > 0)
            def _():
                pass_att(h - 1)

        each_head(merge_step)

    @pl.when(block_core(x) == s)
    def _():
        each_head(lambda i: own_copy(i).wait())

    @pl.when(block_core(x) != s)
    def _():
        each_head(lambda i: own_share(i).wait_recv())

    each_head(lambda h: att_pair(x, h, sib_half).wait_recv())
    step = step_ref[z]

    def gathered(src):
        return jnp.concatenate(
            [
                jnp.concatenate([att[src * heads + h, rows] for h in range(heads)], axis=1)
                for rows in (sib_half, tok_half)
            ],
            axis=0,
        )

    def product(attended, src, t):
        rows = pl.ds(pl.multiple_of(src * w_rows, w_rows), w_rows)
        at = pl.ds(pl.multiple_of(t * tile, tile), tile)
        return jnp.dot(attended, w_full[rows, at], preferred_element_type=jnp.float32)

    attended_own = gathered(x)

    def project(t, carry):
        projected[t] = product(attended_own, x, t)
        return carry

    lax.fori_loop(0, tiles, project, 0)

    @pl.when(z < 2)
    def _():
        lax.fori_loop(0, heads - 1, lambda h, c: (pass_att(h), c)[1], 0)

    pass_att(heads - 1)

    def other_waits(h):
        for other in others:
            for half_piece in range(2):
                for dy in range(1, n_str):
                    y_wait(other, dy, 2 * h + half_piece)
            att_pair(other, h, sib_half).wait_recv()

    each_head(other_waits)
    attended_others = [gathered(other) for other in others]

    def project_last(t, carry):
        whole = projected[t]
        for other, attended in zip(others, attended_others):
            whole = whole + product(attended, other, t)
        here = out_cols(s, t)
        gate_row = jnp.zeros((1, tile), jnp.float32)
        for i in range(gate_ref.shape[0]):
            gate_row = jnp.where(step == i, gate_ref[i : i + 1, here], gate_row)
        gated = (gate_row * whole).astype(jnp.bfloat16)
        out_half[t] = gated[:tok]
        out_piece(s, t).start()
        out_own[t] = gated[tok:]
        out_copy(t).start()
        return carry

    lax.fori_loop(0, tiles, project_last, 0)

    def out_wait(t, carry):
        out_piece(sib, t).wait_recv()
        out_piece(s, t).wait_send()
        out_copy(t).wait()
        return carry

    lax.fori_loop(0, tiles, out_wait, 0)

    def sent(h):
        sib_k(h, tok_half).wait_send()
        sib_v(h, tok_half).wait_send()
        att_pair(x, h, tok_half).wait_send()
        for other in others:
            att_piece(other, h).wait_send()
            att_pair(other, h, tok_half).wait_send()

        @pl.when(block_core(x) == s)
        def _():
            own_share(h).wait_send()

        @pl.when(z == 0)
        def _():
            zero_k(h).wait_send()
            zero_v(h).wait_send()

        @pl.when(z == 1)
        def _():
            fwd_k(h, tok_half).wait_send()
            fwd_v(h, tok_half).wait_send()

        @pl.when(z >= 2)
        def _():
            down(lambda c: pass_q(c, h).wait_send(), z)

        @pl.when(z >= 1)
        def _():
            down(lambda c: (pass_acc(c, h).wait_send(), pass_stat(c, h).wait_send()), z + 1)

    def sent_weights(i):
        for other in others:
            for dy in range(1, n_str):
                y_piece(other, dy, i).wait_send()
            x_piece(other, i).wait_send()

            @pl.when(block_core(other) == s)
            def _(other=other):
                relay(other, i).wait_send()

    each_head(sent)
    each_piece(sent_weights)


def hand_over(from_ref, to_ref, sems):
    rows = from_ref.shape[0] // COPIES
    copies = [
        pltpu.make_async_copy(
            from_ref.at[i * rows : (i + 1) * rows], to_ref.at[i * rows : (i + 1) * rows], sems.at[i]
        )
        for i in range(COPIES)
    ]
    for copy in copies:
        copy.start()
    for copy in copies:
        copy.wait()


def solution(mesh):
    n_str, n_span = mesh.shape["streams"], mesh.shape["span"]
    n_head, n_seq = mesh.shape["head"], mesh.shape["seq"]
    sizes = (n_str, n_span, n_head, n_seq)

    def on_device(query_rows, key_rows, value_rows, out_weight, gate_table, step_index, block_mask):
        tok = query_rows.shape[0]
        heads = query_rows.shape[1] // HD
        cols = gate_table.shape[1]
        half = cols // n_seq
        tile = 256 if half % 256 == 0 else 128
        tiles = half // tile
        pieces = 2 * heads
        piece = out_weight.shape[0] // n_str // pieces
        vmem, any_space = pltpu.VMEM, pl.ANY
        dma = pltpu.SemaphoreType.DMA
        low, wide = jnp.bfloat16, jnp.float32
        flops = 4 * heads * tok * tok * n_seq * n_span * HD + 2 * tok * n_head * heads * HD * cols
        result = pl.pallas_call(
            functools.partial(kernel, sizes),
            out_shape=jax.ShapeDtypeStruct((tok, cols), low),
            in_specs=[
                pl.BlockSpec(memory_space=pltpu.SMEM),
                pl.BlockSpec(memory_space=pltpu.SMEM),
                pl.BlockSpec(memory_space=any_space),
                pl.BlockSpec(memory_space=any_space),
                pl.BlockSpec(memory_space=any_space),
                pl.BlockSpec(memory_space=any_space),
                pl.BlockSpec(memory_space=vmem),
            ],
            out_specs=pl.BlockSpec(memory_space=any_space),
            scratch_shapes=[
                vmem((n_span, heads, tok, HD), low),
                vmem((heads, n_seq * tok, HD), low),
                vmem((heads, n_seq * tok, HD), low),
                vmem((heads, n_seq * tok, HD), low),
                vmem((heads, n_seq * tok, HD), low),
                vmem((n_span, heads, HD, tok), wide),
                vmem((n_span, heads, 8, tok), wide),
                vmem((n_span, heads, HD, tok), low),
                vmem((n_span, heads, 8, tok), wide),
                vmem((n_span, heads, HD, tok), low),
                vmem((n_span, heads, 8, tok), wide),
                vmem((n_head * heads, n_seq * tok, HD), low),
                vmem((n_head * heads * HD, half), low),
                vmem((tiles, tok, tile), low),
                vmem((tiles, tok, tile), low),
                dma((tiles,)),
                vmem((n_head, pieces, piece, half), low),
                vmem((heads, HD, 2 * n_seq * tok), low),
                vmem((tiles, n_seq * tok, tile), wide),
                dma((n_head, pieces)),
                dma((n_head, pieces)),
                dma((3, heads)),
                dma((2, heads)),
                dma((2, heads)),
                dma((2, heads)),
                dma((2, heads)),
                dma((2, heads)),
                dma((2, heads)),
                dma((n_span, heads)),
                dma((n_span, heads)),
                dma((n_span, heads)),
                dma((n_span, heads)),
                dma((n_span, heads)),
                dma((n_span, heads)),
                dma((n_head, pieces)),
                dma((n_head, pieces)),
                dma((n_head, n_str, pieces)),
                dma((n_head, n_str, pieces)),
                dma((heads,)),
                dma((heads,)),
                dma((heads,)),
                dma((n_head, heads)),
                dma((n_head, heads)),
                dma((n_head, heads)),
                dma((n_head, heads)),
                dma((tiles,)),
                dma((tiles,)),
            ],
            compiler_params=pltpu.CompilerParams(
                collective_id=0, has_side_effects=True, vmem_limit_bytes=56 * 1024 * 1024
            ),
            cost_estimate=pl.CostEstimate(
                flops=flops, bytes_accessed=6 * out_weight.size, transcendentals=0
            ),
        )(step_index, block_mask, query_rows, key_rows, value_rows, out_weight, gate_table)
        return pl.pallas_call(
            hand_over,
            out_shape=jax.ShapeDtypeStruct((tok, cols), low),
            in_specs=[pl.BlockSpec(memory_space=any_space)],
            out_specs=pl.BlockSpec(memory_space=any_space),
            scratch_shapes=[dma((COPIES,))],
        )(result)

    in_specs = (
        P(("streams", "span", "seq"), "head"),
        P(("streams", "span", "seq"), "head"),
        P(("streams", "span", "seq"), "head"),
        P("head", "seq"),
        P(None, "head"),
        P("streams"),
        P("streams", None),
    )
    out_specs = P(("streams", "span", "seq"), "head")
    return jax.shard_map(
        on_device, mesh=mesh, in_specs=in_specs, out_specs=out_specs, check_vma=False
    )
```

```python
import functools
import math

import jax
import jax.numpy as jnp
from jax import lax
from jax.experimental import pallas as pl
from jax.experimental.pallas import tpu as pltpu
from jax.sharding import PartitionSpec as P

HD = 128
NEG_FLOOR = -1e30
COPIES = 4
MESH = pl.DeviceIdType.MESH
SCORE_SCALE = math.log2(math.e) / math.sqrt(HD)


def kernel(
    sizes,
    step_ref,
    mask_ref,
    q_ref,
    k_ref,
    v_ref,
    w_ref,
    gate_ref,
    out_ref,
    q_all,
    k_own,
    v_own,
    k_zero,
    v_zero,
    part_acc,
    part_stat,
    acc_out,
    stat_out,
    acc_in,
    stat_in,
    att,
    w_full,
    out_half,
    out_own,
    out_store,
    w_relay,
    w_stage,
    own_stage,
    stage_sem,
    share_sem,
    v_turned,
    projected,
    relay_send,
    relay_recv,
    load_sem,
    sib_send,
    sib_recv,
    zero_send,
    zero_recv,
    fwd_send,
    fwd_recv,
    q_send,
    q_recv,
    acc_send,
    acc_recv,
    stat_send,
    stat_recv,
    x_send,
    x_recv,
    y_send,
    y_recv,
    own_load,
    own_send,
    own_recv,
    att_send,
    att_recv,
    pair_send,
    pair_recv,
    out_send,
    out_recv,
):
    n_str, n_span, n_head, n_seq = sizes
    y = lax.axis_index("streams")
    z = lax.axis_index("span")
    x = lax.axis_index("head")
    s = lax.axis_index("seq")
    sib = 1 - s
    tok = q_ref.shape[0]
    heads = q_ref.shape[1] // HD
    w_rows = w_ref.shape[0]
    cols = out_ref.shape[1]
    half = cols // n_seq
    tile = 256 if half % 256 == 0 else 128
    tiles = half // tile
    y_rows = w_rows // n_str
    pieces = 2 * heads
    piece = y_rows // pieces
    own_piece = w_rows // heads

    def remote(src, dst, ss, rs, **where):
        return pltpu.make_async_remote_copy(
            src_ref=src, dst_ref=dst, send_sem=ss, recv_sem=rs, device_id=where, device_id_type=MESH
        )

    def head_cols(h):
        return pl.ds(pl.multiple_of(h * HD, HD), HD)

    def each_head(body):
        lax.fori_loop(0, heads, lambda h, c: (body(h), c)[1], 0)

    def each_piece(body):
        lax.fori_loop(0, pieces, lambda i, c: (body(i), c)[1], 0)

    def down(body, low):
        lax.fori_loop(0, n_span - low, lambda i, c: (body(n_span - 1 - i), c)[1], 0)

    tok_half = pl.ds(pl.multiple_of(s * tok, tok), tok)
    sib_half = pl.ds(pl.multiple_of(sib * tok, tok), tok)

    def load_q(h):
        return pltpu.make_async_copy(q_ref.at[:, head_cols(h)], q_all.at[z, h], load_sem.at[0, h])

    def load_k(h):
        return pltpu.make_async_copy(
            k_ref.at[:, head_cols(h)], k_own.at[h, tok_half], load_sem.at[1, h]
        )

    def load_v(h):
        return pltpu.make_async_copy(
            v_ref.at[:, head_cols(h)], v_own.at[h, tok_half], load_sem.at[2, h]
        )

    def sib_k(h, half):
        return remote(
            k_own.at[h, half], k_own.at[h, half], sib_send.at[0, h], sib_recv.at[0, h], seq=sib
        )

    def sib_v(h, half):
        return remote(
            v_own.at[h, half], v_own.at[h, half], sib_send.at[1, h], sib_recv.at[1, h], seq=sib
        )

    def zero_k(h):
        return remote(
            k_own.at[h, tok_half], k_zero.at[h, tok_half], zero_send.at[0, h], zero_recv.at[0, h], span=1
        )

    def zero_v(h):
        return remote(
            v_own.at[h, tok_half], v_zero.at[h, tok_half], zero_send.at[1, h], zero_recv.at[1, h], span=1
        )

    def fwd_k(h, half):
        return remote(
            k_zero.at[h, half], k_zero.at[h, half], fwd_send.at[0, h], fwd_recv.at[0, h], seq=sib
        )

    def fwd_v(h, half):
        return remote(
            v_zero.at[h, half], v_zero.at[h, half], fwd_send.at[1, h], fwd_recv.at[1, h], seq=sib
        )

    def pass_q(c, h):
        return remote(q_all.at[c, h], q_all.at[c, h], q_send.at[c, h], q_recv.at[c, h], span=z - 1)

    def pass_acc(c, h):
        return remote(
            acc_out.at[c, h], acc_in.at[c, h], acc_send.at[c, h], acc_recv.at[c, h], span=z + 1
        )

    def pass_stat(c, h):
        return remote(
            stat_out.at[c, h], stat_in.at[c, h], stat_send.at[c, h], stat_recv.at[c, h], span=z + 1
        )

    def w_at(src_x, part, i):
        first = src_x * w_rows + part * y_rows + i * piece
        return w_full.at[pl.ds(pl.multiple_of(first, piece), piece)]

    def block_core(dst_x):
        return (dst_x * n_seq) // n_head

    def block_cols(dst_x, core):
        first = lax.rem(dst_x, n_head // n_seq) * cols + core * half
        return pl.ds(pl.multiple_of(first, HD), half)

    def piece_rows(i):
        return pl.ds(pl.multiple_of(i * piece, piece), piece)

    def load_w(dst_x, core):
        return pltpu.make_async_copy(
            w_ref.at[pl.ds(pl.multiple_of(y * y_rows, y_rows), y_rows), block_cols(dst_x, core)],
            w_stage.at[dst_x, core],
            stage_sem.at[dst_x, core],
        )

    def load_share():
        return pltpu.make_async_copy(w_ref.at[:, block_cols(x, sib)], own_stage, share_sem.at[0])

    def x_piece(dst_x, i):
        return remote(
            w_stage.at[dst_x, s, piece_rows(i)],
            w_at(x, y, i),
            x_send.at[dst_x, i],
            x_recv.at[x, i],
            head=dst_x,
        )

    def relay(dst_x, i):
        return remote(
            w_stage.at[dst_x, sib, piece_rows(i)],
            w_relay.at[dst_x, i],
            relay_send.at[dst_x, i],
            relay_recv.at[dst_x, i],
            seq=sib,
        )

    def x_relayed(dst_x, i):
        return remote(
            w_relay.at[dst_x, i],
            w_at(x, y, i),
            x_send.at[dst_x, i],
            x_recv.at[x, i],
            head=dst_x,
        )

    def x_wait(src_x, i):
        ref = w_at(src_x, y, i)
        remote(ref, ref, x_send.at[src_x, i], x_recv.at[src_x, i], head=src_x).wait_recv()

    def y_piece(src_x, dy, i):
        ref = w_at(src_x, y, i)
        return remote(
            ref, ref, y_send.at[src_x, dy, i], y_recv.at[src_x, dy, i], streams=lax.rem(y + dy, n_str)
        )

    def y_wait(src_x, dy, i):
        from_y = lax.rem(y - dy + n_str, n_str)
        ref = w_at(src_x, from_y, i)
        remote(
            ref, ref, y_send.at[src_x, dy, i], y_recv.at[src_x, dy, i], streams=from_y
        ).wait_recv()

    def own_rows(i):
        return pl.ds(pl.multiple_of(i * own_piece, own_piece), own_piece)

    def own_at(i):
        first = x * w_rows + i * own_piece
        return w_full.at[pl.ds(pl.multiple_of(first, own_piece), own_piece)]

    def own_copy(i):
        return pltpu.make_async_copy(
            w_ref.at[own_rows(i), block_cols(x, s)], own_at(i), own_load.at[i]
        )

    def own_share(i):
        return remote(
            own_stage.at[own_rows(i)], own_at(i), own_send.at[i], own_recv.at[i], seq=sib
        )

    def att_piece(dst_x, h):
        ref = att.at[x * heads + h, tok_half]
        return remote(ref, ref, att_send.at[dst_x, h], att_recv.at[x, h], head=dst_x)

    def att_wait(src_x, h):
        ref = att.at[src_x * heads + h, tok_half]
        remote(ref, ref, att_send.at[src_x, h], att_recv.at[src_x, h], head=src_x).wait_recv()

    def att_pair(src_x, h, rows):
        ref = att.at[src_x * heads + h, rows]
        return remote(ref, ref, pair_send.at[src_x, h], pair_recv.at[src_x, h], seq=sib)

    def out_cols(core, t):
        return pl.ds(pl.multiple_of(core * half + t * tile, tile), tile)

    def out_piece(core, t):
        return remote(
            out_half.at[t], out_ref.at[:, out_cols(core, t)], out_send.at[t], out_recv.at[t], seq=sib
        )

    def out_copy(t):
        return pltpu.make_async_copy(out_own.at[t], out_ref.at[:, out_cols(s, t)], out_store.at[t])

    others = [lax.rem(x + dx, n_head) for dx in range(1, n_head)]

    barrier = pltpu.get_barrier_semaphore()

    def greet(**where):
        pl.semaphore_signal(barrier, inc=1, device_id=where, device_id_type=MESH)

    greet(seq=sib)
    for other in others:
        for core in range(n_seq):
            greet(head=other, seq=core)
    for dy in range(1, n_str):
        greet(streams=lax.rem(y + dy, n_str))

    @pl.when(z > 0)
    def _():
        greet(span=z - 1)

    @pl.when(z < n_span - 1)
    def _():
        greet(span=z + 1)

    each_head(lambda h: (load_q(h).start(), load_k(h).start(), load_v(h).start()))
    for other in others:

        @pl.when(block_core(other) == s)
        def _(other=other):
            for core in range(n_seq):
                load_w(other, core).start()

    @pl.when(block_core(x) == s)
    def _():
        load_share().start()

    beside = jnp.where(z > 0, 1, 0) + jnp.where(z < n_span - 1, 1, 0)
    pl.semaphore_wait(barrier, 1 + n_seq * (n_head - 1) + (n_str - 1) + beside)

    each_head(lambda h: (load_q(h).wait(), load_k(h).wait(), load_v(h).wait()))

    @pl.when(z >= 2)
    def _():
        pass_q(z, 0).start()

    @pl.when(z == 0)
    def _():
        each_head(lambda h: (zero_k(h).start(), zero_v(h).start()))

    each_head(lambda h: (sib_k(h, tok_half).start(), sib_v(h, tok_half).start()))
    for other in others:

        @pl.when(block_core(other) == s)
        def _(other=other):
            for core in range(n_seq):
                load_w(other, core).wait()
            each_piece(lambda i: (relay(other, i).start(), x_piece(other, i).start()))

    @pl.when(block_core(x) == s)
    def _():
        load_share().wait()

    def block(q, keys, v_t, flags):
        scores = [
            lax.dot_general(k, q, (((1,), (1,)), ((), ())), preferred_element_type=jnp.float32)
            * SCORE_SCALE
            for k in keys
        ]
        tops = [
            jnp.where(flag == 1, jnp.max(each, axis=0, keepdims=True), NEG_FLOOR)
            for each, flag in zip(scores, flags)
        ]
        top = functools.reduce(jnp.maximum, tops)
        probs = [
            jnp.exp2(each - jnp.where(flag == 1, top, -NEG_FLOOR))
            for each, flag in zip(scores, flags)
        ]
        total = sum(jnp.sum(each, axis=0, keepdims=True) for each in probs)
        low = jnp.concatenate([each.astype(jnp.bfloat16) for each in probs], axis=0)
        return top, total, jnp.dot(v_t, low, preferred_element_type=jnp.float32)

    def merge(a, b):
        top = jnp.maximum(a[0], b[0])
        wa, wb = jnp.exp2(a[0] - top), jnp.exp2(b[0] - top)
        return top, wa * a[1] + wb * b[1], wa * a[2] + wb * b[2]

    def get_part(c, h):
        return part_stat[c, h, 0:1], part_stat[c, h, 1:2], part_acc[c, h]

    def put_part(c, h, part):
        part_stat[c, h, 0:1] = part[0]
        part_stat[c, h, 1:2] = part[1]
        part_acc[c, h] = part[2]

    def emit(c, h, part):
        @pl.when(c > z)
        def _():
            stat_out[c, h, 0:1] = part[0]
            stat_out[c, h, 1:2] = part[1]
            acc_out[c, h] = part[2].astype(jnp.bfloat16)
            pass_acc(c, h).start()
            pass_stat(c, h).start()

        @pl.when(c == z)
        def _():
            att[x * heads + h, tok_half] = (part[2] / part[1]).T.astype(jnp.bfloat16)
            for other in others:
                att_piece(other, h).start()
            att_pair(x, h, tok_half).start()

    def pass_att(h):
        for other in others:
            att_wait(other, h)
            att_pair(other, h, tok_half).start()

    def pass_on(h):
        def one(c):
            pass_q(c, h).wait_recv()

            @pl.when(z >= 2)
            def _():
                pass_q(c, h).start()

        down(one, z + 1)

        @pl.when((z >= 2) & (h + 1 < heads))
        def _():
            pass_q(z, h + 1).start()

    @pl.when(z >= 2)
    def _():
        pass_on(0)

    def pass_w(h):
        for i in (2 * h, 2 * h + 1):
            for other in others:
                x_wait(other, i)
                for dy in range(1, n_str):
                    y_piece(other, dy, i).start()

    for other in others:

        @pl.when(block_core(other) != s)
        def _(other=other):
            each_piece(lambda i: (relay(other, i).wait_recv(), x_relayed(other, i).start()))

    def share_zero(h):
        zero_k(h).wait_recv()
        fwd_k(h, tok_half).start()
        zero_v(h).wait_recv()
        fwd_v(h, tok_half).start()

    @pl.when(z == 1)
    def _():
        share_zero(0)

    def zero_block(c, h, v_t):
        return block(q_all[c, h], [k_own[h], k_zero[h]], v_t, [mask_ref[c, 1], mask_ref[c, 0]])

    def head_step(h):
        @pl.when((z >= 2) & (h + 1 < heads))
        def _():
            pass_on(h + 1)

        @pl.when(z == 1)
        def _():
            pass_on(h)

        @pl.when(block_core(x) == s)
        def _():
            own_copy(h).start()
            own_share(h).start()

        sib_k(h, sib_half).wait_recv()
        sib_v(h, sib_half).wait_recv()

        k_here = k_own[h]
        v_here = v_own[h].T

        @pl.when(z != 1)
        def _():
            def own_block(c):
                put_part(c, h, block(q_all[c, h], [k_here], v_here, [mask_ref[c, z]]))

            down(own_block, z)

        @pl.when(z == 1)
        def _():
            fwd_k(h, sib_half).wait_recv()
            fwd_v(h, sib_half).wait_recv()
            both = jnp.concatenate([v_here, v_zero[h].T], axis=1)
            v_turned[h] = both

            def later(c):
                emit(c, h, zero_block(c, h, both))

                @pl.when((c == n_span - 1) & (h + 1 < heads))
                def _():
                    share_zero(h + 1)

            down(later, 2)

        @pl.when(z == 0)
        def _():
            emit(z, h, get_part(z, h))

        @pl.when(z < 2)
        def _():
            pass_w(h)

        @pl.when((z >= 2) & ((h == 2) | (h == 4)))
        def _():
            pass_w(h // 2 - 1)

    each_head(head_step)

    @pl.when(z == 1)
    def _():
        def own_step(h):
            emit(1, h, zero_block(1, h, v_turned[h]))

        each_head(own_step)

    @pl.when(z >= 2)
    def _():
        def merge_step(h):
            def one(c):
                pass_acc(c, h).wait_recv()
                pass_stat(c, h).wait_recv()
                before = (
                    stat_in[c, h, 0:1],
                    stat_in[c, h, 1:2],
                    acc_in[c, h].astype(jnp.float32),
                )
                emit(c, h, merge(get_part(c, h), before))

            down(one, z)

            @pl.when(h + 2 < heads)
            def _():
                pass_w(h + 2)

            @pl.when(h > 0)
            def _():
                pass_att(h - 1)

        each_head(merge_step)

    @pl.when(block_core(x) == s)
    def _():
        each_head(lambda i: own_copy(i).wait())

    @pl.when(block_core(x) != s)
    def _():
        each_head(lambda i: own_share(i).wait_recv())

    each_head(lambda h: att_pair(x, h, sib_half).wait_recv())
    step = step_ref[z]

    def gathered(src):
        return jnp.concatenate(
            [
                jnp.concatenate([att[src * heads + h, rows] for h in range(heads)], axis=1)
                for rows in (sib_half, tok_half)
            ],
            axis=0,
        )

    def product(attended, src, t):
        rows = pl.ds(pl.multiple_of(src * w_rows, w_rows), w_rows)
        at = pl.ds(pl.multiple_of(t * tile, tile), tile)
        return jnp.dot(attended, w_full[rows, at], preferred_element_type=jnp.float32)

    attended_own = gathered(x)

    def project(t, carry):
        projected[t] = product(attended_own, x, t)
        return carry

    lax.fori_loop(0, tiles, project, 0)

    @pl.when(z < 2)
    def _():
        lax.fori_loop(0, heads - 1, lambda h, c: (pass_att(h), c)[1], 0)

    pass_att(heads - 1)

    def other_waits(h):
        for other in others:
            for half_piece in range(2):
                for dy in range(1, n_str):
                    y_wait(other, dy, 2 * h + half_piece)
            att_pair(other, h, sib_half).wait_recv()

    each_head(other_waits)
    attended_others = [gathered(other) for other in others]

    def project_last(t, carry):
        whole = projected[t]
        for other, attended in zip(others, attended_others):
            whole = whole + product(attended, other, t)
        here = out_cols(s, t)
        gate_row = jnp.zeros((1, tile), jnp.float32)
        for i in range(gate_ref.shape[0]):
            gate_row = jnp.where(step == i, gate_ref[i : i + 1, here], gate_row)
        gated = (gate_row * whole).astype(jnp.bfloat16)
        out_half[t] = gated[:tok]
        out_piece(s, t).start()
        out_own[t] = gated[tok:]
        out_copy(t).start()
        return carry

    lax.fori_loop(0, tiles, project_last, 0)

    def out_wait(t, carry):
        out_piece(sib, t).wait_recv()
        out_piece(s, t).wait_send()
        out_copy(t).wait()
        return carry

    lax.fori_loop(0, tiles, out_wait, 0)

    def sent(h):
        sib_k(h, tok_half).wait_send()
        sib_v(h, tok_half).wait_send()
        att_pair(x, h, tok_half).wait_send()
        for other in others:
            att_piece(other, h).wait_send()
            att_pair(other, h, tok_half).wait_send()

        @pl.when(block_core(x) == s)
        def _():
            own_share(h).wait_send()

        @pl.when(z == 0)
        def _():
            zero_k(h).wait_send()
            zero_v(h).wait_send()

        @pl.when(z == 1)
        def _():
            fwd_k(h, tok_half).wait_send()
            fwd_v(h, tok_half).wait_send()

        @pl.when(z >= 2)
        def _():
            down(lambda c: pass_q(c, h).wait_send(), z)

        @pl.when(z >= 1)
        def _():
            down(lambda c: (pass_acc(c, h).wait_send(), pass_stat(c, h).wait_send()), z + 1)

    def sent_weights(i):
        for other in others:
            for dy in range(1, n_str):
                y_piece(other, dy, i).wait_send()
            x_piece(other, i).wait_send()

            @pl.when(block_core(other) == s)
            def _(other=other):
                relay(other, i).wait_send()

    each_head(sent)
    each_piece(sent_weights)


def hand_over(from_ref, to_ref):
    to_ref[...] = from_ref[...]


def solution(mesh):
    n_str, n_span = mesh.shape["streams"], mesh.shape["span"]
    n_head, n_seq = mesh.shape["head"], mesh.shape["seq"]
    sizes = (n_str, n_span, n_head, n_seq)

    def on_device(query_rows, key_rows, value_rows, out_weight, gate_table, step_index, block_mask):
        tok = query_rows.shape[0]
        heads = query_rows.shape[1] // HD
        cols = gate_table.shape[1]
        half = cols // n_seq
        tile = 256 if half % 256 == 0 else 128
        tiles = half // tile
        pieces = 2 * heads
        piece = out_weight.shape[0] // n_str // pieces
        vmem, any_space = pltpu.VMEM, pl.ANY
        dma = pltpu.SemaphoreType.DMA
        low, wide = jnp.bfloat16, jnp.float32
        flops = 4 * heads * tok * tok * n_seq * n_span * HD + 2 * tok * n_head * heads * HD * cols
        result = pl.pallas_call(
            functools.partial(kernel, sizes),
            out_shape=jax.ShapeDtypeStruct((tok, cols), low),
            in_specs=[
                pl.BlockSpec(memory_space=pltpu.SMEM),
                pl.BlockSpec(memory_space=pltpu.SMEM),
                pl.BlockSpec(memory_space=any_space),
                pl.BlockSpec(memory_space=any_space),
                pl.BlockSpec(memory_space=any_space),
                pl.BlockSpec(memory_space=any_space),
                pl.BlockSpec(memory_space=vmem),
            ],
            out_specs=pl.BlockSpec(memory_space=any_space),
            scratch_shapes=[
                vmem((n_span, heads, tok, HD), low),
                vmem((heads, n_seq * tok, HD), low),
                vmem((heads, n_seq * tok, HD), low),
                vmem((heads, n_seq * tok, HD), low),
                vmem((heads, n_seq * tok, HD), low),
                vmem((n_span, heads, HD, tok), wide),
                vmem((n_span, heads, 8, tok), wide),
                vmem((n_span, heads, HD, tok), low),
                vmem((n_span, heads, 8, tok), wide),
                vmem((n_span, heads, HD, tok), low),
                vmem((n_span, heads, 8, tok), wide),
                vmem((n_head * heads, n_seq * tok, HD), low),
                vmem((n_head * heads * HD, half), low),
                vmem((tiles, tok, tile), low),
                vmem((tiles, tok, tile), low),
                dma((tiles,)),
                vmem((n_head, pieces, piece, half), low),
                vmem((n_head, n_seq, pieces * piece, half), low),
                vmem((out_weight.shape[0], half), low),
                dma((n_head, n_seq)),
                dma((1,)),
                vmem((heads, HD, 2 * n_seq * tok), low),
                vmem((tiles, n_seq * tok, tile), wide),
                dma((n_head, pieces)),
                dma((n_head, pieces)),
                dma((3, heads)),
                dma((2, heads)),
                dma((2, heads)),
                dma((2, heads)),
                dma((2, heads)),
                dma((2, heads)),
                dma((2, heads)),
                dma((n_span, heads)),
                dma((n_span, heads)),
                dma((n_span, heads)),
                dma((n_span, heads)),
                dma((n_span, heads)),
                dma((n_span, heads)),
                dma((n_head, pieces)),
                dma((n_head, pieces)),
                dma((n_head, n_str, pieces)),
                dma((n_head, n_str, pieces)),
                dma((heads,)),
                dma((heads,)),
                dma((heads,)),
                dma((n_head, heads)),
                dma((n_head, heads)),
                dma((n_head, heads)),
                dma((n_head, heads)),
                dma((tiles,)),
                dma((tiles,)),
            ],
            compiler_params=pltpu.CompilerParams(
                collective_id=0, has_side_effects=True, vmem_limit_bytes=56 * 1024 * 1024
            ),
            cost_estimate=pl.CostEstimate(
                flops=flops, bytes_accessed=6 * out_weight.size, transcendentals=0
            ),
        )(step_index, block_mask, query_rows, key_rows, value_rows, out_weight, gate_table)
        rows = pl.BlockSpec((tok // COPIES, cols), lambda i: (i, 0))
        return pl.pallas_call(
            hand_over,
            out_shape=jax.ShapeDtypeStruct((tok, cols), low),
            grid=(COPIES,),
            in_specs=[rows],
            out_specs=rows,
        )(result)

    in_specs = (
        P(("streams", "span", "seq"), "head"),
        P(("streams", "span", "seq"), "head"),
        P(("streams", "span", "seq"), "head"),
        P("head", "seq"),
        P(None, "head"),
        P("streams"),
        P("streams", None),
    )
    out_specs = P(("streams", "span", "seq"), "head")
    return jax.shard_map(
        on_device, mesh=mesh, in_specs=in_specs, out_specs=out_specs, check_vma=False
    )
```

```python
import functools
import math

import jax
import jax.numpy as jnp
from jax import lax
from jax.experimental import pallas as pl
from jax.experimental.pallas import tpu as pltpu
from jax.sharding import PartitionSpec as P

HD = 128
NEG_FLOOR = -1e30
MESH = pl.DeviceIdType.MESH
SCORE_SCALE = math.log2(math.e) / math.sqrt(HD)


def kernel(
    sizes,
    step_ref,
    mask_ref,
    q_ref,
    k_ref,
    v_ref,
    w_ref,
    gate_ref,
    out_ref,
    q_all,
    k_own,
    v_own,
    k_zero,
    v_zero,
    part_acc,
    part_stat,
    acc_out,
    stat_out,
    acc_in,
    stat_in,
    att,
    w_full,
    out_half,
    out_own,
    out_store,
    w_relay,
    w_stage,
    own_stage,
    stage_sem,
    share_sem,
    v_turned,
    projected,
    relay_send,
    relay_recv,
    load_sem,
    sib_send,
    sib_recv,
    zero_send,
    zero_recv,
    fwd_send,
    fwd_recv,
    q_send,
    q_recv,
    acc_send,
    acc_recv,
    stat_send,
    stat_recv,
    x_send,
    x_recv,
    y_send,
    y_recv,
    own_load,
    own_send,
    own_recv,
    att_send,
    att_recv,
    pair_send,
    pair_recv,
    out_send,
    out_recv,
):
    n_str, n_span, n_head, n_seq = sizes
    y = lax.axis_index("streams")
    z = lax.axis_index("span")
    x = lax.axis_index("head")
    s = lax.axis_index("seq")
    sib = 1 - s
    tok = q_ref.shape[0]
    heads = q_ref.shape[1] // HD
    w_rows = w_ref.shape[0]
    cols = out_ref.shape[1]
    half = cols // n_seq
    tile = 256 if half % 256 == 0 else 128
    tiles = half // tile
    y_rows = w_rows // n_str
    pieces = 2 * heads
    piece = y_rows // pieces
    own_piece = w_rows // heads

    def remote(src, dst, ss, rs, **where):
        return pltpu.make_async_remote_copy(
            src_ref=src, dst_ref=dst, send_sem=ss, recv_sem=rs, device_id=where, device_id_type=MESH
        )

    def head_cols(h):
        return pl.ds(pl.multiple_of(h * HD, HD), HD)

    def each_head(body):
        lax.fori_loop(0, heads, lambda h, c: (body(h), c)[1], 0)

    def each_piece(body):
        lax.fori_loop(0, pieces, lambda i, c: (body(i), c)[1], 0)

    def down(body, low):
        lax.fori_loop(0, n_span - low, lambda i, c: (body(n_span - 1 - i), c)[1], 0)

    tok_half = pl.ds(pl.multiple_of(s * tok, tok), tok)
    sib_half = pl.ds(pl.multiple_of(sib * tok, tok), tok)

    def load_q(h):
        return pltpu.make_async_copy(q_ref.at[:, head_cols(h)], q_all.at[z, h], load_sem.at[0, h])

    def load_k(h):
        return pltpu.make_async_copy(
            k_ref.at[:, head_cols(h)], k_own.at[h, tok_half], load_sem.at[1, h]
        )

    def load_v(h):
        return pltpu.make_async_copy(
            v_ref.at[:, head_cols(h)], v_own.at[h, tok_half], load_sem.at[2, h]
        )

    def sib_k(h, half):
        return remote(
            k_own.at[h, half], k_own.at[h, half], sib_send.at[0, h], sib_recv.at[0, h], seq=sib
        )

    def sib_v(h, half):
        return remote(
            v_own.at[h, half], v_own.at[h, half], sib_send.at[1, h], sib_recv.at[1, h], seq=sib
        )

    def zero_k(h):
        return remote(
            k_own.at[h, tok_half], k_zero.at[h, tok_half], zero_send.at[0, h], zero_recv.at[0, h], span=1
        )

    def zero_v(h):
        return remote(
            v_own.at[h, tok_half], v_zero.at[h, tok_half], zero_send.at[1, h], zero_recv.at[1, h], span=1
        )

    def fwd_k(h, half):
        return remote(
            k_zero.at[h, half], k_zero.at[h, half], fwd_send.at[0, h], fwd_recv.at[0, h], seq=sib
        )

    def fwd_v(h, half):
        return remote(
            v_zero.at[h, half], v_zero.at[h, half], fwd_send.at[1, h], fwd_recv.at[1, h], seq=sib
        )

    def pass_q(c, h):
        return remote(q_all.at[c, h], q_all.at[c, h], q_send.at[c, h], q_recv.at[c, h], span=z - 1)

    def pass_acc(c, h):
        return remote(
            acc_out.at[c, h], acc_in.at[z, h], acc_send.at[c, h], acc_recv.at[z, h], span=c
        )

    def pass_stat(c, h):
        return remote(
            stat_out.at[c, h], stat_in.at[z, h], stat_send.at[c, h], stat_recv.at[z, h], span=c
        )

    def take_part(e, h):
        acc, stat = acc_in.at[e, h], stat_in.at[e, h]
        remote(acc, acc, acc_send.at[e, h], acc_recv.at[e, h], span=e).wait_recv()
        remote(stat, stat, stat_send.at[e, h], stat_recv.at[e, h], span=e).wait_recv()
        return stat_in[e, h, 0:1], stat_in[e, h, 1:2], acc_in[e, h].astype(jnp.float32)

    def w_at(src_x, part, i):
        first = src_x * w_rows + part * y_rows + i * piece
        return w_full.at[pl.ds(pl.multiple_of(first, piece), piece)]

    def block_core(dst_x):
        return (dst_x * n_seq) // n_head

    def block_cols(dst_x, core):
        first = lax.rem(dst_x, n_head // n_seq) * cols + core * half
        return pl.ds(pl.multiple_of(first, HD), half)

    def piece_rows(i):
        return pl.ds(pl.multiple_of(i * piece, piece), piece)

    def load_w(dst_x, core):
        return pltpu.make_async_copy(
            w_ref.at[pl.ds(pl.multiple_of(y * y_rows, y_rows), y_rows), block_cols(dst_x, core)],
            w_stage.at[dst_x, core],
            stage_sem.at[dst_x, core],
        )

    def load_share():
        return pltpu.make_async_copy(w_ref.at[:, block_cols(x, sib)], own_stage, share_sem.at[0])

    def x_piece(dst_x, i):
        return remote(
            w_stage.at[dst_x, s, piece_rows(i)],
            w_at(x, y, i),
            x_send.at[dst_x, i],
            x_recv.at[x, i],
            head=dst_x,
        )

    def relay(dst_x, i):
        return remote(
            w_stage.at[dst_x, sib, piece_rows(i)],
            w_relay.at[dst_x, i],
            relay_send.at[dst_x, i],
            relay_recv.at[dst_x, i],
            seq=sib,
        )

    def x_relayed(dst_x, i):
        return remote(
            w_relay.at[dst_x, i],
            w_at(x, y, i),
            x_send.at[dst_x, i],
            x_recv.at[x, i],
            head=dst_x,
        )

    def x_wait(src_x, i):
        ref = w_at(src_x, y, i)
        remote(ref, ref, x_send.at[src_x, i], x_recv.at[src_x, i], head=src_x).wait_recv()

    def y_piece(src_x, dy, i):
        ref = w_at(src_x, y, i)
        return remote(
            ref, ref, y_send.at[src_x, dy, i], y_recv.at[src_x, dy, i], streams=lax.rem(y + dy, n_str)
        )

    def y_wait(src_x, dy, i):
        from_y = lax.rem(y - dy + n_str, n_str)
        ref = w_at(src_x, from_y, i)
        remote(
            ref, ref, y_send.at[src_x, dy, i], y_recv.at[src_x, dy, i], streams=from_y
        ).wait_recv()

    def own_rows(i):
        return pl.ds(pl.multiple_of(i * own_piece, own_piece), own_piece)

    def own_at(i):
        first = x * w_rows + i * own_piece
        return w_full.at[pl.ds(pl.multiple_of(first, own_piece), own_piece)]

    def own_copy(i):
        return pltpu.make_async_copy(
            w_ref.at[own_rows(i), block_cols(x, s)], own_at(i), own_load.at[i]
        )

    def own_share(i):
        return remote(
            own_stage.at[own_rows(i)], own_at(i), own_send.at[i], own_recv.at[i], seq=sib
        )

    def att_piece(dst_x, h):
        ref = att.at[x * heads + h, tok_half]
        return remote(ref, ref, att_send.at[dst_x, h], att_recv.at[x, h], head=dst_x)

    def att_wait(src_x, h):
        ref = att.at[src_x * heads + h, tok_half]
        remote(ref, ref, att_send.at[src_x, h], att_recv.at[src_x, h], head=src_x).wait_recv()

    def att_pair(src_x, h, rows):
        ref = att.at[src_x * heads + h, rows]
        return remote(ref, ref, pair_send.at[src_x, h], pair_recv.at[src_x, h], seq=sib)

    def out_cols(core, t):
        return pl.ds(pl.multiple_of(core * half + t * tile, tile), tile)

    def out_piece(core, t):
        return remote(
            out_half.at[t], out_ref.at[:, out_cols(core, t)], out_send.at[t], out_recv.at[t], seq=sib
        )

    def out_copy(t):
        return pltpu.make_async_copy(out_own.at[t], out_ref.at[:, out_cols(s, t)], out_store.at[t])

    others = [lax.rem(x + dx, n_head) for dx in range(1, n_head)]

    barrier = pltpu.get_barrier_semaphore()

    def greet(**where):
        pl.semaphore_signal(barrier, inc=1, device_id=where, device_id_type=MESH)

    greet(seq=sib)
    for other in others:
        for core in range(n_seq):
            greet(head=other, seq=core)
    for dy in range(1, n_str):
        greet(streams=lax.rem(y + dy, n_str))

    for dz in range(1, n_span):
        greet(span=lax.rem(z + dz, n_span))

    each_head(lambda h: (load_q(h).start(), load_k(h).start(), load_v(h).start()))
    for other in others:

        @pl.when(block_core(other) == s)
        def _(other=other):
            for core in range(n_seq):
                load_w(other, core).start()

    @pl.when(block_core(x) == s)
    def _():
        load_share().start()

    pl.semaphore_wait(barrier, 1 + n_seq * (n_head - 1) + (n_str - 1) + (n_span - 1))

    each_head(lambda h: (load_q(h).wait(), load_k(h).wait(), load_v(h).wait()))

    @pl.when(z >= 2)
    def _():
        pass_q(z, 0).start()

    @pl.when(z == 0)
    def _():
        each_head(lambda h: (zero_k(h).start(), zero_v(h).start()))

    each_head(lambda h: (sib_k(h, tok_half).start(), sib_v(h, tok_half).start()))
    for other in others:

        @pl.when(block_core(other) == s)
        def _(other=other):
            for core in range(n_seq):
                load_w(other, core).wait()
            each_piece(lambda i: (relay(other, i).start(), x_piece(other, i).start()))

    @pl.when(block_core(x) == s)
    def _():
        load_share().wait()

    def block(q, keys, v_t, flags):
        scores = [
            lax.dot_general(k, q, (((1,), (1,)), ((), ())), preferred_element_type=jnp.float32)
            * SCORE_SCALE
            for k in keys
        ]
        tops = [
            jnp.where(flag == 1, jnp.max(each, axis=0, keepdims=True), NEG_FLOOR)
            for each, flag in zip(scores, flags)
        ]
        top = functools.reduce(jnp.maximum, tops)
        probs = [
            jnp.exp2(each - jnp.where(flag == 1, top, -NEG_FLOOR))
            for each, flag in zip(scores, flags)
        ]
        total = sum(jnp.sum(each, axis=0, keepdims=True) for each in probs)
        low = jnp.concatenate([each.astype(jnp.bfloat16) for each in probs], axis=0)
        return top, total, jnp.dot(v_t, low, preferred_element_type=jnp.float32)

    def merge(a, b):
        top = jnp.maximum(a[0], b[0])
        wa, wb = jnp.exp2(a[0] - top), jnp.exp2(b[0] - top)
        return top, wa * a[1] + wb * b[1], wa * a[2] + wb * b[2]

    def get_part(h):
        return part_stat[h, 0:1], part_stat[h, 1:2], part_acc[h]

    def put_part(h, part):
        part_stat[h, 0:1] = part[0]
        part_stat[h, 1:2] = part[1]
        part_acc[h] = part[2]

    def send_part(c, h, part):
        stat_out[c, h, 0:1] = part[0]
        stat_out[c, h, 1:2] = part[1]
        acc_out[c, h] = part[2].astype(jnp.bfloat16)
        pass_acc(c, h).start()
        pass_stat(c, h).start()

    def finish(h, part):
        att[x * heads + h, tok_half] = (part[2] / part[1]).T.astype(jnp.bfloat16)
        for other in others:
            att_piece(other, h).start()
        att_pair(x, h, tok_half).start()

    def pass_att(h):
        for other in others:
            att_wait(other, h)
            att_pair(other, h, tok_half).start()

    def pass_on(h):
        def one(c):
            pass_q(c, h).wait_recv()

            @pl.when(z >= 2)
            def _():
                pass_q(c, h).start()

        down(one, z + 1)

        @pl.when((z >= 2) & (h + 1 < heads))
        def _():
            pass_q(z, h + 1).start()

    @pl.when(z >= 2)
    def _():
        pass_on(0)

    def pass_w(h):
        for i in (2 * h, 2 * h + 1):
            for other in others:
                x_wait(other, i)
                for dy in range(1, n_str):
                    y_piece(other, dy, i).start()

    for other in others:

        @pl.when(block_core(other) != s)
        def _(other=other):
            each_piece(lambda i: (relay(other, i).wait_recv(), x_relayed(other, i).start()))

    def share_zero(h):
        zero_k(h).wait_recv()
        fwd_k(h, tok_half).start()
        zero_v(h).wait_recv()
        fwd_v(h, tok_half).start()

    @pl.when(z == 1)
    def _():
        share_zero(0)

    def zero_block(c, h, v_t):
        return block(q_all[c, h], [k_own[h], k_zero[h]], v_t, [mask_ref[c, 1], mask_ref[c, 0]])

    def head_step(h):
        @pl.when((z >= 2) & (h + 1 < heads))
        def _():
            pass_on(h + 1)

        @pl.when(z == 1)
        def _():
            pass_on(h)

        @pl.when(block_core(x) == s)
        def _():
            own_copy(h).start()
            own_share(h).start()

        sib_k(h, sib_half).wait_recv()
        sib_v(h, sib_half).wait_recv()

        k_here = k_own[h]
        v_here = v_own[h].T

        @pl.when(z != 1)
        def _():
            def own_block(c):
                part = block(q_all[c, h], [k_here], v_here, [mask_ref[c, z]])

                @pl.when(c > z)
                def _():
                    send_part(c, h, part)

                @pl.when(c == z)
                def _():
                    put_part(h, part)

            served = jnp.where(z == 0, 1, n_span - z)
            lax.fori_loop(0, served, lambda i, c: (own_block(z + served - 1 - i), c)[1], 0)

        @pl.when(z == 1)
        def _():
            fwd_k(h, sib_half).wait_recv()
            fwd_v(h, sib_half).wait_recv()
            both = jnp.concatenate([v_here, v_zero[h].T], axis=1)
            v_turned[h] = both

            def later(c):
                send_part(c, h, zero_block(c, h, both))

                @pl.when((c == n_span - 1) & (h + 1 < heads))
                def _():
                    share_zero(h + 1)

            down(later, 2)

        @pl.when(z == 0)
        def _():
            finish(h, get_part(h))

        @pl.when(z < 2)
        def _():
            pass_w(h)

        @pl.when((z >= 2) & ((h == 2) | (h == 4)))
        def _():
            pass_w(h // 2 - 1)

    each_head(head_step)

    @pl.when(z == 1)
    def _():
        def own_step(h):
            finish(h, zero_block(1, h, v_turned[h]))

        each_head(own_step)

    @pl.when(z >= 2)
    def _():
        def merge_step(h):
            def one(i, carry):
                put_part(h, merge(get_part(h), take_part(z - 1 - i, h)))
                return carry

            lax.fori_loop(0, z - 1, one, 0)
            finish(h, get_part(h))

            @pl.when(h + 2 < heads)
            def _():
                pass_w(h + 2)

            @pl.when(h > 0)
            def _():
                pass_att(h - 1)

        each_head(merge_step)

    @pl.when(block_core(x) == s)
    def _():
        each_head(lambda i: own_copy(i).wait())

    @pl.when(block_core(x) != s)
    def _():
        each_head(lambda i: own_share(i).wait_recv())

    each_head(lambda h: att_pair(x, h, sib_half).wait_recv())
    step = step_ref[z]

    def gathered(src):
        return jnp.concatenate(
            [
                jnp.concatenate([att[src * heads + h, rows] for h in range(heads)], axis=1)
                for rows in (sib_half, tok_half)
            ],
            axis=0,
        )

    def product(attended, src, t):
        rows = pl.ds(pl.multiple_of(src * w_rows, w_rows), w_rows)
        at = pl.ds(pl.multiple_of(t * tile, tile), tile)
        return jnp.dot(attended, w_full[rows, at], preferred_element_type=jnp.float32)

    attended_own = gathered(x)

    def project(t, carry):
        projected[t] = product(attended_own, x, t)
        return carry

    lax.fori_loop(0, tiles, project, 0)

    @pl.when(z < 2)
    def _():
        lax.fori_loop(0, heads - 1, lambda h, c: (pass_att(h), c)[1], 0)

    pass_att(heads - 1)

    def other_waits(h):
        for other in others:
            for half_piece in range(2):
                for dy in range(1, n_str):
                    y_wait(other, dy, 2 * h + half_piece)
            att_pair(other, h, sib_half).wait_recv()

    each_head(other_waits)
    attended_others = [gathered(other) for other in others]

    def project_last(t, carry):
        whole = projected[t]
        for other, attended in zip(others, attended_others):
            whole = whole + product(attended, other, t)
        here = out_cols(s, t)
        gate_row = jnp.zeros((1, tile), jnp.float32)
        for i in range(gate_ref.shape[0]):
            gate_row = jnp.where(step == i, gate_ref[i : i + 1, here], gate_row)
        gated = (gate_row * whole).astype(jnp.bfloat16)
        out_half[t] = gated[:tok]
        out_piece(s, t).start()
        out_own[t] = gated[tok:]
        out_copy(t).start()
        return carry

    lax.fori_loop(0, tiles, project_last, 0)

    def out_wait(t, carry):
        out_piece(sib, t).wait_recv()
        out_piece(s, t).wait_send()
        out_copy(t).wait()
        return carry

    lax.fori_loop(0, tiles, out_wait, 0)

    def sent(h):
        sib_k(h, tok_half).wait_send()
        sib_v(h, tok_half).wait_send()
        att_pair(x, h, tok_half).wait_send()
        for other in others:
            att_piece(other, h).wait_send()
            att_pair(other, h, tok_half).wait_send()

        @pl.when(block_core(x) == s)
        def _():
            own_share(h).wait_send()

        @pl.when(z == 0)
        def _():
            zero_k(h).wait_send()
            zero_v(h).wait_send()

        @pl.when(z == 1)
        def _():
            fwd_k(h, tok_half).wait_send()
            fwd_v(h, tok_half).wait_send()

        @pl.when(z >= 2)
        def _():
            down(lambda c: pass_q(c, h).wait_send(), z)

        @pl.when(z >= 1)
        def _():
            down(lambda c: (pass_acc(c, h).wait_send(), pass_stat(c, h).wait_send()), z + 1)

    def sent_weights(i):
        for other in others:
            for dy in range(1, n_str):
                y_piece(other, dy, i).wait_send()
            x_piece(other, i).wait_send()

            @pl.when(block_core(other) == s)
            def _(other=other):
                relay(other, i).wait_send()

    each_head(sent)
    each_piece(sent_weights)


def solution(mesh):
    n_str, n_span = mesh.shape["streams"], mesh.shape["span"]
    n_head, n_seq = mesh.shape["head"], mesh.shape["seq"]
    sizes = (n_str, n_span, n_head, n_seq)

    def on_device(query_rows, key_rows, value_rows, out_weight, gate_table, step_index, block_mask):
        tok = query_rows.shape[0]
        heads = query_rows.shape[1] // HD
        cols = gate_table.shape[1]
        half = cols // n_seq
        tile = 256 if half % 256 == 0 else 128
        tiles = half // tile
        pieces = 2 * heads
        piece = out_weight.shape[0] // n_str // pieces
        vmem, any_space = pltpu.VMEM, pl.ANY
        dma = pltpu.SemaphoreType.DMA
        low, wide = jnp.bfloat16, jnp.float32
        flops = 4 * heads * tok * tok * n_seq * n_span * HD + 2 * tok * n_head * heads * HD * cols
        return pl.pallas_call(
            functools.partial(kernel, sizes),
            out_shape=jax.ShapeDtypeStruct((tok, cols), low),
            in_specs=[
                pl.BlockSpec(memory_space=pltpu.SMEM),
                pl.BlockSpec(memory_space=pltpu.SMEM),
                pl.BlockSpec(memory_space=any_space),
                pl.BlockSpec(memory_space=any_space),
                pl.BlockSpec(memory_space=any_space),
                pl.BlockSpec(memory_space=any_space),
                pl.BlockSpec(memory_space=vmem),
            ],
            out_specs=pl.BlockSpec(memory_space=any_space),
            scratch_shapes=[
                vmem((n_span, heads, tok, HD), low),
                vmem((heads, n_seq * tok, HD), low),
                vmem((heads, n_seq * tok, HD), low),
                vmem((heads, n_seq * tok, HD), low),
                vmem((heads, n_seq * tok, HD), low),
                vmem((heads, HD, tok), wide),
                vmem((heads, 8, tok), wide),
                vmem((n_span, heads, HD, tok), low),
                vmem((n_span, heads, 8, tok), wide),
                vmem((n_span, heads, HD, tok), low),
                vmem((n_span, heads, 8, tok), wide),
                vmem((n_head * heads, n_seq * tok, HD), low),
                vmem((n_head * heads * HD, half), low),
                vmem((tiles, tok, tile), low),
                vmem((tiles, tok, tile), low),
                dma((tiles,)),
                vmem((n_head, pieces, piece, half), low),
                vmem((n_head, n_seq, pieces * piece, half), low),
                vmem((out_weight.shape[0], half), low),
                dma((n_head, n_seq)),
                dma((1,)),
                vmem((heads, HD, 2 * n_seq * tok), low),
                vmem((tiles, n_seq * tok, tile), wide),
                dma((n_head, pieces)),
                dma((n_head, pieces)),
                dma((3, heads)),
                dma((2, heads)),
                dma((2, heads)),
                dma((2, heads)),
                dma((2, heads)),
                dma((2, heads)),
                dma((2, heads)),
                dma((n_span, heads)),
                dma((n_span, heads)),
                dma((n_span, heads)),
                dma((n_span, heads)),
                dma((n_span, heads)),
                dma((n_span, heads)),
                dma((n_head, pieces)),
                dma((n_head, pieces)),
                dma((n_head, n_str, pieces)),
                dma((n_head, n_str, pieces)),
                dma((heads,)),
                dma((heads,)),
                dma((heads,)),
                dma((n_head, heads)),
                dma((n_head, heads)),
                dma((n_head, heads)),
                dma((n_head, heads)),
                dma((tiles,)),
                dma((tiles,)),
            ],
            compiler_params=pltpu.CompilerParams(
                collective_id=0, has_side_effects=True, vmem_limit_bytes=56 * 1024 * 1024
            ),
            cost_estimate=pl.CostEstimate(
                flops=flops, bytes_accessed=6 * out_weight.size, transcendentals=0
            ),
        )(step_index, block_mask, query_rows, key_rows, value_rows, out_weight, gate_table)

    in_specs = (
        P(("streams", "span", "seq"), "head"),
        P(("streams", "span", "seq"), "head"),
        P(("streams", "span", "seq"), "head"),
        P("head", "seq"),
        P(None, "head"),
        P("streams"),
        P("streams", None),
    )
    out_specs = P(("streams", "span", "seq"), "head")
    return jax.shard_map(
        on_device, mesh=mesh, in_specs=in_specs, out_specs=out_specs, check_vma=False
    )
```

```python
import functools
import math

import jax
import jax.numpy as jnp
from jax import lax
from jax.experimental import pallas as pl
from jax.experimental.pallas import tpu as pltpu
from jax.sharding import PartitionSpec as P

HD = 128
NEG_FLOOR = -1e30
MESH = pl.DeviceIdType.MESH
SCORE_SCALE = math.log2(math.e) / math.sqrt(HD)


def kernel(
    sizes,
    step_ref,
    mask_ref,
    q_ref,
    k_ref,
    v_ref,
    w_ref,
    gate_ref,
    out_ref,
    q_all,
    k_own,
    v_own,
    k_zero,
    v_zero,
    part_acc,
    part_stat,
    acc_out,
    stat_out,
    acc_in,
    stat_in,
    att,
    w_full,
    out_half,
    out_own,
    out_store,
    w_relay,
    w_stage,
    own_stage,
    stage_sem,
    share_sem,
    v_turned,
    projected,
    relay_send,
    relay_recv,
    load_sem,
    sib_send,
    sib_recv,
    zero_send,
    zero_recv,
    fwd_send,
    fwd_recv,
    q_send,
    q_recv,
    acc_send,
    acc_recv,
    stat_send,
    stat_recv,
    x_send,
    x_recv,
    y_send,
    y_recv,
    own_load,
    own_send,
    own_recv,
    att_send,
    att_recv,
    pair_send,
    pair_recv,
    out_send,
    out_recv,
):
    n_str, n_span, n_head, n_seq = sizes
    y = lax.axis_index("streams")
    z = lax.axis_index("span")
    x = lax.axis_index("head")
    s = lax.axis_index("seq")
    sib = 1 - s
    tok = q_ref.shape[0]
    heads = q_ref.shape[1] // HD
    w_rows = w_ref.shape[0]
    cols = out_ref.shape[1]
    half = cols // n_seq
    tile = 256 if half % 256 == 0 else 128
    tiles = half // tile
    y_rows = w_rows // n_str
    pieces = 2 * heads
    piece = y_rows // pieces
    own_piece = w_rows // heads

    def remote(src, dst, ss, rs, **where):
        return pltpu.make_async_remote_copy(
            src_ref=src, dst_ref=dst, send_sem=ss, recv_sem=rs, device_id=where, device_id_type=MESH
        )

    def head_cols(h):
        return pl.ds(pl.multiple_of(h * HD, HD), HD)

    def each_head(body):
        lax.fori_loop(0, heads, lambda h, c: (body(h), c)[1], 0)

    def each_piece(body):
        lax.fori_loop(0, pieces, lambda i, c: (body(i), c)[1], 0)

    def down(body, low):
        lax.fori_loop(0, n_span - low, lambda i, c: (body(n_span - 1 - i), c)[1], 0)

    tok_half = pl.ds(pl.multiple_of(s * tok, tok), tok)
    sib_half = pl.ds(pl.multiple_of(sib * tok, tok), tok)

    def load_q(h):
        return pltpu.make_async_copy(q_ref.at[:, head_cols(h)], q_all.at[z, h], load_sem.at[0, h])

    def load_k(h):
        return pltpu.make_async_copy(
            k_ref.at[:, head_cols(h)], k_own.at[h, tok_half], load_sem.at[1, h]
        )

    def load_v(h):
        return pltpu.make_async_copy(
            v_ref.at[:, head_cols(h)], v_own.at[h, tok_half], load_sem.at[2, h]
        )

    def sib_k(h, half):
        return remote(
            k_own.at[h, half], k_own.at[h, half], sib_send.at[0, h], sib_recv.at[0, h], seq=sib
        )

    def sib_v(h, half):
        return remote(
            v_own.at[h, half], v_own.at[h, half], sib_send.at[1, h], sib_recv.at[1, h], seq=sib
        )

    def zero_k(h):
        return remote(
            k_own.at[h, tok_half], k_zero.at[h, tok_half], zero_send.at[0, h], zero_recv.at[0, h], span=1
        )

    def zero_v(h):
        return remote(
            v_own.at[h, tok_half], v_zero.at[h, tok_half], zero_send.at[1, h], zero_recv.at[1, h], span=1
        )

    def fwd_k(h, half):
        return remote(
            k_zero.at[h, half], k_zero.at[h, half], fwd_send.at[0, h], fwd_recv.at[0, h], seq=sib
        )

    def fwd_v(h, half):
        return remote(
            v_zero.at[h, half], v_zero.at[h, half], fwd_send.at[1, h], fwd_recv.at[1, h], seq=sib
        )

    def pass_q(c, h):
        return remote(q_all.at[c, h], q_all.at[c, h], q_send.at[c, h], q_recv.at[c, h], span=z - 1)

    def pass_acc(c, h):
        return remote(
            acc_out.at[c, h], acc_in.at[z, h], acc_send.at[c, h], acc_recv.at[z, h], span=c
        )

    def pass_stat(c, h):
        return remote(
            stat_out.at[c, h], stat_in.at[z, h], stat_send.at[c, h], stat_recv.at[z, h], span=c
        )

    def take_part(e, h):
        acc, stat = acc_in.at[e, h], stat_in.at[e, h]
        remote(acc, acc, acc_send.at[e, h], acc_recv.at[e, h], span=e).wait_recv()
        remote(stat, stat, stat_send.at[e, h], stat_recv.at[e, h], span=e).wait_recv()
        return stat_in[e, h, 0:1], stat_in[e, h, 1:2], acc_in[e, h].astype(jnp.float32)

    def w_at(src_x, part, i):
        first = src_x * w_rows + part * y_rows + i * piece
        return w_full.at[pl.ds(pl.multiple_of(first, piece), piece)]

    def block_core(dst_x):
        return (dst_x * n_seq) // n_head

    def block_cols(dst_x, core):
        first = lax.rem(dst_x, n_head // n_seq) * cols + core * half
        return pl.ds(pl.multiple_of(first, HD), half)

    def piece_rows(i):
        return pl.ds(pl.multiple_of(i * piece, piece), piece)

    def load_w(dst_x, core):
        return pltpu.make_async_copy(
            w_ref.at[pl.ds(pl.multiple_of(y * y_rows, y_rows), y_rows), block_cols(dst_x, core)],
            w_stage.at[dst_x, core],
            stage_sem.at[dst_x, core],
        )

    def load_share():
        return pltpu.make_async_copy(w_ref.at[:, block_cols(x, sib)], own_stage, share_sem.at[0])

    def x_piece(dst_x, i):
        return remote(
            w_stage.at[dst_x, s, piece_rows(i)],
            w_at(x, y, i),
            x_send.at[dst_x, i],
            x_recv.at[x, i],
            head=dst_x,
        )

    def relay(dst_x, i):
        return remote(
            w_stage.at[dst_x, sib, piece_rows(i)],
            w_relay.at[dst_x, i],
            relay_send.at[dst_x, i],
            relay_recv.at[dst_x, i],
            seq=sib,
        )

    def x_relayed(dst_x, i):
        return remote(
            w_relay.at[dst_x, i],
            w_at(x, y, i),
            x_send.at[dst_x, i],
            x_recv.at[x, i],
            head=dst_x,
        )

    def x_wait(src_x, i):
        ref = w_at(src_x, y, i)
        remote(ref, ref, x_send.at[src_x, i], x_recv.at[src_x, i], head=src_x).wait_recv()

    def y_piece(src_x, dy, i):
        ref = w_at(src_x, y, i)
        return remote(
            ref, ref, y_send.at[src_x, dy, i], y_recv.at[src_x, dy, i], streams=lax.rem(y + dy, n_str)
        )

    def y_wait(src_x, dy, i):
        from_y = lax.rem(y - dy + n_str, n_str)
        ref = w_at(src_x, from_y, i)
        remote(
            ref, ref, y_send.at[src_x, dy, i], y_recv.at[src_x, dy, i], streams=from_y
        ).wait_recv()

    def own_rows(i):
        return pl.ds(pl.multiple_of(i * own_piece, own_piece), own_piece)

    def own_at(i):
        first = x * w_rows + i * own_piece
        return w_full.at[pl.ds(pl.multiple_of(first, own_piece), own_piece)]

    def own_copy(i):
        return pltpu.make_async_copy(
            w_ref.at[own_rows(i), block_cols(x, s)], own_at(i), own_load.at[i]
        )

    def own_share(i):
        return remote(
            own_stage.at[own_rows(i)], own_at(i), own_send.at[i], own_recv.at[i], seq=sib
        )

    def att_piece(dst_x, h):
        ref = att.at[x * heads + h, tok_half]
        return remote(ref, ref, att_send.at[dst_x, h], att_recv.at[x, h], head=dst_x)

    def att_wait(src_x, h):
        ref = att.at[src_x * heads + h, tok_half]
        remote(ref, ref, att_send.at[src_x, h], att_recv.at[src_x, h], head=src_x).wait_recv()

    def att_pair(src_x, h, rows):
        ref = att.at[src_x * heads + h, rows]
        return remote(ref, ref, pair_send.at[src_x, h], pair_recv.at[src_x, h], seq=sib)

    def out_cols(core, t):
        return pl.ds(pl.multiple_of(core * half + t * tile, tile), tile)

    def out_piece(core, t):
        return remote(
            out_half.at[t], out_ref.at[:, out_cols(core, t)], out_send.at[t], out_recv.at[t], seq=sib
        )

    def out_copy(t):
        return pltpu.make_async_copy(out_own.at[t], out_ref.at[:, out_cols(s, t)], out_store.at[t])

    others = [lax.rem(x + dx, n_head) for dx in range(1, n_head)]

    barrier = pltpu.get_barrier_semaphore()

    def greet(**where):
        pl.semaphore_signal(barrier, inc=1, device_id=where, device_id_type=MESH)

    greet(seq=sib)
    for other in others:
        for core in range(n_seq):
            greet(head=other, seq=core)
    for dy in range(1, n_str):
        greet(streams=lax.rem(y + dy, n_str))

    for dz in range(1, n_span):
        greet(span=lax.rem(z + dz, n_span))

    for other in others:

        @pl.when(block_core(other) == s)
        def _(other=other):
            for core in range(n_seq):
                load_w(other, core).start()

    each_head(lambda h: (load_q(h).start(), load_k(h).start(), load_v(h).start()))

    @pl.when(block_core(x) == s)
    def _():
        load_share().start()

    pl.semaphore_wait(barrier, 1 + n_seq * (n_head - 1) + (n_str - 1) + (n_span - 1))

    for other in others:

        @pl.when(block_core(other) == s)
        def _(other=other):
            for core in range(n_seq):
                load_w(other, core).wait()
            each_piece(lambda i: (relay(other, i).start(), x_piece(other, i).start()))

    each_head(lambda h: (load_q(h).wait(), load_k(h).wait(), load_v(h).wait()))

    @pl.when(z >= 2)
    def _():
        pass_q(z, 0).start()

    @pl.when(z == 0)
    def _():
        each_head(lambda h: (zero_k(h).start(), zero_v(h).start()))

    each_head(lambda h: (sib_k(h, tok_half).start(), sib_v(h, tok_half).start()))
    for other in others:

        @pl.when(block_core(other) != s)
        def _(other=other):
            each_piece(lambda i: (relay(other, i).wait_recv(), x_relayed(other, i).start()))

    @pl.when(block_core(x) == s)
    def _():
        load_share().wait()

    def block(q, keys, v_t, flags):
        scores = [
            lax.dot_general(k, q, (((1,), (1,)), ((), ())), preferred_element_type=jnp.float32)
            * SCORE_SCALE
            for k in keys
        ]
        tops = [
            jnp.where(flag == 1, jnp.max(each, axis=0, keepdims=True), NEG_FLOOR)
            for each, flag in zip(scores, flags)
        ]
        top = functools.reduce(jnp.maximum, tops)
        probs = [
            jnp.exp2(each - jnp.where(flag == 1, top, -NEG_FLOOR))
            for each, flag in zip(scores, flags)
        ]
        total = sum(jnp.sum(each, axis=0, keepdims=True) for each in probs)
        low = jnp.concatenate([each.astype(jnp.bfloat16) for each in probs], axis=0)
        return top, total, jnp.dot(v_t, low, preferred_element_type=jnp.float32)

    def merge(a, b):
        top = jnp.maximum(a[0], b[0])
        wa, wb = jnp.exp2(a[0] - top), jnp.exp2(b[0] - top)
        return top, wa * a[1] + wb * b[1], wa * a[2] + wb * b[2]

    def get_part(h):
        return part_stat[h, 0:1], part_stat[h, 1:2], part_acc[h]

    def put_part(h, part):
        part_stat[h, 0:1] = part[0]
        part_stat[h, 1:2] = part[1]
        part_acc[h] = part[2]

    def send_part(c, h, part):
        stat_out[c, h, 0:1] = part[0]
        stat_out[c, h, 1:2] = part[1]
        acc_out[c, h] = part[2].astype(jnp.bfloat16)
        pass_acc(c, h).start()
        pass_stat(c, h).start()

    def finish(h, part):
        att[x * heads + h, tok_half] = (part[2] / part[1]).T.astype(jnp.bfloat16)
        for other in others:
            att_piece(other, h).start()
        att_pair(x, h, tok_half).start()

    def pass_att(h):
        for other in others:
            att_wait(other, h)
            att_pair(other, h, tok_half).start()

    def pass_on(h):
        def one(c):
            pass_q(c, h).wait_recv()

            @pl.when(z >= 2)
            def _():
                pass_q(c, h).start()

        down(one, z + 1)

        @pl.when((z >= 2) & (h + 1 < heads))
        def _():
            pass_q(z, h + 1).start()

    @pl.when(z >= 2)
    def _():
        pass_on(0)

    def pass_w(h):
        for i in (2 * h, 2 * h + 1):
            for other in others:
                x_wait(other, i)
                for dy in range(1, n_str):
                    y_piece(other, dy, i).start()

    def share_zero(h):
        zero_k(h).wait_recv()
        fwd_k(h, tok_half).start()
        zero_v(h).wait_recv()
        fwd_v(h, tok_half).start()

    @pl.when(z == 1)
    def _():
        share_zero(0)

    def zero_block(c, h, v_t):
        return block(q_all[c, h], [k_own[h], k_zero[h]], v_t, [mask_ref[c, 1], mask_ref[c, 0]])

    def head_step(h):
        @pl.when((z >= 2) & (h + 1 < heads))
        def _():
            pass_on(h + 1)

        @pl.when(z == 1)
        def _():
            pass_on(h)

        @pl.when(block_core(x) == s)
        def _():
            own_copy(h).start()
            own_share(h).start()

        sib_k(h, sib_half).wait_recv()
        sib_v(h, sib_half).wait_recv()

        k_here = k_own[h]
        v_here = v_own[h].T

        @pl.when(z != 1)
        def _():
            def own_block(c):
                part = block(q_all[c, h], [k_here], v_here, [mask_ref[c, z]])

                @pl.when(c > z)
                def _():
                    send_part(c, h, part)

                @pl.when(c == z)
                def _():
                    put_part(h, part)

            served = jnp.where(z == 0, 1, n_span - z)
            lax.fori_loop(0, served, lambda i, c: (own_block(z + served - 1 - i), c)[1], 0)

        @pl.when(z == 1)
        def _():
            fwd_k(h, sib_half).wait_recv()
            fwd_v(h, sib_half).wait_recv()
            both = jnp.concatenate([v_here, v_zero[h].T], axis=1)
            v_turned[h] = both

            def later(c):
                send_part(c, h, zero_block(c, h, both))

                @pl.when((c == n_span - 1) & (h + 1 < heads))
                def _():
                    share_zero(h + 1)

            down(later, 2)

        @pl.when(z == 0)
        def _():
            finish(h, get_part(h))

        @pl.when(z < 2)
        def _():
            pass_w(h)

        @pl.when((z >= 2) & ((h == 2) | (h == 4)))
        def _():
            pass_w(h // 2 - 1)

    each_head(head_step)

    @pl.when(z == 1)
    def _():
        def own_step(h):
            finish(h, zero_block(1, h, v_turned[h]))

        each_head(own_step)

    @pl.when(z >= 2)
    def _():
        def merge_step(h):
            def one(i, carry):
                put_part(h, merge(get_part(h), take_part(z - 1 - i, h)))
                return carry

            lax.fori_loop(0, z - 1, one, 0)
            finish(h, get_part(h))

            @pl.when(h + 2 < heads)
            def _():
                pass_w(h + 2)

            @pl.when(h > 0)
            def _():
                pass_att(h - 1)

        each_head(merge_step)

    @pl.when(block_core(x) == s)
    def _():
        each_head(lambda i: own_copy(i).wait())

    @pl.when(block_core(x) != s)
    def _():
        each_head(lambda i: own_share(i).wait_recv())

    each_head(lambda h: att_pair(x, h, sib_half).wait_recv())
    step = step_ref[z]

    def gathered(src):
        return jnp.concatenate(
            [
                jnp.concatenate([att[src * heads + h, rows] for h in range(heads)], axis=1)
                for rows in (sib_half, tok_half)
            ],
            axis=0,
        )

    def product(attended, src, t):
        rows = pl.ds(pl.multiple_of(src * w_rows, w_rows), w_rows)
        at = pl.ds(pl.multiple_of(t * tile, tile), tile)
        return jnp.dot(attended, w_full[rows, at], preferred_element_type=jnp.float32)

    attended_own = gathered(x)

    def project(t, carry):
        projected[t] = product(attended_own, x, t)
        return carry

    lax.fori_loop(0, tiles, project, 0)

    @pl.when(z < 2)
    def _():
        lax.fori_loop(0, heads - 1, lambda h, c: (pass_att(h), c)[1], 0)

    pass_att(heads - 1)

    def other_waits(h):
        for other in others:
            for half_piece in range(2):
                for dy in range(1, n_str):
                    y_wait(other, dy, 2 * h + half_piece)
            att_pair(other, h, sib_half).wait_recv()

    each_head(other_waits)
    attended_others = [gathered(other) for other in others]

    def project_last(t, carry):
        whole = projected[t]
        for other, attended in zip(others, attended_others):
            whole = whole + product(attended, other, t)
        here = out_cols(s, t)
        gate_row = jnp.zeros((1, tile), jnp.float32)
        for i in range(gate_ref.shape[0]):
            gate_row = jnp.where(step == i, gate_ref[i : i + 1, here], gate_row)
        gated = (gate_row * whole).astype(jnp.bfloat16)
        out_half[t] = gated[:tok]
        out_piece(s, t).start()
        out_own[t] = gated[tok:]
        out_copy(t).start()
        return carry

    lax.fori_loop(0, tiles, project_last, 0)

    def out_wait(t, carry):
        out_piece(sib, t).wait_recv()
        out_piece(s, t).wait_send()
        out_copy(t).wait()
        return carry

    lax.fori_loop(0, tiles, out_wait, 0)

    def sent(h):
        sib_k(h, tok_half).wait_send()
        sib_v(h, tok_half).wait_send()
        att_pair(x, h, tok_half).wait_send()
        for other in others:
            att_piece(other, h).wait_send()
            att_pair(other, h, tok_half).wait_send()

        @pl.when(block_core(x) == s)
        def _():
            own_share(h).wait_send()

        @pl.when(z == 0)
        def _():
            zero_k(h).wait_send()
            zero_v(h).wait_send()

        @pl.when(z == 1)
        def _():
            fwd_k(h, tok_half).wait_send()
            fwd_v(h, tok_half).wait_send()

        @pl.when(z >= 2)
        def _():
            down(lambda c: pass_q(c, h).wait_send(), z)

        @pl.when(z >= 1)
        def _():
            down(lambda c: (pass_acc(c, h).wait_send(), pass_stat(c, h).wait_send()), z + 1)

    def sent_weights(i):
        for other in others:
            for dy in range(1, n_str):
                y_piece(other, dy, i).wait_send()
            x_piece(other, i).wait_send()

            @pl.when(block_core(other) == s)
            def _(other=other):
                relay(other, i).wait_send()

    each_head(sent)
    each_piece(sent_weights)


def solution(mesh):
    n_str, n_span = mesh.shape["streams"], mesh.shape["span"]
    n_head, n_seq = mesh.shape["head"], mesh.shape["seq"]
    sizes = (n_str, n_span, n_head, n_seq)

    def on_device(query_rows, key_rows, value_rows, out_weight, gate_table, step_index, block_mask):
        tok = query_rows.shape[0]
        heads = query_rows.shape[1] // HD
        cols = gate_table.shape[1]
        half = cols // n_seq
        tile = 256 if half % 256 == 0 else 128
        tiles = half // tile
        pieces = 2 * heads
        piece = out_weight.shape[0] // n_str // pieces
        vmem, any_space = pltpu.VMEM, pl.ANY
        dma = pltpu.SemaphoreType.DMA
        low, wide = jnp.bfloat16, jnp.float32
        flops = 4 * heads * tok * tok * n_seq * n_span * HD + 2 * tok * n_head * heads * HD * cols
        return pl.pallas_call(
            functools.partial(kernel, sizes),
            out_shape=jax.ShapeDtypeStruct((tok, cols), low),
            in_specs=[
                pl.BlockSpec(memory_space=pltpu.SMEM),
                pl.BlockSpec(memory_space=pltpu.SMEM),
                pl.BlockSpec(memory_space=any_space),
                pl.BlockSpec(memory_space=any_space),
                pl.BlockSpec(memory_space=any_space),
                pl.BlockSpec(memory_space=any_space),
                pl.BlockSpec(memory_space=vmem),
            ],
            out_specs=pl.BlockSpec(memory_space=any_space),
            scratch_shapes=[
                vmem((n_span, heads, tok, HD), low),
                vmem((heads, n_seq * tok, HD), low),
                vmem((heads, n_seq * tok, HD), low),
                vmem((heads, n_seq * tok, HD), low),
                vmem((heads, n_seq * tok, HD), low),
                vmem((heads, HD, tok), wide),
                vmem((heads, 8, tok), wide),
                vmem((n_span, heads, HD, tok), low),
                vmem((n_span, heads, 8, tok), wide),
                vmem((n_span, heads, HD, tok), low),
                vmem((n_span, heads, 8, tok), wide),
                vmem((n_head * heads, n_seq * tok, HD), low),
                vmem((n_head * heads * HD, half), low),
                vmem((tiles, tok, tile), low),
                vmem((tiles, tok, tile), low),
                dma((tiles,)),
                vmem((n_head, pieces, piece, half), low),
                vmem((n_head, n_seq, pieces * piece, half), low),
                vmem((out_weight.shape[0], half), low),
                dma((n_head, n_seq)),
                dma((1,)),
                vmem((heads, HD, 2 * n_seq * tok), low),
                vmem((tiles, n_seq * tok, tile), wide),
                dma((n_head, pieces)),
                dma((n_head, pieces)),
                dma((3, heads)),
                dma((2, heads)),
                dma((2, heads)),
                dma((2, heads)),
                dma((2, heads)),
                dma((2, heads)),
                dma((2, heads)),
                dma((n_span, heads)),
                dma((n_span, heads)),
                dma((n_span, heads)),
                dma((n_span, heads)),
                dma((n_span, heads)),
                dma((n_span, heads)),
                dma((n_head, pieces)),
                dma((n_head, pieces)),
                dma((n_head, n_str, pieces)),
                dma((n_head, n_str, pieces)),
                dma((heads,)),
                dma((heads,)),
                dma((heads,)),
                dma((n_head, heads)),
                dma((n_head, heads)),
                dma((n_head, heads)),
                dma((n_head, heads)),
                dma((tiles,)),
                dma((tiles,)),
            ],
            compiler_params=pltpu.CompilerParams(
                collective_id=0, has_side_effects=True, vmem_limit_bytes=56 * 1024 * 1024
            ),
            cost_estimate=pl.CostEstimate(
                flops=flops, bytes_accessed=6 * out_weight.size, transcendentals=0
            ),
        )(step_index, block_mask, query_rows, key_rows, value_rows, out_weight, gate_table)

    in_specs = (
        P(("streams", "span", "seq"), "head"),
        P(("streams", "span", "seq"), "head"),
        P(("streams", "span", "seq"), "head"),
        P("head", "seq"),
        P(None, "head"),
        P("streams"),
        P("streams", None),
    )
    out_specs = P(("streams", "span", "seq"), "head")
    return jax.shard_map(
        on_device, mesh=mesh, in_specs=in_specs, out_specs=out_specs, check_vma=False
    )
```
